32 devices in a mesh: dp: 16 (over z, y, core), tensor: 2 (over x).
Axes of the slice: x: 2, y: 2, z: 4, core: 2. Of those that a mesh axis runs over, the one named last changes fastest.
Arguments:
- images: bfloat16 [16, 577, 1024], P('dp'), may hold values from -6 to 6
- teacher: bfloat16 [16, 577, 1024], P('dp'), may hold values from -8 to 8
- image_mask: int32 [16], P('dp'), may hold values from 0 to 1, as said below
- attn_gain: bfloat16 [1024], replicated, may hold values from 0.5 to 1.5
- attn_shift: bfloat16 [1024], replicated, may hold values from -0.5 to 0.5
- in_weight: bfloat16 [1024, 3, 1024], P(None, None, 'tensor'), may hold values from -0.1875 to 0.1875
- in_bias: bfloat16 [2, 1024], P(None, 'tensor'), may hold values from -0.5 to 0.5
- out_weight: bfloat16 [1024, 1024], P('tensor'), may hold values from -2 to 2
- out_bias: bfloat16 [1024], replicated, may hold values from -1 to 1
- mlp_gain: bfloat16 [1024], replicated, may hold values from 0.5 to 1.5
- mlp_shift: bfloat16 [1024], replicated, may hold values from -1 to 1
- up_weight: bfloat16 [1024, 4096], P(None, 'tensor'), may hold values from -0.1875 to 0.1875
- up_bias: bfloat16 [4096], P('tensor'), may hold values from -4 to 4
- down_weight: bfloat16 [4096, 1024], P('tensor'), may hold values from -0.1875 to 0.1875
- down_bias: bfloat16 [1024], replicated, may hold values from -1 to 1
Outputs:
- block_out: bfloat16 [16, 577, 1024], P('dp')
- loss: float32 [], replicated
- grad_images: bfloat16 [16, 577, 1024], P('dp')
- grad_attn_gain: float32 [1024], replicated
- grad_attn_shift: float32 [1024], replicated
- grad_in_weight: float32 [1024, 3, 1024], P('dp', None, 'tensor')
- grad_in_bias: float32 [2, 1024], P(None, 'tensor')
- grad_out_weight: float32 [1024, 1024], P('tensor', 'dp')
- grad_out_bias: float32 [1024], replicated
- grad_mlp_gain: float32 [1024], replicated
- grad_mlp_shift: float32 [1024], replicated
- grad_up_weight: float32 [1024, 4096], P('dp', 'tensor')
- grad_up_bias: float32 [4096], P('tensor')
- grad_down_weight: float32 [4096, 1024], P('tensor', 'dp')
- grad_down_bias: float32 [1024], replicated
The draws below stay inside these ranges and needn't reach their ends.
Inputs may be any that keep to these rules, and one draw needn't show every extreme that they name: `image_mask`: the first image is always a real one.
All inputs are finite; a program needn't handle non-finite values.
Results may differ from the reference program's by a relative error of at most 0.0085.
Values sent between devices are 32-bit elements; how exact they have to be, the bound alone decides.
No kernel may reach another device: no remote copies, remote signals or barrier semaphores. Data moves between devices by JAX's collectives and lax.ppermute only.
A program may use at most 128 MiB of HBM per device.

```python
import jax
import jax.numpy as jnp
from jax import lax

D = 1024
HEADS = 16
HD = 64
FF = 4096
SEQ = 577
IMG_DEV = 1
IMAGES = 16


def draw_image_mask(key, part):
    drawn = jax.random.randint(key, (IMAGES,), 0, 8)
    valid = jnp.where(drawn < 7, 1, 0).astype(jnp.int32)
    return valid.at[0].set(1)


def block_scale(key, dims, cuts, least, largest):
    gain = 1.0
    for dim, parts in cuts:
        steps = jax.random.uniform(jax.random.fold_in(jax.random.fold_in(key, 6), dim), (parts,), jnp.float32, least / len(cuts), largest / len(cuts))
        gain = gain * jnp.repeat(jnp.exp(steps), dims[dim] // parts).reshape((-1,) + (1,) * (len(dims) - 1 - dim))
    return gain


def gaussian(rng, dims, deviation, reach, cuts=(), held_as=jnp.bfloat16):
    values = deviation * jax.random.normal(rng, dims, jnp.float32)
    if cuts:
        values = values * block_scale(rng, dims, cuts, -0.22, 0.18)
    return jnp.clip(values, -reach, reach).astype(held_as)


def setup_inputs(seed: int = 0) -> dict:
    streams_of = jax.random.split(jax.random.key(seed), 16)
    images = gaussian(streams_of[0], (IMAGES, SEQ, D), 1.0, 6.0, ((0, 16),))
    teacher = gaussian(streams_of[1], (IMAGES, SEQ, D), 1.5, 8.0, ((0, 16),))
    image_mask = draw_image_mask(jax.random.fold_in(streams_of[15], 71), 0)
    attn_gain = jnp.clip(1.0 + 0.1 * jax.random.normal(streams_of[3], (D,), jnp.float32), 0.5, 1.5).astype(jnp.bfloat16)
    attn_shift = gaussian(streams_of[4], (D,), 0.05, 0.5)
    in_weight = gaussian(streams_of[5], (D, 3, D), D ** -0.5, 0.1875, ((2, 2),))
    in_bias = gaussian(streams_of[6], (2, D), 0.05, 0.5, ((1, 2),))
    out_weight = gaussian(streams_of[7], (D, D), (max(D // 128, 1)) ** -0.5, 2.0, ((0, 2),))
    out_bias = gaussian(streams_of[8], (D,), 0.1, 1.0)
    mlp_gain = jnp.clip(1.0 + 0.1 * jax.random.normal(streams_of[9], (D,), jnp.float32), 0.5, 1.5).astype(jnp.bfloat16)
    mlp_shift = gaussian(streams_of[10], (D,), 0.1, 1.0)
    up_weight = gaussian(streams_of[11], (D, FF), D ** -0.5, 0.1875, ((1, 2),))
    up_bias = gaussian(streams_of[12], (FF,), 0.5, 4.0, ((0, 2),))
    down_weight = gaussian(streams_of[13], (FF, D), (FF // 4) ** -0.5, 0.1875, ((0, 2),))
    down_bias = gaussian(streams_of[14], (D,), 0.1, 1.0)
    return {"images": images, "teacher": teacher, "image_mask": image_mask, "attn_gain": attn_gain, "attn_shift": attn_shift, "in_weight": in_weight, "in_bias": in_bias, "out_weight": out_weight, "out_bias": out_bias, "mlp_gain": mlp_gain, "mlp_shift": mlp_shift, "up_weight": up_weight, "up_bias": up_bias, "down_weight": down_weight, "down_bias": down_bias}


epsilon = 1e-05
score_scale = 0.125
highest = lax.Precision.HIGHEST

@jax.custom_vjp
def low(v):
    return lax.optimization_barrier(v.astype(jnp.bfloat16)).astype(jnp.float32)

@jax.custom_vjp
def low_back(v):
    return v

def low_keep(v):
    return (low(v), None)

def low_pass(kept, grad):
    return (grad,)

def back_keep(v):
    return (v, None)

def back_low(kept, grad):
    return (low(grad),)
low.defvjp(low_keep, low_pass)
low_back.defvjp(back_keep, back_low)

def both_ways(value):
    return low(low_back(value))

def layer_norm(hidden, scales, offset):
    centred = hidden - lax.optimization_barrier(jnp.mean(hidden, axis=-1, keepdims=True))
    return centred * lax.rsqrt(lax.optimization_barrier(jnp.mean(centred * centred, axis=-1, keepdims=True)) + epsilon) * scales + offset

def attend(pieces):
    query_heads, key_heads, value_heads = pieces
    scores = low_back(jnp.einsum('qhd,khd->hqk', query_heads, key_heads, precision=highest) * score_scale)
    weights_low = low(jax.nn.softmax(scores, axis=-1))
    return jnp.einsum('hqk,khd->qhd', weights_low, value_heads, precision=highest)

def forward_group(params, inputs, targets, valid):
    attn_gain, attn_shift, in_weight, in_bias, out_weight, out_bias, mlp_gain, mlp_shift, up_weight, up_bias, down_weight, down_bias = params
    hidden = inputs.reshape(-1, D)
    act_one = low(layer_norm(hidden, attn_gain, attn_shift))
    projected = jnp.einsum('rd,dcf->rcf', act_one, in_weight, precision=highest)
    query_rows = both_ways(projected[:, 0] + in_bias[0])
    key_rows = both_ways(projected[:, 1])
    value_rows = both_ways(projected[:, 2] + in_bias[1])
    head_shape = (IMG_DEV, SEQ, HEADS, HD)
    context = lax.map(jax.checkpoint(attend), (query_rows.reshape(head_shape), key_rows.reshape(head_shape), value_rows.reshape(head_shape)))
    context = both_ways(context.reshape(-1, D))
    attn_branch = low_back(jnp.dot(context, out_weight, precision=highest))
    middle = hidden + attn_branch + out_bias
    act_two = low(layer_norm(middle, mlp_gain, mlp_shift))
    pre_act = low_back(jnp.dot(act_two, up_weight, precision=highest) + up_bias)
    inner = low(pre_act * jax.nn.sigmoid(1.702 * pre_act))
    mlp_branch = low_back(jnp.dot(inner, down_weight, precision=highest))
    result = middle + mlp_branch + down_bias
    error = result - targets.reshape(-1, D)
    row_weight = jnp.repeat(valid, SEQ)[:, None]
    return (result.reshape(inputs.shape), jnp.sum(row_weight * error * error))

def reference(images, teacher, image_mask, attn_gain, attn_shift, in_weight, in_bias, out_weight, out_bias, mlp_gain, mlp_shift, up_weight, up_bias, down_weight, down_bias):
    params = tuple((array.astype(jnp.float32) for array in (attn_gain, attn_shift, in_weight, in_bias, out_weight, out_bias, mlp_gain, mlp_shift, up_weight, up_bias, down_weight, down_bias)))
    groups = IMAGES // IMG_DEV
    inputs = images.astype(jnp.float32).reshape(groups, IMG_DEV, SEQ, D)
    targets = teacher.astype(jnp.float32).reshape(groups, IMG_DEV, SEQ, D)
    valid = image_mask.astype(jnp.float32).reshape(groups, IMG_DEV)
    token_count = jnp.sum(valid) * SEQ

    def objective(weights_all, states):

        def step(carry, pieces):
            result, squares = jax.checkpoint(forward_group)(weights_all, pieces[0], pieces[1], pieces[2])
            return (carry + squares, result)
        squares, results = lax.scan(step, jnp.zeros((), jnp.float32), (states, targets, valid))
        return (squares / token_count, results)
    (loss, results), pullback = jax.vjp(objective, params, inputs)
    grad_params, grad_inputs = pullback((jnp.ones((), jnp.float32), jnp.zeros_like(results)))
    block_out = results.reshape(IMAGES, SEQ, D).astype(jnp.bfloat16)
    grad_images = grad_inputs.reshape(IMAGES, SEQ, D).astype(jnp.bfloat16)
    return (block_out, loss, grad_images, grad_params[0], grad_params[1], grad_params[2], grad_params[3], grad_params[4], grad_params[5], grad_params[6], grad_params[7], grad_params[8], grad_params[9], grad_params[10], grad_params[11])
```

```python
import jax
import jax.numpy as jnp
from jax import lax
from jax.experimental import pallas as pl
from jax.experimental.pallas import tpu as pltpu
from jax.sharding import PartitionSpec as P

HD = 64

epsilon = 1e-05
score_scale = 0.125
quick_rate = 1.702
log2_e = 1.4426950408889634
score_rate = score_scale * log2_e

NN = (((1,), (0,)), ((), ()))
NT = (((1,), (1,)), ((), ()))
VMEM_BYTES = 48 * 2**20


def dot(matrix_a, matrix_b, dims=NN):
    return lax.dot_general(matrix_a, matrix_b, dims, preferred_element_type=jnp.float32)


def layer_norm(hidden, scales, offset):
    centred = hidden - jnp.mean(hidden, axis=-1, keepdims=True)
    inverse = lax.rsqrt(jnp.mean(centred * centred, axis=-1, keepdims=True) + epsilon)
    normed = centred * inverse
    return (normed * scales + offset, normed, inverse)


def norm_back(grad_out, normed, inverse, scales):
    scaled = grad_out * scales
    centred = scaled - jnp.mean(scaled, axis=-1, keepdims=True)
    return (centred - normed * jnp.mean(scaled * normed, axis=-1, keepdims=True)) * inverse


def first_head(shape):
    return lax.broadcasted_iota(jnp.int32, shape, len(shape) - 1) < HD


def attend_kernel(query_ref, key_ref, value_ref, context_ref, log_ref):
    seq_len, width = key_ref.shape
    low = first_head((seq_len, 2 * HD))
    zero = jnp.zeros((), jnp.bfloat16)
    for pair in range(width // (2 * HD)):
        cols = slice(2 * HD * pair, 2 * HD * (pair + 1))
        query, key = query_ref[:, cols], key_ref[:, cols]
        value_t = jnp.transpose(value_ref[:, cols])
        parts = []
        for half in range(2):
            one_key = jnp.where(low if half == 0 else ~low, key, zero)
            scores = dot(one_key, query, NT)
            top = jnp.max(scores, axis=0, keepdims=True)
            weights = jnp.exp2((scores - top) * score_rate)
            total = jnp.sum(weights, axis=0, keepdims=True)
            weights_low = (weights * (1.0 / total)).astype(jnp.bfloat16)
            parts.append(dot(value_t[HD * half : HD * (half + 1)], weights_low))
            head = 2 * pair + half
            log_ref[head : head + 1, :] = top * score_rate + jnp.log2(total)
        context_ref[:, cols] = jnp.transpose(jnp.concatenate(parts, axis=0)).astype(
            context_ref.dtype
        )


def attend(query, key, value):
    rows, width = query.shape
    seq_len = key.shape[0]
    heads = width // HD
    return pl.pallas_call(
        attend_kernel,
        out_shape=(
            jax.ShapeDtypeStruct((rows, width), jnp.bfloat16),
            jax.ShapeDtypeStruct((heads, rows), jnp.float32),
        ),
        compiler_params=pltpu.CompilerParams(vmem_limit_bytes=VMEM_BYTES),
        cost_estimate=pl.CostEstimate(
            flops=16 * rows * seq_len * width,
            bytes_accessed=8 * seq_len * width,
            transcendentals=rows * seq_len * heads,
        ),
        name="attend",
    )(query, key, value)


def attend_back_kernel(
    query_ref, key_ref, value_ref, log_ref, grad_ref, grad_query_ref, grad_key_ref, grad_value_ref
):
    seq_len, width = key_ref.shape
    low = first_head((seq_len, 2 * HD))
    zero = jnp.zeros((), jnp.bfloat16)
    for pair in range(width // (2 * HD)):
        cols = slice(2 * HD * pair, 2 * HD * (pair + 1))
        query, key, value = query_ref[:, cols], key_ref[:, cols], value_ref[:, cols]
        grad = grad_ref[:, cols]
        key_t = jnp.transpose(key)
        grad_query, grad_key, grad_value = [], [], []
        for half in range(2):
            kept = low if half == 0 else ~low
            head = 2 * pair + half
            scores = dot(jnp.where(kept, key, zero), query, NT)
            weights = jnp.exp2(scores * score_rate - log_ref[head : head + 1, :])
            grad_weights = dot(jnp.where(kept, value, zero), grad, NT)
            grad_value.append(dot(weights.astype(jnp.bfloat16), grad))
            row_sum = jnp.sum(grad_weights * weights, axis=0, keepdims=True)
            grad_scores = (weights * (grad_weights - row_sum)).astype(jnp.bfloat16)
            grad_key.append(dot(grad_scores, query))
            grad_query.append(dot(key_t[HD * half : HD * (half + 1)], grad_scores))
        grad_query_ref[:, cols] = (
            jnp.transpose(jnp.concatenate(grad_query, axis=0)) * score_scale
        ).astype(jnp.bfloat16)
        grad_key_ref[:, cols] = (jnp.where(low, grad_key[0], grad_key[1]) * score_scale).astype(
            jnp.bfloat16
        )
        grad_value_ref[:, cols] = jnp.where(low, grad_value[0], grad_value[1]).astype(jnp.bfloat16)


def attend_back(query, key, value, log_total, grad_context):
    seq_len, width = key.shape
    heads = width // HD
    shape = jax.ShapeDtypeStruct((seq_len, width), jnp.bfloat16)
    return pl.pallas_call(
        attend_back_kernel,
        out_shape=(shape, shape, shape),
        compiler_params=pltpu.CompilerParams(vmem_limit_bytes=VMEM_BYTES),
        cost_estimate=pl.CostEstimate(
            flops=40 * seq_len * seq_len * width,
            bytes_accessed=14 * seq_len * width,
            transcendentals=seq_len * seq_len * heads,
        ),
        name="attend_back",
    )(query, key, value, log_total, grad_context)


def make_shards(mesh):
    groups = mesh.shape["dp"]
    bits = groups.bit_length() - 1
    assert groups == 1 << bits and mesh.shape["tensor"] == 2

    def swap_tensor(value):
        return lax.ppermute(value, "tensor", [(0, 1), (1, 0)])

    def swap_bit(value, bit):
        return lax.ppermute(value, "dp", [(i, i ^ (1 << bit)) for i in range(groups)])

    def sum_dp(value):
        for bit in range(bits):
            value = value + swap_bit(value, bit)
        return value

    def own_bit(bit):
        return (lax.axis_index("dp") >> bit) & 1

    def pick(value, which):
        return lax.dynamic_index_in_dim(value, which, axis=1, keepdims=False)

    def scatter_grad(rows_by, columns_by):
        width = rows_by.shape[1]
        part = width // groups
        transposed = rows_by.T.reshape(groups // 2, 2, part, rows_by.shape[0])
        mine = own_bit(0)
        give = dot(pick(transposed, 1 - mine).reshape(width // 2, -1), columns_by)
        keep = dot(pick(transposed, mine).reshape(width // 2, -1), columns_by)
        total = keep + swap_bit(give, 0)
        for bit in range(1, bits):
            split = total.reshape(groups >> (bit + 1), 2, part, -1)
            mine = own_bit(bit)
            total = pick(split, mine) + swap_bit(pick(split, 1 - mine), bit)
        return total.reshape(part, -1)

    def shards(
        images,
        teacher,
        image_mask,
        attn_gain,
        attn_shift,
        in_weight,
        in_bias,
        out_weight,
        out_bias,
        mlp_gain,
        mlp_shift,
        up_weight,
        up_bias,
        down_weight,
        down_bias,
    ):
        image_count, seq_len, width = images.shape
        row_count = image_count * seq_len
        local_width = in_weight.shape[2]
        gain_one = attn_gain.astype(jnp.float32)
        gain_two = mlp_gain.astype(jnp.float32)
        shift_two = mlp_shift.astype(jnp.float32)
        bias_in = in_bias.astype(jnp.float32)
        bias_out = out_bias.astype(jnp.float32)
        bias_up = up_bias.astype(jnp.float32)
        bias_down = down_bias.astype(jnp.float32)
        cut = 256
        chunks = (slice(0, cut), slice(cut, row_count))

        valid = image_mask.astype(jnp.float32)[0]
        count_all = sum_dp(jnp.full((8, 128), valid * seq_len, jnp.float32))[0, 0]

        hidden = images.reshape(row_count, width).astype(jnp.float32)
        targets = teacher.reshape(row_count, width)
        normed_out, normed_one, inverse_one = layer_norm(
            hidden, gain_one, attn_shift.astype(jnp.float32)
        )
        act_one = normed_out.astype(jnp.bfloat16)
        weights_in = jnp.swapaxes(in_weight, 0, 1)
        query = (dot(act_one, weights_in[0]) + bias_in[0]).astype(jnp.bfloat16)
        key = dot(act_one, weights_in[1]).astype(jnp.bfloat16)
        value = (dot(act_one, weights_in[2]) + bias_in[1]).astype(jnp.bfloat16)

        context, log_total, attn_part, middle = [], [], [], []
        for rows in chunks:
            part, logs = attend(query[rows], key, value)
            context.append(part)
            log_total.append(logs)
            attn_part.append(dot(part, out_weight))
        attn_other = [swap_tensor(part) for part in attn_part]
        act_two, inner, slope, mlp_part, normed_two, inverse_two = [], [], [], [], [], []
        for rows, part, other in zip(chunks, attn_part, attn_other):
            mid = hidden[rows] + (part + other) + bias_out
            normed_out, normed, inverse = layer_norm(mid, gain_two, shift_two)
            act = normed_out.astype(jnp.bfloat16)
            pre_act = dot(act, up_weight) + bias_up
            sigma = jax.nn.sigmoid(quick_rate * pre_act)
            low = (pre_act * sigma).astype(jnp.bfloat16)
            middle.append(mid)
            normed_two.append(normed)
            inverse_two.append(inverse)
            act_two.append(act)
            inner.append(low)
            slope.append(sigma + pre_act * quick_rate * sigma * (1.0 - sigma))
            mlp_part.append(dot(low, down_weight))
        mlp_other = [swap_tensor(part) for part in mlp_part]
        result, grad_result, grad_low, grad_pre, two_part = [], [], [], [], []
        squares = jnp.zeros((), jnp.float32)
        for i, rows in enumerate(chunks):
            res = middle[i] + (mlp_part[i] + mlp_other[i]) + bias_down
            error = res - targets[rows].astype(jnp.float32)
            squares = squares + jnp.sum(valid * error * error)
            grad = 2.0 * valid * error / count_all
            low = grad.astype(jnp.bfloat16)
            pre = (dot(low, down_weight, NT) * slope[i]).astype(jnp.bfloat16)
            result.append(res.astype(jnp.bfloat16))
            grad_result.append(grad)
            grad_low.append(low)
            grad_pre.append(pre)
            two_part.append(dot(pre, up_weight, NT))
        two_other = [swap_tensor(part) for part in two_part]
        join = lambda parts: jnp.concatenate(parts, axis=0)
        full_grad_pre = join(grad_pre)
        full_down = scatter_grad(join(grad_low), join(inner))
        full_up = scatter_grad(join(act_two), full_grad_pre)
        grad_down_bias = sum(jnp.sum(part, axis=0) for part in grad_result)
        grad_up_bias = jnp.sum(full_grad_pre.astype(jnp.float32), axis=0)
        grad_middle, grad_attn, grad_context = [], [], []
        grad_mlp_gain = grad_mlp_shift = grad_out_bias = 0.0
        for i, rows in enumerate(chunks):
            grad_two = two_part[i] + two_other[i]
            grad_mlp_gain += jnp.sum(grad_two * normed_two[i], axis=0)
            grad_mlp_shift += jnp.sum(grad_two, axis=0)
            grad_mid = grad_result[i] + norm_back(
                grad_two, normed_two[i], inverse_two[i], gain_two
            )
            grad_out_bias += jnp.sum(grad_mid, axis=0)
            low = grad_mid.astype(jnp.bfloat16)
            grad_middle.append(grad_mid)
            grad_attn.append(low)
            grad_context.append(dot(low, out_weight, NT).astype(jnp.bfloat16))
        full_out = scatter_grad(join(grad_attn), join(context))
        grad_query, grad_key, grad_value = attend_back(
            query, key, value, jnp.concatenate(log_total, axis=1), join(grad_context)
        )
        grad_in_bias = jnp.stack(
            [
                jnp.sum(grad_query.astype(jnp.float32), axis=0),
                jnp.sum(grad_value.astype(jnp.float32), axis=0),
            ]
        )
        one_part = []
        for rows in chunks:
            one_part.append(
                dot(grad_query[rows], weights_in[0], NT)
                + dot(grad_key[rows], weights_in[1], NT)
                + dot(grad_value[rows], weights_in[2], NT)
            )
        one_other = [swap_tensor(part) for part in one_part]
        full_in = scatter_grad(
            act_one, jnp.concatenate([grad_query, grad_key, grad_value], axis=1)
        )
        grad_attn_gain = grad_attn_shift = 0.0
        grad_images = []
        for i, rows in enumerate(chunks):
            grad_attn_gain += jnp.sum(one_part[i] * normed_one[rows], axis=0)
            grad_attn_shift += jnp.sum(one_part[i], axis=0)
            grad_one = one_part[i] + one_other[i]
            grad_images.append(
                (
                    grad_middle[i]
                    + norm_back(grad_one, normed_one[rows], inverse_one[rows], gain_one)
                ).astype(jnp.bfloat16)
            )
        first = jnp.stack([grad_attn_gain, grad_attn_shift])
        first = first + swap_tensor(first)
        small = jnp.concatenate(
            [
                first.reshape(-1),
                grad_in_bias.reshape(-1),
                grad_out_bias,
                grad_mlp_gain,
                grad_mlp_shift,
                grad_up_bias,
                grad_down_bias,
                jnp.full((128,), squares),
            ]
        )
        small = sum_dp(small.reshape(-1, 128)).reshape(-1)
        sizes = (width, width, 2 * local_width, width, width, width, bias_up.shape[0], width, 128)
        pieces = []
        start = 0
        for size in sizes:
            pieces.append(small[start : start + size])
            start += size
        shape = (image_count, seq_len, width)
        return (
            join(result).reshape(shape),
            pieces[8][0] / count_all,
            join(grad_images).reshape(shape),
            pieces[0],
            pieces[1],
            full_in.reshape(-1, 3, local_width),
            pieces[2].reshape(2, local_width),
            full_out.T,
            pieces[3],
            pieces[4],
            pieces[5],
            full_up,
            pieces[6],
            full_down.T,
            pieces[7],
        )

    return shards


def solution(mesh):
    placed = (
        P("dp", None, None),
        P("dp", None, None),
        P("dp"),
        P(),
        P(),
        P(None, None, "tensor"),
        P(None, "tensor"),
        P("tensor", None),
        P(),
        P(),
        P(),
        P(None, "tensor"),
        P("tensor"),
        P("tensor", None),
        P(),
    )
    return jax.shard_map(
        make_shards(mesh),
        mesh=mesh,
        in_specs=placed,
        out_specs=(
            P("dp", None, None),
            P(),
            P("dp", None, None),
            P(),
            P(),
            P("dp", None, "tensor"),
            P(None, "tensor"),
            P("tensor", "dp"),
            P(),
            P(),
            P(),
            P("dp", "tensor"),
            P("tensor"),
            P("tensor", "dp"),
            P(),
        ),
        check_vma=False,
    )
```

```python
import jax
import jax.numpy as jnp
from jax import lax
from jax.experimental import pallas as pl
from jax.experimental.pallas import tpu as pltpu
from jax.sharding import PartitionSpec as P

HD = 64

epsilon = 1e-05
score_scale = 0.125
quick_rate = 1.702
log2_e = 1.4426950408889634
score_rate = score_scale * log2_e

NN = (((1,), (0,)), ((), ()))
NT = (((1,), (1,)), ((), ()))
VMEM_BYTES = 48 * 2**20
BRIEF = pl.CostEstimate(flops=1, bytes_accessed=1, transcendentals=0)


def dot(matrix_a, matrix_b, dims=NN):
    return lax.dot_general(matrix_a, matrix_b, dims, preferred_element_type=jnp.float32)


def layer_norm(hidden, scales, offset):
    centred = hidden - jnp.mean(hidden, axis=-1, keepdims=True)
    inverse = lax.rsqrt(jnp.mean(centred * centred, axis=-1, keepdims=True) + epsilon)
    normed = centred * inverse
    return (normed * scales + offset, normed, inverse)


def norm_back(grad_out, normed, inverse, scales):
    scaled = grad_out * scales
    centred = scaled - jnp.mean(scaled, axis=-1, keepdims=True)
    return (centred - normed * jnp.mean(scaled * normed, axis=-1, keepdims=True)) * inverse


def first_head(shape):
    return lax.broadcasted_iota(jnp.int32, shape, len(shape) - 1) < HD


def local_call(
    kernel, outs, ins, after=(), scratch=(), smem=0, name=None
):
    count = len(ins)

    def body(*refs):
        kernel(*refs[:count], *refs[count + len(after) :])

    return pl.pallas_call(
        body,
        out_shape=tuple(outs),
        in_specs=[pl.BlockSpec(memory_space=pltpu.SMEM)] * smem
        + [pl.BlockSpec(memory_space=pltpu.VMEM)] * (count - smem)
        + [pl.BlockSpec(memory_space=pl.ANY)] * len(after),
        out_specs=tuple(pl.BlockSpec(memory_space=pltpu.VMEM) for _ in outs),
        scratch_shapes=list(scratch),
        compiler_params=pltpu.CompilerParams(vmem_limit_bytes=VMEM_BYTES),
        cost_estimate=BRIEF,
        name=name,
    )(*ins, *after)


def part_blocks(source, bit, high, low, keep_ref, give_ref):
    for j in range(high):
        keep_ref[low * j : low * (j + 1)] = source[
            pl.ds(pl.multiple_of((2 * j + bit) * low, 8), low)
        ]
        give_ref[low * j : low * (j + 1)] = source[
            pl.ds(pl.multiple_of((2 * j + 1 - bit) * low, 8), low)
        ]


def lanes(rows):
    return -(-rows // 128) * 128


def turn(value, bit, part, scratch, keep_ref, give_ref):
    rows = value.shape[0]
    scratch[:, :rows] = jnp.transpose(value)
    if scratch.shape[1] > rows:
        scratch[:, rows:] = jnp.zeros((scratch.shape[0], scratch.shape[1] - rows), jnp.float32)
    part_blocks(scratch, bit, value.shape[1] // (2 * part), part, keep_ref, give_ref)


def like(shape, dtype=jnp.float32):
    return jax.ShapeDtypeStruct(shape, dtype)


def attend_kernel(query_ref, key_ref, value_ref, first_ref, second_ref, log_ref):
    seq_len, width = query_ref.shape
    cut = first_ref.shape[0]
    low = first_head((seq_len, 2 * HD))
    zero = jnp.zeros((), jnp.bfloat16)
    for pair in range(width // (2 * HD)):
        start, stop = 2 * HD * pair, 2 * HD * (pair + 1)
        cols = slice(start, stop)
        query, key = query_ref[:, cols], key_ref[:, cols]
        value_t = jnp.transpose(value_ref[:, cols])
        parts = []
        for half in range(2):
            one_key = jnp.where(low if half == 0 else ~low, key, zero)
            scores = dot(one_key, query, NT)
            top = jnp.max(scores, axis=0, keepdims=True)
            weights = jnp.exp2((scores - top) * score_rate)
            total = jnp.sum(weights, axis=0, keepdims=True)
            weights_low = (weights * (1.0 / total)).astype(jnp.bfloat16)
            parts.append(dot(value_t[HD * half : HD * (half + 1)], weights_low))
            head = 2 * pair + half
            log_ref[head : head + 1, :] = top * score_rate + jnp.log2(total)
        context = jnp.transpose(jnp.concatenate(parts, axis=0)).astype(jnp.bfloat16)
        context = context.astype(jnp.float32)
        first_ref[:, cols] = context[:cut]
        second_ref[:, cols] = context[cut:]


def attend(query, key, value, cut, after=()):
    rows, width = query.shape
    return local_call(
        attend_kernel,
        (like((cut, width)), like((rows - cut, width)), like((width // HD, rows))),
        (query, key, value),
        after,
        name="attend",
    )


def turn_step(bit, value, part, after=()):
    rows, width = value.shape
    half = like((width // 2, lanes(rows)))

    def kernel(bit_ref, value_ref, keep_ref, give_ref, scratch):
        turn(value_ref[...].astype(jnp.float32), bit_ref[0], part, scratch, keep_ref, give_ref)

    return local_call(
        kernel,
        (half, half),
        (bit, value),
        after,
        scratch=(pltpu.VMEM((width, lanes(rows)), jnp.float32),),
        smem=1,
        name="turn",
    )


def attend_back_kernel(query_ref, key_ref, value_ref, log_ref, *refs):
    grad_refs, grads_ref = refs[:-1], refs[-1]
    seq_len, width = query_ref.shape
    low = first_head((seq_len, 2 * HD))
    zero = jnp.zeros((), jnp.bfloat16)
    round_low = lambda v: v.astype(jnp.bfloat16).astype(jnp.float32)
    for pair in range(width // (2 * HD)):
        start, stop = 2 * HD * pair, 2 * HD * (pair + 1)
        cols = slice(start, stop)
        query, key, value = query_ref[:, cols], key_ref[:, cols], value_ref[:, cols]
        grad = jnp.concatenate([one[:, cols] for one in grad_refs], axis=0)
        key_t = jnp.transpose(key)
        grad_query, grad_key, grad_value = [], [], []
        for half in range(2):
            kept = low if half == 0 else ~low
            head = 2 * pair + half
            scores = dot(jnp.where(kept, key, zero), query, NT)
            weights = jnp.exp2(scores * score_rate - log_ref[head : head + 1, :])
            grad_weights = dot(jnp.where(kept, value, zero), grad, NT)
            grad_value.append(dot(weights.astype(jnp.bfloat16), grad))
            row_sum = jnp.sum(grad_weights * weights, axis=0, keepdims=True)
            grad_scores = (weights * (grad_weights - row_sum)).astype(jnp.bfloat16)
            grad_key.append(dot(grad_scores, query))
            grad_query.append(dot(key_t[HD * half : HD * (half + 1)], grad_scores))
        grads_ref[:, start:stop] = round_low(
            jnp.transpose(jnp.concatenate(grad_query, axis=0)) * score_scale
        )
        grads_ref[:, width + start : width + stop] = round_low(
            jnp.where(low, grad_key[0], grad_key[1]) * score_scale
        )
        grads_ref[:, 2 * width + start : 2 * width + stop] = round_low(
            jnp.where(low, grad_value[0], grad_value[1])
        )


def attend_back(query, key, value, log_total, grad_context, after=()):
    seq_len, width = query.shape
    return local_call(
        attend_back_kernel,
        (like((seq_len, 3 * width)),),
        (query, key, value, log_total, *grad_context),
        after,
        name="attend_back",
    )[0]


def mlp_kernel(
    rows, inside, part, places_ref, bit_ref, hidden_ref, context_ref, other_ref, weight_ref, *refs
):
    pieces, (bias_ref, gain_ref, shift_ref, up_ref, up_bias_ref, down_ref) = refs[:4], refs[4:10]
    middle_ref, normed_ref, inverse_ref, turned_ref, given_ref, inner_ref, slope_ref, part_ref = (
        refs[10:18]
    )
    weight_other, act_ref, scratch = refs[18:]

    @pl.when(pl.program_id(0) == 0)
    def _():
        block = pieces[0].shape[0]
        for i, piece in enumerate(pieces):
            start = pl.multiple_of(places_ref[i] * block, block)
            weight_other[pl.ds(start, block)] = piece[...].astype(jnp.bfloat16)
        branch = dot(context_ref[inside].astype(jnp.bfloat16), weight_ref[...]) + dot(
            other_ref[inside].astype(jnp.bfloat16), weight_other[...]
        )
        middle = hidden_ref[rows].astype(jnp.float32) + branch + bias_ref[...]
        normed_out, normed, inverse = layer_norm(middle, gain_ref[...], shift_ref[...])
        middle_ref[...] = middle
        normed_ref[...] = normed
        inverse_ref[...] = inverse
        act = normed_out.astype(jnp.bfloat16)
        act_ref[...] = act
        turn(act.astype(jnp.float32), bit_ref[0], part, scratch, turned_ref, given_ref)

    pre_act = dot(act_ref[...], up_ref[...]) + up_bias_ref[...]
    sigma = 0.5 + 0.5 * jnp.tanh((0.5 * quick_rate) * pre_act)
    inner = (pre_act * sigma).astype(jnp.bfloat16)
    inner_ref[...] = inner.astype(jnp.float32)
    slope_ref[...] = sigma + pre_act * quick_rate * sigma * (1.0 - sigma)
    product = dot(inner, down_ref[...])

    @pl.when(pl.program_id(0) == 0)
    def _():
        part_ref[...] = product

    @pl.when(pl.program_id(0) > 0)
    def _():
        part_ref[...] += product


def mlp_step(
    rows, inside, part, places, bit, hidden, context, other, weight, pieces, bias, gain, shift,
    up, up_bias, down, after=(), tile=512,
):
    width = hidden.shape[1]
    count = rows.stop - rows.start
    units = up.shape[1]
    ins = (places, bit, hidden, context, other, weight, *pieces, bias, gain, shift)

    def body(*refs):
        mlp_kernel(rows, inside, part, *refs[: len(ins) + 3], *refs[len(ins) + 3 + len(after) :])

    whole = lambda shape: pl.BlockSpec(shape, lambda i: (0,) * len(shape))
    half = (width // 2, lanes(count))
    return pl.pallas_call(
        body,
        out_shape=(
            like((count, width)),
            like((count, width)),
            like((count, 1)),
            like(half),
            like(half),
            like((count, units)),
            like((count, units)),
            like((count, width)),
        ),
        grid=(units // tile,),
        in_specs=[pl.BlockSpec(memory_space=pltpu.SMEM)] * 2
        + [whole(v.shape) for v in ins[2:]]
        + [
            pl.BlockSpec((width, tile), lambda i: (0, i)),
            pl.BlockSpec((1, tile), lambda i: (0, i)),
            pl.BlockSpec((tile, width), lambda i: (i, 0)),
        ]
        + [pl.BlockSpec(memory_space=pl.ANY)] * len(after),
        out_specs=(
            whole((count, width)),
            whole((count, width)),
            whole((count, 1)),
            whole(half),
            whole(half),
            pl.BlockSpec((count, tile), lambda i: (0, i)),
            pl.BlockSpec((count, tile), lambda i: (0, i)),
            whole((count, width)),
        ),
        scratch_shapes=[
            pltpu.VMEM(weight.shape, jnp.bfloat16),
            pltpu.VMEM((count, width), jnp.bfloat16),
            pltpu.VMEM((width, lanes(count)), jnp.float32),
        ],
        compiler_params=pltpu.CompilerParams(vmem_limit_bytes=VMEM_BYTES),
        cost_estimate=BRIEF,
        name="mlp",
    )(*ins, up, up_bias, down, *after)


def result_kernel(
    rows, part, scale_ref, bit_ref, middle_ref, part_ref, other_ref, bias_ref, target_ref, *outs
):
    out_ref, grad_ref, low_ref, turned_ref, given_ref, sums_ref, scratch = outs
    result = middle_ref[...] + (part_ref[...] + other_ref[...]) + bias_ref[...]
    error = result - target_ref[rows].astype(jnp.float32)
    grad = error * scale_ref[0]
    low = grad.astype(jnp.bfloat16)
    out_ref[...] = result.astype(jnp.bfloat16)
    grad_ref[...] = grad
    low_ref[...] = low
    turn(low.astype(jnp.float32), bit_ref[0], part, scratch, turned_ref, given_ref)
    sums_ref[0:1] = jnp.sum(grad, axis=0, keepdims=True)
    sums_ref[1:2] = jnp.sum(error * error, axis=0, keepdims=True)


def result_step(rows, row_part, scale, bit, middle, part, other, bias, target, after=()):
    count, width = middle.shape
    half = like((width // 2, lanes(count)))
    return local_call(
        lambda *refs: result_kernel(rows, row_part, *refs),
        (
            like((count, width), jnp.bfloat16),
            like((count, width)),
            like((count, width), jnp.bfloat16),
            half,
            half,
            like((2, width)),
        ),
        (scale, bit, middle, part, other, bias, target),
        after,
        scratch=(pltpu.VMEM((width, lanes(count)), jnp.float32),),
        smem=2,
        name="result_error",
    )


def mlp_back_kernel(low_ref, slope_ref, down_ref, up_ref, pre_ref, two_ref, sums_ref):
    pre = (dot(low_ref[...], down_ref[...], NT) * slope_ref[...]).astype(jnp.bfloat16)
    pre_ref[...] = pre.astype(jnp.float32)
    sums_ref[...] = jnp.sum(pre.astype(jnp.float32), axis=0, keepdims=True)
    two = dot(pre, up_ref[...], NT)

    @pl.when(pl.program_id(0) == 0)
    def _():
        two_ref[...] = two

    @pl.when(pl.program_id(0) > 0)
    def _():
        two_ref[...] += two


def mlp_back(low, slope, down, up, after=(), tile=512):
    count, width = low.shape
    units = up.shape[1]

    def body(*refs):
        mlp_back_kernel(*refs[:4], *refs[4 + len(after) :])

    return pl.pallas_call(
        body,
        out_shape=(
            like((count, units)),
            like((count, width)),
            like((1, units)),
        ),
        grid=(units // tile,),
        in_specs=[
            pl.BlockSpec((count, width), lambda i: (0, 0)),
            pl.BlockSpec((count, tile), lambda i: (0, i)),
            pl.BlockSpec((tile, width), lambda i: (i, 0)),
            pl.BlockSpec((width, tile), lambda i: (0, i)),
        ]
        + [pl.BlockSpec(memory_space=pl.ANY)] * len(after),
        out_specs=(
            pl.BlockSpec((count, tile), lambda i: (0, i)),
            pl.BlockSpec((count, width), lambda i: (0, 0)),
            pl.BlockSpec((1, tile), lambda i: (0, i)),
        ),
        compiler_params=pltpu.CompilerParams(vmem_limit_bytes=VMEM_BYTES),
        cost_estimate=BRIEF,
        name="mlp_back",
    )(low, slope, down, up, *after)


def middle_back_kernel(
    row_part, bit_ref, part_ref, other_ref, grad_ref, normed_ref, inverse_ref, gain_ref, weight_ref,
    *outs
):
    mid_ref, turned_ref, given_ref, context_ref, sums_ref, scratch = outs
    grad_two = part_ref[...] + other_ref[...]
    normed = normed_ref[...]
    mid = grad_ref[...] + norm_back(grad_two, normed, inverse_ref[...], gain_ref[...])
    low = mid.astype(jnp.bfloat16)
    mid_ref[...] = mid
    context_ref[...] = dot(low, weight_ref[...], NT).astype(jnp.bfloat16)
    turn(low.astype(jnp.float32), bit_ref[0], row_part, scratch, turned_ref, given_ref)
    sums_ref[0:1] = jnp.sum(mid, axis=0, keepdims=True)
    sums_ref[1:2] = jnp.sum(grad_two * normed, axis=0, keepdims=True)
    sums_ref[2:3] = jnp.sum(grad_two, axis=0, keepdims=True)


def middle_back(row_part, bit, part, other, grad, normed, inverse, gain, weight, after=()):
    count, width = grad.shape
    half = like((width // 2, lanes(count)))
    return local_call(
        lambda *refs: middle_back_kernel(row_part, *refs),
        (
            like((count, width)),
            half,
            half,
            like((count, weight.shape[0]), jnp.bfloat16),
            like((3, width)),
        ),
        (bit, part, other, grad, normed, inverse, gain, weight),
        after,
        scratch=(pltpu.VMEM((width, lanes(count)), jnp.float32),),
        smem=1,
        name="middle_back",
    )


def project_back_kernel(grads_ref, weight_ref, state_ref, part_ref, sums_ref, bias_ref):
    width = weight_ref.shape[2]
    low = lambda j: grads_ref[:, j * width : (j + 1) * width].astype(jnp.bfloat16)
    part = dot(low(0), weight_ref[0], NT)
    for j in (1, 2):
        part = part + dot(low(j), weight_ref[j], NT)
    part_ref[...] = part
    normed = layer_norm(state_ref[...].astype(jnp.float32), 1.0, 0.0)[1]
    sums_ref[0:1] = jnp.sum(part * normed, axis=0, keepdims=True)
    sums_ref[1:2] = jnp.sum(part, axis=0, keepdims=True)
    bias_ref[...] = jnp.sum(grads_ref[...], axis=0, keepdims=True)


def project_back(grads, weight, states, after=()):
    rows, width = states.shape
    return local_call(
        project_back_kernel,
        (like((rows, width)), like((2, width)), like((1, grads.shape[1]))),
        (grads, weight, states),
        after,
        name="project_back",
    )


def last_kernel(count, part_ref, other_ref, state_ref, gain_ref, *refs):
    mids, results, (grad_ref, out_ref) = refs[:count], refs[count : 2 * count], refs[2 * count :]
    start = 0
    for mid, result in zip(mids, results):
        rows = slice(start, start + mid.shape[0])
        _, normed, inverse = layer_norm(state_ref[rows].astype(jnp.float32), 1.0, 0.0)
        grad_one = part_ref[rows] + other_ref[rows]
        grad_ref[rows] = (
            mid[...] + norm_back(grad_one, normed, inverse, gain_ref[...])
        ).astype(jnp.bfloat16)
        out_ref[rows] = result[...]
        start = rows.stop


def last_step(mids, part, other, states, gain, results, after=()):
    return local_call(
        lambda *refs: last_kernel(len(mids), *refs),
        (like(states.shape, jnp.bfloat16),) * 2,
        (part, other, states, gain, *mids, *results),
        after,
        name="input_grad",
    )


def outer_kernel(high, low, plans, bit_ref, *refs):
    count = sum(len(lefts) + rights for _, lefts, rights in plans)
    operands, (give_ref, keep_ref), scratch = refs[:count], refs[count : count + 2], refs[count + 2 :]
    rounded, full = list(scratch[:-1]), scratch[-1]
    operands = list(operands)
    for (first, last), lefts, rights in plans:
        left_refs = [operands.pop(0) for _ in lefts]
        right_refs = [operands.pop(0) for _ in range(rights)]
        low_refs = [rounded.pop(0) for _ in lefts]

        @pl.when(pl.program_id(0) == first)
        def _():
            for out, left in zip(low_refs, left_refs):
                out[...] = left[:, : out.shape[1]].astype(jnp.bfloat16)

        @pl.when((pl.program_id(0) >= first) & (pl.program_id(0) < last))
        def _():
            total = None
            for out, (index, rows) in zip(low_refs, lefts):
                product = dot(out[...], right_refs[index][rows].astype(jnp.bfloat16))
                total = product if total is None else total + product
            full[...] = total

    part_blocks(full, bit_ref[0], high, low, keep_ref, give_ref)


def outer_sum(bit, high, groups, after=(), tile=512):
    width = groups[0][0][0][0].shape[0]
    low = width // (2 * high)
    operands, specs, scratch, plans = [], [], [], []
    first = 0
    for lefts, rights, start, columns in groups:
        last = first + columns // tile
        places, index, row = [], 0, 0
        for v, rows in lefts:
            operands.append(v)
            specs.append(pl.BlockSpec(v.shape, lambda i: (0, 0)))
            scratch.append(pltpu.VMEM((width, rows), jnp.bfloat16))
            if row == rights[index].shape[0]:
                index, row = index + 1, 0
            places.append((index, slice(row, row + rows)))
            row += rows
        for v in rights:
            operands.append(v)
            place = lambda i, s=start // tile, f=first, n=last - first: (
                0,
                s + jnp.clip(i - f, 0, n - 1),
            )
            specs.append(pl.BlockSpec((v.shape[0], tile), place))
        plans.append(((first, last), places, len(rights)))
        first = last

    def body(*refs):
        count = 1 + len(operands)
        outer_kernel(high, low, plans, *refs[:count], *refs[count + len(after) :])

    return pl.pallas_call(
        body,
        out_shape=(like((width // 2, first * tile)),) * 2,
        grid=(first,),
        in_specs=[pl.BlockSpec(memory_space=pltpu.SMEM)]
        + specs
        + [pl.BlockSpec(memory_space=pl.ANY)] * len(after),
        out_specs=(pl.BlockSpec((width // 2, tile), lambda i: (0, i)),) * 2,
        scratch_shapes=scratch + [pltpu.VMEM((width, tile), jnp.float32)],
        compiler_params=pltpu.CompilerParams(vmem_limit_bytes=VMEM_BYTES),
        cost_estimate=BRIEF,
        name="weight_grad",
    )(bit, *operands, *after)


def split_kernel(bit_ref, keep_ref, came_ref, give_out, keep_out):
    bit = bit_ref[0]
    keep_out[0] = keep_ref[0, bit] + came_ref[0, bit]
    give_out[0] = keep_ref[0, 1 - bit] + came_ref[0, 1 - bit]


def add_split(bit, keep, came, high, after=()):
    rows, columns = keep.shape
    low = rows // (2 * high)
    halves = (high, 2, low, columns)

    def body(*refs):
        split_kernel(*refs[:3], *refs[3 + len(after) :])

    give, kept = pl.pallas_call(
        body,
        out_shape=(like((high, low, columns)),) * 2,
        grid=(high,),
        in_specs=[pl.BlockSpec(memory_space=pltpu.SMEM)]
        + [pl.BlockSpec((1, 2, low, columns), lambda i: (i, 0, 0, 0))] * 2
        + [pl.BlockSpec(memory_space=pl.ANY)] * len(after),
        out_specs=(pl.BlockSpec((1, low, columns), lambda i: (i, 0, 0)),) * 2,
        compiler_params=pltpu.CompilerParams(vmem_limit_bytes=VMEM_BYTES),
        cost_estimate=BRIEF,
        name="add_split",
    )(bit, keep.reshape(halves), came.reshape(halves), *after)
    return give.reshape(rows // 2, columns), kept.reshape(rows // 2, columns)


def tie(value, *others):
    return lax.optimization_barrier((value, *others))[0]


def make_shards(mesh):
    groups = mesh.shape["dp"]
    bits = groups.bit_length() - 1
    assert groups == 1 << bits and mesh.shape["tensor"] == 2

    def swap_tensor(value):
        return lax.ppermute(value, "tensor", [(0, 1), (1, 0)])

    def swap_bit(value, bit):
        return lax.ppermute(value, "dp", [(i, i ^ (1 << bit)) for i in range(groups)])

    def sum_dp(value):
        for bit in range(bits):
            value = value + swap_bit(value, bit)
        return value

    def own_bit(bit):
        return ((lax.axis_index("dp") >> bit) & 1).astype(jnp.int32).reshape(1)

    class Scatter:
        def __init__(self, groups_of, order, after=()):
            self.left = list(range(1, bits))[::-1]
            self.order = list(order)
            bit = self.order[0]
            self.give, self.keep = outer_sum(
                own_bit(bit), 1 << self.left.index(bit), groups_of, after
            )
            self.came = None

        def send(self):
            bit = self.order.pop(0)
            self.came = swap_bit(self.give, bit)
            self.left.remove(bit)
            self.give = None

        def fold(self):
            bit = self.order[0]
            self.give, self.keep = add_split(
                own_bit(bit), self.keep, self.came, 1 << self.left.index(bit)
            )
            self.came = None

        def move(self):
            self.fold()
            self.send()

        def finish(self):
            while self.order:
                self.move()
            return self.keep + self.came

    def sync(scatters, *arrays):
        held = [(one.give, one.keep, one.came) for one in scatters]
        held, arrays = lax.optimization_barrier((held, arrays))
        for one, (give, keep, came) in zip(scatters, held):
            one.give, one.keep, one.came = give, keep, came
        return arrays

    def shards(
        images,
        teacher,
        image_mask,
        attn_gain,
        attn_shift,
        in_weight,
        in_bias,
        out_weight,
        out_bias,
        mlp_gain,
        mlp_shift,
        up_weight,
        up_bias,
        down_weight,
        down_bias,
    ):
        image_count, seq_len, width = images.shape
        row_count = image_count * seq_len
        local_width = in_weight.shape[2]
        gain_one = attn_gain.astype(jnp.float32)[None]
        shift_one = attn_shift.astype(jnp.float32)[None]
        gain_two = mlp_gain.astype(jnp.float32)[None]
        shift_two = mlp_shift.astype(jnp.float32)[None]
        bias_in = in_bias.astype(jnp.float32)
        bias_out = out_bias.astype(jnp.float32)[None]
        bias_up = up_bias.astype(jnp.float32)[None]
        bias_down = down_bias.astype(jnp.float32)[None]
        chunks, start = [], 0
        for stop in (304, row_count):
            chunks.append(slice(start, stop))
            start = stop
        cut = chunks[0].stop
        part = width // groups
        core_bit = own_bit(0)
        low_first = tuple(range(1, bits))
        high_first = tuple(range(2, bits)) + (1,)
        swap_core = lambda value: swap_bit(value, 0)

        quarter = local_width // 4
        dp_index = lax.axis_index("dp")
        piece = lax.dynamic_slice_in_dim(out_weight, (dp_index & 3) * quarter, quarter, axis=0)
        pieces = [swap_tensor(piece.astype(jnp.float32))]
        places = jnp.stack([(dp_index & 3) ^ way for way in (0, 2, 1, 3)]).astype(jnp.int32)

        states = images.reshape(row_count, width)
        targets = teacher.reshape(row_count, width)
        act_one = layer_norm(states.astype(jnp.float32), gain_one, shift_one)[0].astype(jnp.bfloat16)
        query = (dot(act_one, in_weight[:, 0]) + bias_in[0]).astype(jnp.bfloat16)
        key = dot(act_one, in_weight[:, 1]).astype(jnp.bfloat16)
        value = (dot(act_one, in_weight[:, 2]) + bias_in[1]).astype(jnp.bfloat16)
        context_first, context_second, log_total = attend(query, key, value, cut)
        context = (context_first, context_second)
        context_other = [swap_tensor(one) for one in context]
        pieces.append(swap_bit(tie(pieces[0], log_total), 1))
        pieces += [swap_core(one) for one in pieces]

        valid = tie(image_mask, log_total).astype(jnp.float32)[0]
        count_all = sum_dp(jnp.full((8, 128), valid * seq_len, jnp.float32))[:1, 0]
        scale = 2.0 * valid / count_all
        turned_one, given_one = turn_step(core_bit, act_one, part, (log_total,))

        middle, normed_two, inverse_two, turned_two, given_two, inner, slope, mlp_part = mlp_out = [
            [] for _ in range(8)
        ]
        scale, turned_one, context_other, pieces = sync([], scale, turned_one, context_other, pieces)

        def mlp_of(i):
            rows = chunks[i]
            step = mlp_step(
                rows,
                slice(0, rows.stop - rows.start),
                part,
                places,
                core_bit,
                states,
                context[i],
                context_other[i],
                out_weight,
                pieces,
                bias_out,
                gain_two,
                shift_two,
                up_weight,
                bias_up,
                down_weight,
            )
            for kept, one in zip(mlp_out, step):
                kept.append(one)

        mlp_of(0)
        mlp_part, context_other, given_two, inner = sync(
            [], mlp_part, context_other, given_two, inner
        )
        mlp_out[4], mlp_out[5], mlp_out[7] = given_two, inner, mlp_part
        mlp_other = [swap_tensor(mlp_part[0])]
        came_two, came_inner = [swap_core(given_two[0])], [swap_core(inner[0])]
        mlp_of(1)
        mlp_part[1], given_two[1], inner[1], came_two, came_inner = sync(
            [], mlp_part[1], given_two[1], inner[1], came_two, came_inner
        )
        mlp_other.append(swap_tensor(mlp_part[1]))
        (mlp_other[0],) = sync([], mlp_other[0])

        result, grad_result, grad_low, turned_low, given_low, result_sums = result_out = [
            [] for _ in range(6)
        ]
        grad_pre, two_part, up_sums = back_out = [[], [], []]
        two_other = []

        def result_of(i, after):
            step = result_step(
                chunks[i],
                part,
                scale,
                core_bit,
                middle[i],
                mlp_part[i],
                mlp_other[i],
                bias_down,
                targets,
                after,
            )
            for kept, one in zip(result_out, step):
                kept.append(one)

        def back_of(i, after):
            step = mlp_back(grad_low[i], slope[i], down_weight, up_weight, after)
            for kept, one in zip(back_out, step):
                kept.append(one)
            two_other.append(swap_tensor(two_part[i]))
            return (two_part[i],)

        grad_middle, turned_attn, given_attn, grad_context, middle_sums = middle_out = [
            [] for _ in range(5)
        ]

        def middle_of(i, after):
            step = middle_back(
                part,
                core_bit,
                two_part[i],
                two_other[i],
                grad_result[i],
                normed_two[i],
                inverse_two[i],
                gain_two,
                out_weight,
                after,
            )
            for kept, one in zip(middle_out, step):
                kept.append(one)
            return (grad_context[i],)

        def small_of(first, in_sums):
            result_all = sum(result_sums)
            middle_all = sum(middle_sums)
            pieces = [
                first.reshape(-1),
                in_sums[0, :local_width],
                in_sums[0, 2 * local_width :],
                middle_all.reshape(-1),
                sum(up_sums).reshape(-1),
                result_all[0],
                jnp.full((128,), valid * jnp.sum(result_all[1])),
            ]
            return jnp.concatenate(pieces).reshape(-1, 128)

        def rows_of(values):
            return [(one, rows.stop - rows.start) for one, rows in zip(values, chunks * 2)]

        half = up_weight.shape[1] // 2
        result_of(0, ())
        token = back_of(0, ())
        (mlp_other[1], *token) = sync([], mlp_other[1], *token)
        result_of(1, token)

        given_low, grad_low[1], slope[1], inner[1], context = sync(
            [], given_low, grad_low[1], slope[1], inner[1], context
        )
        came_low = [swap_core(one) for one in given_low]
        came_inner.append(swap_core(inner[1]))
        came_context = [swap_core(one) for one in context]
        back_of(1, ())
        came_low, came_inner, came_context, grad_pre, given_two = sync(
            [], came_low, came_inner, came_context, grad_pre, given_two
        )

        came_pre = [swap_core(one) for one in grad_pre]
        came_two.append(swap_core(given_two[1]))
        left, right = rows_of(turned_low + came_low), inner + came_inner
        down_a = Scatter([(left, right, 0, half)], high_first)
        down_b = Scatter([(left, right, half, half)], low_first, (down_a.give,))
        came_pre, came_two = sync([down_a, down_b], came_pre, came_two)

        down_b.send()
        down_a.send()
        left, right = rows_of(turned_two + came_two), grad_pre + came_pre
        up_a = Scatter([(left, right, 0, half)], low_first)
        up_b = Scatter([(left, right, half, half)], low_first, (up_a.give,))
        two_other[0], given_one = sync([down_a, down_b, up_a, up_b], two_other[0], given_one)

        came_one = swap_core(given_one)
        up_a.send()
        down_a.move()
        down_b.move()
        token = middle_of(0, ())
        middle_of(1, token)
        grads = attend_back(query, key, value, log_total, grad_context)
        grads, given_attn, came_one = sync([down_a, down_b, up_a, up_b], grads, given_attn, came_one)

        up_b.send()
        came_grads = swap_core(grads)
        came_attn = [swap_core(one) for one in given_attn]
        one_part, one_sums, in_sums = project_back(grads, jnp.swapaxes(in_weight, 0, 1), states)
        first = swap_tensor(one_sums)
        came_grads, came_attn, one_part, first = sync(
            [down_a, down_b, up_a, up_b], came_grads, came_attn, one_part, first
        )

        one_other = swap_tensor(one_part)
        up_a.move()
        down_b.move()
        down_a.move()
        left = [(turned_one, row_count), (came_one, row_count)]
        right = [grads, came_grads]
        in_a = Scatter([(left, right, 0, 2 * local_width)], low_first)
        in_b = Scatter(
            [
                (left, right, 2 * local_width, local_width),
                (
                    rows_of(turned_attn + came_attn),
                    list(context) + came_context,
                    0,
                    local_width,
                ),
            ],
            low_first,
            (in_a.give,),
        )
        small = small_of(first + one_sums, in_sums)
        (small,) = sync([down_a, down_b, up_a, up_b, in_a, in_b], small)

        in_a.send()
        up_b.move()
        up_a.move()
        full_down = jnp.concatenate([down_a.finish(), down_b.finish()], axis=1)
        more = swap_bit(small, 0)
        small, more, full_down = sync([up_a, up_b, in_a, in_b], small, more, full_down)

        in_b.send()
        in_a.move()
        up_b.move()
        small = small + more
        more = swap_bit(small, 1)
        small, more, one_other = sync([up_a, up_b, in_a, in_b], small, more, one_other)

        in_b.move()
        in_a.move()
        full_up = jnp.concatenate([up_a.finish(), up_b.finish()], axis=1)
        grad_images, block_out = last_step(
            grad_middle, one_part, one_other, states, gain_one, result
        )
        small = small + more
        more = swap_bit(small, 2)
        small, more, full_up, grad_images, block_out = sync(
            [in_a, in_b], small, more, full_up, grad_images, block_out
        )

        in_b.move()
        small = small + more
        for bit in range(3, bits):
            small = small + swap_bit(small, bit)
        full_in_a = in_a.finish()
        full_in_b = in_b.finish()
        full_in = jnp.concatenate([full_in_a, full_in_b[:, :local_width]], axis=1)
        full_out = full_in_b[:, local_width:]
        sizes = (width, width, 2 * local_width, width, width, width, up_bias.shape[0], width, 128)
        small = small.reshape(-1)
        bits_of = []
        start = 0
        for size in sizes:
            bits_of.append(small[start : start + size])
            start += size
        shape = (image_count, seq_len, width)
        return (
            block_out.reshape(shape),
            bits_of[8][0] / count_all[0],
            grad_images.reshape(shape),
            bits_of[0],
            bits_of[1],
            full_in.reshape(-1, 3, local_width),
            bits_of[2].reshape(2, local_width),
            full_out.T,
            bits_of[3],
            bits_of[4],
            bits_of[5],
            full_up,
            bits_of[6],
            full_down.T,
            bits_of[7],
        )

    return shards


def solution(mesh):
    placed = (
        P("dp", None, None),
        P("dp", None, None),
        P("dp"),
        P(),
        P(),
        P(None, None, "tensor"),
        P(None, "tensor"),
        P("tensor", None),
        P(),
        P(),
        P(),
        P(None, "tensor"),
        P("tensor"),
        P("tensor", None),
        P(),
    )
    return jax.shard_map(
        make_shards(mesh),
        mesh=mesh,
        in_specs=placed,
        out_specs=(
            P("dp", None, None),
            P(),
            P("dp", None, None),
            P(),
            P(),
            P("dp", None, "tensor"),
            P(None, "tensor"),
            P("tensor", "dp"),
            P(),
            P(),
            P(),
            P("dp", "tensor"),
            P("tensor"),
            P("tensor", "dp"),
            P(),
        ),
        check_vma=False,
    )
```

```python
import jax
import jax.numpy as jnp
from jax import lax
from jax.experimental import pallas as pl
from jax.experimental.pallas import tpu as pltpu
from jax.sharding import PartitionSpec as P

HD = 64

epsilon = 1e-05
score_scale = 0.125
quick_rate = 1.702
log2_e = 1.4426950408889634
score_rate = score_scale * log2_e

NN = (((1,), (0,)), ((), ()))
NT = (((1,), (1,)), ((), ()))
VMEM_BYTES = 48 * 2**20
BRIEF = pl.CostEstimate(flops=1, bytes_accessed=1, transcendentals=0)


def dot(matrix_a, matrix_b, dims=NN):
    return lax.dot_general(matrix_a, matrix_b, dims, preferred_element_type=jnp.float32)


def layer_norm(hidden, scales, offset):
    centred = hidden - jnp.mean(hidden, axis=-1, keepdims=True)
    inverse = lax.rsqrt(jnp.mean(centred * centred, axis=-1, keepdims=True) + epsilon)
    normed = centred * inverse
    return (normed * scales + offset, normed, inverse)


def norm_back(grad_out, normed, inverse, scales):
    scaled = grad_out * scales
    centred = scaled - jnp.mean(scaled, axis=-1, keepdims=True)
    return (centred - normed * jnp.mean(scaled * normed, axis=-1, keepdims=True)) * inverse


def first_head(shape):
    return lax.broadcasted_iota(jnp.int32, shape, len(shape) - 1) < HD


def local_call(
    kernel, outs, ins, after=(), scratch=(), smem=0, name=None
):
    count = len(ins)

    def body(*refs):
        kernel(*refs[:count], *refs[count + len(after) :])

    return pl.pallas_call(
        body,
        out_shape=tuple(outs),
        in_specs=[pl.BlockSpec(memory_space=pltpu.SMEM)] * smem
        + [pl.BlockSpec(memory_space=pltpu.VMEM)] * (count - smem)
        + [pl.BlockSpec(memory_space=pl.ANY)] * len(after),
        out_specs=tuple(pl.BlockSpec(memory_space=pltpu.VMEM) for _ in outs),
        scratch_shapes=list(scratch),
        compiler_params=pltpu.CompilerParams(vmem_limit_bytes=VMEM_BYTES),
        cost_estimate=BRIEF,
        name=name,
    )(*ins, *after)


def part_blocks(source, bit, high, low, keep_ref, give_ref):
    for j in range(high):
        keep_ref[low * j : low * (j + 1)] = source[
            pl.ds(pl.multiple_of((2 * j + bit) * low, 8), low)
        ]
        give_ref[low * j : low * (j + 1)] = source[
            pl.ds(pl.multiple_of((2 * j + 1 - bit) * low, 8), low)
        ]


def lanes(rows):
    return -(-rows // 128) * 128


def turn(value, bit, part, scratch, keep_ref, give_ref):
    rows = value.shape[0]
    scratch[:, :rows] = jnp.transpose(value)
    if scratch.shape[1] > rows:
        scratch[:, rows:] = jnp.zeros((scratch.shape[0], scratch.shape[1] - rows), jnp.float32)
    part_blocks(scratch, bit, value.shape[1] // (2 * part), part, keep_ref, give_ref)


def like(shape, dtype=jnp.float32):
    return jax.ShapeDtypeStruct(shape, dtype)


def enter_kernel(state_ref, scales_ref, weight_ref, bias_ref, act_ref, out_ref):
    which = pl.program_id(0)

    @pl.when(which == 0)
    def _():
        act_ref[...] = layer_norm(
            state_ref[...].astype(jnp.float32), scales_ref[0:1], scales_ref[1:2]
        )[0].astype(jnp.bfloat16)

    biases = bias_ref[...].astype(jnp.float32)
    zero = jnp.zeros_like(biases[0:1])
    bias = jnp.where(which == 0, biases[0:1], jnp.where(which == 2, biases[1:2], zero))
    out_ref[0] = (dot(act_ref[...], weight_ref[0]) + bias).astype(jnp.bfloat16)


def enter(states, scales, weight, bias):
    rows, width = states.shape
    local = weight.shape[2]
    return pl.pallas_call(
        enter_kernel,
        out_shape=(
            like((rows, width), jnp.bfloat16),
            like((3, rows, local), jnp.bfloat16),
        ),
        grid=(3,),
        in_specs=[
            pl.BlockSpec((rows, width), lambda i: (0, 0)),
            pl.BlockSpec((2, width), lambda i: (0, 0)),
            pl.BlockSpec((1, width, local), lambda i: (i, 0, 0)),
            pl.BlockSpec((2, local), lambda i: (0, 0)),
        ],
        out_specs=(
            pl.BlockSpec((rows, width), lambda i: (0, 0)),
            pl.BlockSpec((1, rows, local), lambda i: (i, 0, 0)),
        ),
        compiler_params=pltpu.CompilerParams(vmem_limit_bytes=VMEM_BYTES),
        cost_estimate=BRIEF,
        name="norm_project",
    )(states, scales, weight, bias)


def attend_kernel(projected_ref, first_ref, second_ref, log_ref):
    _, seq_len, width = projected_ref.shape
    cut = first_ref.shape[0]
    low = first_head((seq_len, 2 * HD))
    zero = jnp.zeros((), jnp.bfloat16)
    for pair in range(width // (2 * HD)):
        start, stop = 2 * HD * pair, 2 * HD * (pair + 1)
        cols = slice(start, stop)
        query, key = projected_ref[0, :, cols], projected_ref[1, :, cols]
        value_t = jnp.transpose(projected_ref[2, :, cols])
        parts = []
        for half in range(2):
            one_key = jnp.where(low if half == 0 else ~low, key, zero)
            scores = dot(one_key, query, NT)
            top = jnp.max(scores, axis=0, keepdims=True)
            weights = jnp.exp2((scores - top) * score_rate)
            total = jnp.sum(weights, axis=0, keepdims=True)
            weights_low = (weights * (1.0 / total)).astype(jnp.bfloat16)
            parts.append(dot(value_t[HD * half : HD * (half + 1)], weights_low))
            head = 2 * pair + half
            log_ref[head : head + 1, :] = top * score_rate + jnp.log2(total)
        context = jnp.transpose(jnp.concatenate(parts, axis=0)).astype(jnp.bfloat16)
        context = context.astype(jnp.float32)
        first_ref[:, cols] = context[:cut]
        second_ref[:, cols] = context[cut:]


def attend(projected, cut, after=()):
    _, rows, width = projected.shape
    return local_call(
        attend_kernel,
        (like((cut, width)), like((rows - cut, width)), like((width // HD, rows))),
        (projected,),
        after,
        name="attend",
    )


def turn_step(bit, value, part, after=()):
    rows, width = value.shape
    half = like((width // 2, lanes(rows)))

    def kernel(bit_ref, value_ref, keep_ref, give_ref, scratch):
        turn(value_ref[...].astype(jnp.float32), bit_ref[0], part, scratch, keep_ref, give_ref)

    return local_call(
        kernel,
        (half, half),
        (bit, value),
        after,
        scratch=(pltpu.VMEM((width, lanes(rows)), jnp.float32),),
        smem=1,
        name="turn",
    )


def attend_back_kernel(projected_ref, log_ref, *refs):
    grad_refs, grads_ref = refs[:-1], refs[-1]
    _, seq_len, width = projected_ref.shape
    low = first_head((seq_len, 2 * HD))
    zero = jnp.zeros((), jnp.bfloat16)
    round_low = lambda v: v.astype(jnp.bfloat16).astype(jnp.float32)
    for pair in range(width // (2 * HD)):
        start, stop = 2 * HD * pair, 2 * HD * (pair + 1)
        cols = slice(start, stop)
        query, key, value = (projected_ref[j, :, cols] for j in range(3))
        grad = jnp.concatenate([one[:, cols] for one in grad_refs], axis=0)
        key_t = jnp.transpose(key)
        grad_query, grad_key, grad_value = [], [], []
        for half in range(2):
            kept = low if half == 0 else ~low
            head = 2 * pair + half
            scores = dot(jnp.where(kept, key, zero), query, NT)
            weights = jnp.exp2(scores * score_rate - log_ref[head : head + 1, :])
            grad_weights = dot(jnp.where(kept, value, zero), grad, NT)
            grad_value.append(dot(weights.astype(jnp.bfloat16), grad))
            row_sum = jnp.sum(grad_weights * weights, axis=0, keepdims=True)
            grad_scores = (weights * (grad_weights - row_sum)).astype(jnp.bfloat16)
            grad_key.append(dot(grad_scores, query))
            grad_query.append(dot(key_t[HD * half : HD * (half + 1)], grad_scores))
        grads_ref[:, start:stop] = round_low(
            jnp.transpose(jnp.concatenate(grad_query, axis=0)) * score_scale
        )
        grads_ref[:, width + start : width + stop] = round_low(
            jnp.where(low, grad_key[0], grad_key[1]) * score_scale
        )
        grads_ref[:, 2 * width + start : 2 * width + stop] = round_low(
            jnp.where(low, grad_value[0], grad_value[1])
        )


def attend_back(projected, log_total, grad_context, after=()):
    _, seq_len, width = projected.shape
    return local_call(
        attend_back_kernel,
        (like((seq_len, 3 * width)),),
        (projected, log_total, *grad_context),
        after,
        name="attend_back",
    )[0]


def mlp_kernel(
    rows, inside, part, places_ref, bit_ref, hidden_ref, context_ref, other_ref, weight_ref, *refs
):
    pieces, (bias_ref, gain_ref, shift_ref, up_ref, up_bias_ref, down_ref) = refs[:4], refs[4:10]
    middle_ref, normed_ref, inverse_ref, turned_ref, given_ref, inner_ref, slope_ref, part_ref = (
        refs[10:18]
    )
    weight_other, act_ref, scratch = refs[18:]

    @pl.when(pl.program_id(0) == 0)
    def _():
        block = pieces[0].shape[0]
        for i, piece in enumerate(pieces):
            start = pl.multiple_of(places_ref[i] * block, block)
            weight_other[pl.ds(start, block)] = piece[...].astype(jnp.bfloat16)
        branch = dot(context_ref[inside].astype(jnp.bfloat16), weight_ref[...]) + dot(
            other_ref[inside].astype(jnp.bfloat16), weight_other[...]
        )
        middle = hidden_ref[rows].astype(jnp.float32) + branch + bias_ref[...]
        normed_out, normed, inverse = layer_norm(middle, gain_ref[...], shift_ref[...])
        middle_ref[...] = middle
        normed_ref[...] = normed
        inverse_ref[...] = inverse
        act = normed_out.astype(jnp.bfloat16)
        act_ref[...] = act
        turn(act.astype(jnp.float32), bit_ref[0], part, scratch, turned_ref, given_ref)

    pre_act = dot(act_ref[...], up_ref[...]) + up_bias_ref[...]
    sigma = 0.5 + 0.5 * jnp.tanh((0.5 * quick_rate) * pre_act)
    inner = (pre_act * sigma).astype(jnp.bfloat16)
    inner_ref[...] = inner.astype(jnp.float32)
    slope_ref[...] = sigma + pre_act * quick_rate * sigma * (1.0 - sigma)
    product = dot(inner, down_ref[...])

    @pl.when(pl.program_id(0) == 0)
    def _():
        part_ref[...] = product

    @pl.when(pl.program_id(0) > 0)
    def _():
        part_ref[...] += product


def mlp_step(
    rows, inside, part, places, bit, hidden, context, other, weight, pieces, bias, gain, shift,
    up, up_bias, down, after=(), tile=512,
):
    width = hidden.shape[1]
    count = rows.stop - rows.start
    units = up.shape[1]
    ins = (places, bit, hidden, context, other, weight, *pieces, bias, gain, shift)

    def body(*refs):
        mlp_kernel(rows, inside, part, *refs[: len(ins) + 3], *refs[len(ins) + 3 + len(after) :])

    whole = lambda shape: pl.BlockSpec(shape, lambda i: (0,) * len(shape))
    half = (width // 2, lanes(count))
    return pl.pallas_call(
        body,
        out_shape=(
            like((count, width)),
            like((count, width)),
            like((count, 1)),
            like(half),
            like(half),
            like((count, units)),
            like((count, units)),
            like((count, width)),
        ),
        grid=(units // tile,),
        in_specs=[pl.BlockSpec(memory_space=pltpu.SMEM)] * 2
        + [whole(v.shape) for v in ins[2:]]
        + [
            pl.BlockSpec((width, tile), lambda i: (0, i)),
            pl.BlockSpec((1, tile), lambda i: (0, i)),
            pl.BlockSpec((tile, width), lambda i: (i, 0)),
        ]
        + [pl.BlockSpec(memory_space=pl.ANY)] * len(after),
        out_specs=(
            whole((count, width)),
            whole((count, width)),
            whole((count, 1)),
            whole(half),
            whole(half),
            pl.BlockSpec((count, tile), lambda i: (0, i)),
            pl.BlockSpec((count, tile), lambda i: (0, i)),
            whole((count, width)),
        ),
        scratch_shapes=[
            pltpu.VMEM(weight.shape, jnp.bfloat16),
            pltpu.VMEM((count, width), jnp.bfloat16),
            pltpu.VMEM((width, lanes(count)), jnp.float32),
        ],
        compiler_params=pltpu.CompilerParams(vmem_limit_bytes=VMEM_BYTES),
        cost_estimate=BRIEF,
        name="mlp",
    )(*ins, up, up_bias, down, *after)


def result_kernel(
    rows, part, scale_ref, bit_ref, middle_ref, part_ref, other_ref, bias_ref, target_ref, *outs
):
    out_ref, grad_ref, low_ref, turned_ref, given_ref, sums_ref, scratch = outs
    result = middle_ref[...] + (part_ref[...] + other_ref[...]) + bias_ref[...]
    error = result - target_ref[rows].astype(jnp.float32)
    grad = error * scale_ref[0]
    low = grad.astype(jnp.bfloat16)
    out_ref[...] = result.astype(jnp.bfloat16)
    grad_ref[...] = grad
    low_ref[...] = low
    turn(low.astype(jnp.float32), bit_ref[0], part, scratch, turned_ref, given_ref)
    sums_ref[0:1] = jnp.sum(grad, axis=0, keepdims=True)
    sums_ref[1:2] = jnp.sum(error * error, axis=0, keepdims=True)


def result_step(rows, row_part, scale, bit, middle, part, other, bias, target, after=()):
    count, width = middle.shape
    half = like((width // 2, lanes(count)))
    return local_call(
        lambda *refs: result_kernel(rows, row_part, *refs),
        (
            like((count, width), jnp.bfloat16),
            like((count, width)),
            like((count, width), jnp.bfloat16),
            half,
            half,
            like((2, width)),
        ),
        (scale, bit, middle, part, other, bias, target),
        after,
        scratch=(pltpu.VMEM((width, lanes(count)), jnp.float32),),
        smem=2,
        name="result_error",
    )


def mlp_back_kernel(low_ref, slope_ref, down_ref, up_ref, pre_ref, two_ref, sums_ref):
    pre = (dot(low_ref[...], down_ref[...], NT) * slope_ref[...]).astype(jnp.bfloat16)
    pre_ref[...] = pre.astype(jnp.float32)
    sums_ref[...] = jnp.sum(pre.astype(jnp.float32), axis=0, keepdims=True)
    two = dot(pre, up_ref[...], NT)

    @pl.when(pl.program_id(0) == 0)
    def _():
        two_ref[...] = two

    @pl.when(pl.program_id(0) > 0)
    def _():
        two_ref[...] += two


def mlp_back(low, slope, down, up, after=(), tile=512):
    count, width = low.shape
    units = up.shape[1]

    def body(*refs):
        mlp_back_kernel(*refs[:4], *refs[4 + len(after) :])

    return pl.pallas_call(
        body,
        out_shape=(
            like((count, units)),
            like((count, width)),
            like((1, units)),
        ),
        grid=(units // tile,),
        in_specs=[
            pl.BlockSpec((count, width), lambda i: (0, 0)),
            pl.BlockSpec((count, tile), lambda i: (0, i)),
            pl.BlockSpec((tile, width), lambda i: (i, 0)),
            pl.BlockSpec((width, tile), lambda i: (0, i)),
        ]
        + [pl.BlockSpec(memory_space=pl.ANY)] * len(after),
        out_specs=(
            pl.BlockSpec((count, tile), lambda i: (0, i)),
            pl.BlockSpec((count, width), lambda i: (0, 0)),
            pl.BlockSpec((1, tile), lambda i: (0, i)),
        ),
        compiler_params=pltpu.CompilerParams(vmem_limit_bytes=VMEM_BYTES),
        cost_estimate=BRIEF,
        name="mlp_back",
    )(low, slope, down, up, *after)


def middle_back_kernel(
    row_part, before, bit_ref, part_ref, other_ref, grad_ref, normed_ref, inverse_ref, gain_ref,
    weight_ref, *refs
):
    earlier, outs = refs[: 2 * before], refs[2 * before :]
    mid_ref, turned_ref, given_ref, context_ref, sums_ref, scratch = outs
    grad_two = part_ref[...] + other_ref[...]
    normed = normed_ref[...]
    mid = grad_ref[...] + norm_back(grad_two, normed, inverse_ref[...], gain_ref[...])
    low = mid.astype(jnp.bfloat16)
    mid_ref[...] = mid
    context_ref[...] = dot(low, weight_ref[...], NT).astype(jnp.bfloat16)
    rows = low.shape[0]
    start = turned_ref.shape[1] - lanes(rows)
    if before:
        turned_ref[:, :start] = earlier[0][...]
        given_ref[:, :start] = earlier[1][...]
    turn(
        low.astype(jnp.float32),
        bit_ref[0],
        row_part,
        scratch,
        turned_ref.at[:, start:],
        given_ref.at[:, start:],
    )
    sums_ref[0:1] = jnp.sum(mid, axis=0, keepdims=True)
    sums_ref[1:2] = jnp.sum(grad_two * normed, axis=0, keepdims=True)
    sums_ref[2:3] = jnp.sum(grad_two, axis=0, keepdims=True)


def middle_back(
    row_part, bit, part, other, grad, normed, inverse, gain, weight, earlier=(), after=()
):
    count, width = grad.shape
    start = earlier[0].shape[1] if earlier else 0
    half = like((width // 2, start + lanes(count)))
    return local_call(
        lambda *refs: middle_back_kernel(row_part, len(earlier) // 2, *refs),
        (
            like((count, width)),
            half,
            half,
            like((count, weight.shape[0]), jnp.bfloat16),
            like((3, width)),
        ),
        (bit, part, other, grad, normed, inverse, gain, weight, *earlier),
        after,
        scratch=(pltpu.VMEM((width, lanes(count)), jnp.float32),),
        smem=1,
        name="middle_back",
    )


def project_back_kernel(grads_ref, weight_ref, state_ref, part_ref, sums_ref, bias_ref):
    width = weight_ref.shape[2]
    low = lambda j: grads_ref[:, j * width : (j + 1) * width].astype(jnp.bfloat16)
    part = dot(low(0), weight_ref[0], NT)
    for j in (1, 2):
        part = part + dot(low(j), weight_ref[j], NT)
    part_ref[...] = part
    normed = layer_norm(state_ref[...].astype(jnp.float32), 1.0, 0.0)[1]
    sums_ref[0:1] = jnp.sum(part * normed, axis=0, keepdims=True)
    sums_ref[1:2] = jnp.sum(part, axis=0, keepdims=True)
    bias_ref[...] = jnp.sum(grads_ref[...], axis=0, keepdims=True)


def project_back(grads, weight, states, after=()):
    rows, width = states.shape
    return local_call(
        project_back_kernel,
        (like((rows, width)), like((2, width)), like((1, grads.shape[1]))),
        (grads, weight, states),
        after,
        name="project_back",
    )


def last_kernel(count, part_ref, other_ref, state_ref, gain_ref, *refs):
    mids, results, (grad_ref, out_ref) = refs[:count], refs[count : 2 * count], refs[2 * count :]
    start = 0
    for mid, result in zip(mids, results):
        rows = slice(start, start + mid.shape[0])
        _, normed, inverse = layer_norm(state_ref[rows].astype(jnp.float32), 1.0, 0.0)
        grad_one = part_ref[rows] + other_ref[rows]
        grad_ref[rows] = (
            mid[...] + norm_back(grad_one, normed, inverse, gain_ref[...])
        ).astype(jnp.bfloat16)
        out_ref[rows] = result[...]
        start = rows.stop


def last_step(mids, part, other, states, gain, results, after=()):
    return local_call(
        lambda *refs: last_kernel(len(mids), *refs),
        (like(states.shape, jnp.bfloat16),) * 2,
        (part, other, states, gain, *mids, *results),
        after,
        name="input_grad",
    )


def outer_kernel(high, low, plans, bit_ref, *refs):
    count = sum(len(lefts) + rights for _, lefts, rights in plans)
    operands, (give_ref, keep_ref), scratch = refs[:count], refs[count : count + 2], refs[count + 2 :]
    rounded, full = list(scratch[:-1]), scratch[-1]
    operands = list(operands)
    for (first, last), lefts, rights in plans:
        left_refs = [operands.pop(0) for _ in lefts]
        offsets = [start for _, _, start in lefts]
        right_refs = [operands.pop(0) for _ in range(rights)]
        low_refs = [rounded.pop(0) for _ in lefts]

        @pl.when(pl.program_id(0) == first)
        def _():
            for out, left in zip(low_refs, zip(left_refs, offsets)):
                out[...] = left[0][:, left[1] : left[1] + out.shape[1]].astype(jnp.bfloat16)

        @pl.when((pl.program_id(0) >= first) & (pl.program_id(0) < last))
        def _():
            total = None
            for out, (index, rows, _) in zip(low_refs, lefts):
                product = dot(out[...], right_refs[index][rows].astype(jnp.bfloat16))
                total = product if total is None else total + product
            full[...] = total

    part_blocks(full, bit_ref[0], high, low, keep_ref, give_ref)


def outer_sum(bit, high, groups, after=(), tile=512):
    width = groups[0][0][0][0].shape[0]
    low = width // (2 * high)
    operands, specs, scratch, plans = [], [], [], []
    first = 0
    for lefts, rights, start, columns in groups:
        last = first + columns // tile
        places, index, row = [], 0, 0
        for v, offset, rows in lefts:
            operands.append(v)
            specs.append(pl.BlockSpec(v.shape, lambda i: (0, 0)))
            scratch.append(pltpu.VMEM((width, rows), jnp.bfloat16))
            if row == rights[index].shape[0]:
                index, row = index + 1, 0
            places.append((index, slice(row, row + rows), offset))
            row += rows
        for v in rights:
            operands.append(v)
            place = lambda i, s=start // tile, f=first, n=last - first: (
                0,
                s + jnp.clip(i - f, 0, n - 1),
            )
            specs.append(pl.BlockSpec((v.shape[0], tile), place))
        plans.append(((first, last), places, len(rights)))
        first = last

    def body(*refs):
        count = 1 + len(operands)
        outer_kernel(high, low, plans, *refs[:count], *refs[count + len(after) :])

    return pl.pallas_call(
        body,
        out_shape=(like((width // 2, first * tile)),) * 2,
        grid=(first,),
        in_specs=[pl.BlockSpec(memory_space=pltpu.SMEM)]
        + specs
        + [pl.BlockSpec(memory_space=pl.ANY)] * len(after),
        out_specs=(pl.BlockSpec((width // 2, tile), lambda i: (0, i)),) * 2,
        scratch_shapes=scratch + [pltpu.VMEM((width, tile), jnp.float32)],
        compiler_params=pltpu.CompilerParams(vmem_limit_bytes=VMEM_BYTES),
        cost_estimate=BRIEF,
        name="weight_grad",
    )(bit, *operands, *after)


def split_kernel(count, bit_ref, *refs):
    bit = bit_ref[0]
    keeps, cames, (give_out, keep_out) = refs[:count], refs[count : 2 * count], refs[2 * count :]
    start = 0
    for keep_ref, came_ref in zip(keeps, cames):
        columns = slice(start, start + keep_ref.shape[-1])
        keep_out[0, :, columns] = keep_ref[0, bit] + came_ref[0, bit]
        give_out[0, :, columns] = keep_ref[0, 1 - bit] + came_ref[0, 1 - bit]
        start = columns.stop


def add_split(bit, keeps, cames, high):
    rows = keeps[0].shape[0]
    low = rows // (2 * high)
    blocks = [v.reshape(high, 2, low, v.shape[1]) for v in (*keeps, *cames)]
    columns = sum(v.shape[1] for v in keeps)
    give, kept = pl.pallas_call(
        lambda *refs: split_kernel(len(keeps), *refs),
        out_shape=(like((high, low, columns)),) * 2,
        grid=(high,),
        in_specs=[pl.BlockSpec(memory_space=pltpu.SMEM)]
        + [pl.BlockSpec((1, *v.shape[1:]), lambda i: (i, 0, 0, 0)) for v in blocks],
        out_specs=(pl.BlockSpec((1, low, columns), lambda i: (i, 0, 0)),) * 2,
        compiler_params=pltpu.CompilerParams(vmem_limit_bytes=VMEM_BYTES),
        cost_estimate=BRIEF,
        name="add_split",
    )(bit, *blocks)
    return give.reshape(rows // 2, columns), kept.reshape(rows // 2, columns)


def finish_kernel(counts, *refs):
    total = sum(counts)
    pairs, outs = list(zip(refs[:total], refs[total : 2 * total])), refs[2 * total :]
    for count, out in zip(counts, outs):
        start = 0
        for _ in range(count):
            keep_ref, came_ref = pairs.pop(0)
            stop = start + keep_ref.shape[1]
            out[:, start:stop] = keep_ref[...] + came_ref[...]
            start = stop


def finish_all(results, after=()):
    return local_call(
        lambda *refs: finish_kernel([len(keeps) for keeps, _ in results], *refs),
        [like((one[0].shape[0], sum(v.shape[1] for v in one))) for one, _ in results],
        (*(v for one, _ in results for v in one), *(v for _, one in results for v in one)),
        after,
        name="finish",
    )


def finish_pair(first, second):
    width = first.keep[0].shape[1]
    local = width // 2
    rows = first.keep[0].shape[0]

    def kernel(keep_one, came_one, keep_two, came_two, in_ref, out_ref):
        in_ref[:, :width] = keep_one[...] + came_one[...]
        value = keep_two[...] + came_two[...]
        in_ref[:, width:] = value[:, :local]
        out_ref[...] = value[:, local:]

    return local_call(
        kernel,
        (like((rows, width + local)), like((rows, local))),
        (*first.keep, *first.came, *second.keep, *second.came),
        name="finish",
    )


def pack_kernel(counts, valid_ref, *refs):
    ins, out = list(refs[:-1]), refs[-1]
    one, projected = ins[:2]
    rest = ins[2:]
    middles, ups, results = (
        rest[: counts],
        rest[counts : 2 * counts],
        rest[2 * counts :],
    )
    width = out.shape[1]
    total = lambda parts: sum(part[...] for part in parts[1:]) + parts[0][...]
    out[...] = jnp.zeros_like(out)
    out[0:2] = one[...]
    local = projected.shape[1] // 3
    out[2:3, :local] = projected[:, :local]
    out[2:3, local : 2 * local] = projected[:, 2 * local :]
    out[3:6] = total(middles)
    up = total(ups)
    rows = up.shape[1] // width
    for row in range(rows):
        out[6 + row : 7 + row] = up[:, row * width : (row + 1) * width]
    result = total(results)
    out[6 + rows : 7 + rows] = result[0:1]
    out[7 + rows : 8 + rows] = result[1:2] * valid_ref[0]


def pack(valid, one, projected, middles, ups, results):
    width = one.shape[1]
    rows = -(-(8 + ups[0].shape[1] // width) // 8) * 8
    return local_call(
        lambda *refs: pack_kernel(len(middles), *refs),
        (like((rows, width)),),
        (valid, one, projected, *middles, *ups, *results),
        smem=1,
        name="pack",
    )[0]


def tie(value, *others):
    return lax.optimization_barrier((value, *others))[0]


def make_shards(mesh):
    groups = mesh.shape["dp"]
    bits = groups.bit_length() - 1
    assert groups == 1 << bits and mesh.shape["tensor"] == 2

    def swap_tensor(value):
        return lax.ppermute(value, "tensor", [(0, 1), (1, 0)])

    def swap_bit(value, bit):
        return lax.ppermute(value, "dp", [(i, i ^ (1 << bit)) for i in range(groups)])

    def sum_dp(value):
        for bit in range(bits):
            value = value + swap_bit(value, bit)
        return value

    def own_bit(bit):
        return ((lax.axis_index("dp") >> bit) & 1).astype(jnp.int32).reshape(1)

    class Scatter:
        def __init__(self, groups_of, order, after=()):
            self.left = list(range(1, bits))[::-1]
            self.order = list(order)
            bit = self.order[0]
            self.give, self.keep = outer_sum(
                own_bit(bit), 1 << self.left.index(bit), groups_of, after
            )
            self.keep, self.came = [self.keep], None

        def send(self):
            bit = self.order.pop(0)
            self.came = [swap_bit(self.give, bit)]
            self.left.remove(bit)
            self.give = None

        def join(self, other):
            self.keep = self.keep + other.keep
            self.came = self.came + other.came

        def fold(self):
            bit = self.order[0]
            self.give, keep = add_split(
                own_bit(bit), self.keep, self.came, 1 << self.left.index(bit)
            )
            self.keep, self.came = [keep], None

        def move(self):
            self.fold()
            self.send()

        def last(self):
            while self.order:
                self.move()
            return self

    def sync(scatters, *arrays):
        held = [(one.give, one.keep, one.came) for one in scatters]
        held, arrays = lax.optimization_barrier((held, arrays))
        for one, (give, keep, came) in zip(scatters, held):
            one.give, one.keep, one.came = give, keep, came
        return arrays

    def shards(
        images,
        teacher,
        image_mask,
        attn_gain,
        attn_shift,
        in_weight,
        in_bias,
        out_weight,
        out_bias,
        mlp_gain,
        mlp_shift,
        up_weight,
        up_bias,
        down_weight,
        down_bias,
    ):
        image_count, seq_len, width = images.shape
        row_count = image_count * seq_len
        local_width = in_weight.shape[2]
        scales_one = jnp.stack([attn_gain, attn_shift]).astype(jnp.float32)
        gain_one = scales_one[0:1]
        gain_two = mlp_gain.astype(jnp.float32)[None]
        shift_two = mlp_shift.astype(jnp.float32)[None]
        bias_out = out_bias.astype(jnp.float32)[None]
        bias_up = up_bias.astype(jnp.float32)[None]
        bias_down = down_bias.astype(jnp.float32)[None]
        weights_in = jnp.swapaxes(in_weight, 0, 1)
        chunks, start = [], 0
        for stop in (352, row_count):
            chunks.append(slice(start, stop))
            start = stop
        cut = chunks[0].stop
        part = width // groups
        core_bit = own_bit(0)
        low_first = tuple(range(1, bits))
        swap_core = lambda value: swap_bit(value, 0)

        quarter = local_width // 4
        dp_index = lax.axis_index("dp")
        piece = lax.dynamic_slice_in_dim(out_weight, (dp_index & 3) * quarter, quarter, axis=0)
        pieces = [swap_tensor(piece.astype(jnp.float32))]
        places = jnp.stack([(dp_index & 3) ^ way for way in (0, 2, 1, 3)]).astype(jnp.int32)

        states = images.reshape(row_count, width)
        targets = teacher.reshape(row_count, width)
        act_one, projected = enter(states, scales_one, weights_in, in_bias)
        *context, log_total = attend(projected, chunks[0].stop)
        context_other = [swap_tensor(one) for one in context]
        pieces.append(swap_bit(tie(pieces[0], log_total), 1))
        pieces += [swap_core(one) for one in pieces]

        valid = image_mask.astype(jnp.float32)[0]
        count = tie(jnp.full((8, 128), valid * seq_len, jnp.float32), log_total)
        count = count + swap_bit(count, 0)
        turned_one, given_one = turn_step(core_bit, act_one, part, (log_total,))

        middle, normed_two, inverse_two, turned_two, given_two, inner, slope, mlp_part = mlp_out = [
            [] for _ in range(8)
        ]
        count, turned_one, given_one, context, context_other[0], pieces = sync(
            [], count, turned_one, given_one, context, context_other[0], pieces
        )
        more = swap_bit(count, 1)

        def mlp_of(i):
            rows = chunks[i]
            step = mlp_step(
                rows,
                slice(0, rows.stop - rows.start),
                part,
                places,
                core_bit,
                states,
                context[i],
                context_other[i],
                out_weight,
                pieces,
                bias_out,
                gain_two,
                shift_two,
                up_weight,
                bias_up,
                down_weight,
            )
            for kept, one in zip(mlp_out, step):
                kept.append(one)

        mlp_of(0)
        mlp_part[0], given_two[0], inner[0], given_one, context, context_other[1], count, more = sync(
            [], mlp_part[0], given_two[0], inner[0], given_one, context, context_other[1], count, more
        )
        count = count + more
        mlp_other = [swap_tensor(mlp_part[0])]
        came_two, came_inner = [swap_core(given_two[0])], [swap_core(inner[0])]
        came_one = swap_core(given_one)
        more = swap_bit(count, 2)
        mlp_of(1)
        mlp_part[1], given_two[1], inner[1], came_two, came_inner, came_one, count, more = sync(
            [], mlp_part[1], given_two[1], inner[1], came_two, came_inner, came_one, count, more
        )
        count = count + more
        mlp_other.append(swap_tensor(mlp_part[1]))
        for bit in range(3, bits):
            count = count + swap_bit(count, bit)
        mlp_other[0], given_two[1], inner[1], count = sync(
            [], mlp_other[0], given_two[1], inner[1], count
        )
        count_all = count[:1, 0]
        scale = 2.0 * valid / count_all

        result, grad_result, grad_low, turned_low, given_low, result_sums = result_out = [
            [] for _ in range(6)
        ]
        grad_pre, two_part, up_sums = back_out = [[], [], []]
        two_other = []

        def result_of(i, after):
            step = result_step(
                chunks[i],
                part,
                scale,
                core_bit,
                middle[i],
                mlp_part[i],
                mlp_other[i],
                bias_down,
                targets,
                after,
            )
            for kept, one in zip(result_out, step):
                kept.append(one)

        def back_of(i, after):
            step = mlp_back(grad_low[i], slope[i], down_weight, up_weight, after)
            for kept, one in zip(back_out, step):
                kept.append(one)
            two_other.append(swap_tensor(two_part[i]))
            return (two_part[i],)

        grad_middle, turned_attn, given_attn, grad_context, middle_sums = middle_out = [
            [] for _ in range(5)
        ]

        def middle_of(i, earlier, after):
            step = middle_back(
                part,
                core_bit,
                two_part[i],
                two_other[i],
                grad_result[i],
                normed_two[i],
                inverse_two[i],
                gain_two,
                out_weight,
                earlier,
                after,
            )
            for kept, one in zip(middle_out, step):
                kept.append(one)
            return (grad_context[i],)

        def rows_of(values):
            return [(one, 0, rows.stop - rows.start) for one, rows in zip(values, chunks * 2)]

        half = up_weight.shape[1] // 2
        came_two.append(swap_core(given_two[1]))
        came_inner.append(swap_core(inner[1]))
        came_context = [swap_core(one) for one in context]
        result_of(0, ())
        back_of(0, ())
        came_two, came_inner, came_context, grad_pre[0], given_low[0], two_part[0] = sync(
            [], came_two, came_inner, came_context, grad_pre[0], given_low[0], two_part[0]
        )
        two_other = [swap_tensor(two_part[0])]
        came_low = [swap_core(given_low[0])]
        result_of(1, (two_part[0],))
        given_low[1], grad_low[1], slope[1] = sync([], given_low[1], grad_low[1], slope[1])

        came_low.append(swap_core(given_low[1]))
        (came_low,) = sync([], came_low)

        left, right = rows_of(turned_low + came_low), inner + came_inner
        part_units = half // 2
        down_b = Scatter([(left, right, 0, part_units)], low_first)
        grad_low[1], slope[1] = sync([down_b], grad_low[1], slope[1])

        down_b.send()
        back_of(1, ())
        down_c = Scatter([(left, right, part_units, part_units)], low_first, (two_part[1],))
        two_part[1], grad_pre, two_other[0] = sync(
            [down_b, down_c], two_part[1], grad_pre, two_other[0]
        )

        two_other.append(swap_tensor(two_part[1]))
        down_c.send()
        came_pre = [swap_core(one) for one in grad_pre]
        down_d = Scatter([(left, right, half, half)], low_first)
        (came_pre,) = sync([down_b, down_c, down_d], came_pre)

        down_d.send()
        down_b.join(down_c)
        down_b.move()
        left, right = rows_of(turned_two + came_two), grad_pre + came_pre
        up_a = Scatter([(left, right, 0, half)], low_first)
        up_b = Scatter([(left, right, half, half)], low_first, (up_a.give,))
        middle_of(0, (), (up_b.give,))
        two_other[1], turned_attn, given_attn = sync(
            [down_b, down_d, up_a, up_b], two_other[1], turned_attn, given_attn
        )
        middle_out[1], middle_out[2] = turned_attn, given_attn

        up_a.send()
        down_b.move()
        down_d.move()
        middle_of(1, (turned_attn[0], given_attn[0]), ())
        grads = attend_back(projected, log_total, grad_context)
        grads, given = sync([down_b, down_d, up_a, up_b], grads, given_attn[1])

        up_b.send()
        came_grads = swap_core(grads)
        came_attn = swap_core(given)
        up_a.move()
        down_d.move()
        one_part, one_sums, in_sums = project_back(grads, weights_in, states)
        left = [(turned_one, 0, row_count), (came_one, 0, row_count)]
        right = [grads, came_grads]
        in_a = Scatter([(left, right, 0, 2 * local_width)], low_first, (one_part,))
        starts = (0, lanes(chunks[0].stop))
        in_b = Scatter(
            [
                (left, right, 2 * local_width, local_width),
                (
                    [
                        (one, start, rows.stop - rows.start)
                        for one in (turned_attn[1], came_attn)
                        for start, rows in zip(starts, chunks)
                    ],
                    [*context, *came_context],
                    0,
                    local_width,
                ),
            ],
            low_first,
            (in_a.give,),
        )
        small = pack(valid.reshape(1), one_sums, in_sums, middle_sums, up_sums, result_sums)
        one_part, small = sync([down_b, down_d, up_a, up_b, in_a, in_b], one_part, small)

        one_other = swap_tensor(one_part)
        in_a.send()
        up_a.move()
        up_b.move()
        small = small + swap_bit(small, 0)
        more = swap_bit(small, 1)
        small, more = sync([up_a, up_b, in_a, in_b], small, more)

        in_b.send()
        up_b.move()
        in_a.move()
        small = small + more
        more = swap_bit(small, 2)
        small, more = sync([up_a, up_b, in_a, in_b], small, more)

        in_b.move()
        in_a.move()
        small = small + more
        for bit in range(3, bits):
            small = small + swap_bit(small, bit)
        up_a.last(), up_b.last()
        (full_up,) = finish_all([(up_a.keep + up_b.keep, up_a.came + up_b.came)])
        grad_images, block_out = last_step(
            grad_middle, one_part, one_other, states, gain_one, result
        )
        small, full_up, grad_images, block_out = sync(
            [in_a, in_b], small, full_up, grad_images, block_out
        )

        in_b.move()
        one_sums = small[:2] + swap_tensor(small[:2])
        downs = [one.last() for one in (down_b, down_d)]
        (full_down,) = finish_all(
            [([one.keep[0] for one in downs], [one.came[0] for one in downs])]
        )
        full_in, full_out = finish_pair(in_a.last(), in_b.last())
        up_rows = up_bias.shape[0] // width
        small_up = small[6 : 6 + up_rows].reshape(-1)
        shape = (image_count, seq_len, width)
        return (
            block_out.reshape(shape),
            jnp.sum(small[7 + up_rows]) / count_all[0],
            grad_images.reshape(shape),
            one_sums[0],
            one_sums[1],
            full_in.reshape(-1, 3, local_width),
            small[2].reshape(2, local_width),
            full_out.T,
            small[3],
            small[4],
            small[5],
            full_up,
            small_up,
            full_down.T,
            small[6 + up_rows],
        )

    return shards


def solution(mesh):
    placed = (
        P("dp", None, None),
        P("dp", None, None),
        P("dp"),
        P(),
        P(),
        P(None, None, "tensor"),
        P(None, "tensor"),
        P("tensor", None),
        P(),
        P(),
        P(),
        P(None, "tensor"),
        P("tensor"),
        P("tensor", None),
        P(),
    )
    return jax.shard_map(
        make_shards(mesh),
        mesh=mesh,
        in_specs=placed,
        out_specs=(
            P("dp", None, None),
            P(),
            P("dp", None, None),
            P(),
            P(),
            P("dp", None, "tensor"),
            P(None, "tensor"),
            P("tensor", "dp"),
            P(),
            P(),
            P(),
            P("dp", "tensor"),
            P("tensor"),
            P("tensor", "dp"),
            P(),
        ),
        check_vma=False,
    )
```

```python
import jax
import jax.numpy as jnp
from jax import lax
from jax.experimental import pallas as pl
from jax.experimental.pallas import tpu as pltpu
from jax.sharding import PartitionSpec as P

HD = 64

epsilon = 1e-05
score_scale = 0.125
quick_rate = 1.702
log2_e = 1.4426950408889634
score_rate = score_scale * log2_e

NN = (((1,), (0,)), ((), ()))
NT = (((1,), (1,)), ((), ()))
VMEM_BYTES = 48 * 2**20
BRIEF = pl.CostEstimate(flops=1, bytes_accessed=1, transcendentals=0)


def dot(matrix_a, matrix_b, dims=NN):
    return lax.dot_general(matrix_a, matrix_b, dims, preferred_element_type=jnp.float32)


def layer_norm(hidden, scales, offset):
    centred = hidden - jnp.mean(hidden, axis=-1, keepdims=True)
    inverse = lax.rsqrt(jnp.mean(centred * centred, axis=-1, keepdims=True) + epsilon)
    normed = centred * inverse
    return (normed * scales + offset, normed, inverse)


def norm_back(grad_out, normed, inverse, scales):
    scaled = grad_out * scales
    centred = scaled - jnp.mean(scaled, axis=-1, keepdims=True)
    return (centred - normed * jnp.mean(scaled * normed, axis=-1, keepdims=True)) * inverse


def first_head(shape):
    return lax.broadcasted_iota(jnp.int32, shape, len(shape) - 1) < HD


def local_call(
    kernel, outs, ins, after=(), scratch=(), smem=0, name=None
):
    count = len(ins)

    def body(*refs):
        kernel(*refs[:count], *refs[count + len(after) :])

    return pl.pallas_call(
        body,
        out_shape=tuple(outs),
        in_specs=[pl.BlockSpec(memory_space=pltpu.SMEM)] * smem
        + [pl.BlockSpec(memory_space=pltpu.VMEM)] * (count - smem)
        + [pl.BlockSpec(memory_space=pl.ANY)] * len(after),
        out_specs=tuple(pl.BlockSpec(memory_space=pltpu.VMEM) for _ in outs),
        scratch_shapes=list(scratch),
        compiler_params=pltpu.CompilerParams(vmem_limit_bytes=VMEM_BYTES),
        cost_estimate=BRIEF,
        name=name,
    )(*ins, *after)


def part_blocks(source, bit, high, low, keep_ref, give_ref):
    for j in range(high):
        keep_ref[low * j : low * (j + 1)] = source[
            pl.ds(pl.multiple_of((2 * j + bit) * low, 8), low)
        ]
        give_ref[low * j : low * (j + 1)] = source[
            pl.ds(pl.multiple_of((2 * j + 1 - bit) * low, 8), low)
        ]


def lanes(rows):
    return -(-rows // 128) * 128


def turn(value, bit, part, scratch, keep_ref, give_ref):
    rows = value.shape[0]
    scratch[:, :rows] = jnp.transpose(value)
    if scratch.shape[1] > rows:
        scratch[:, rows:] = jnp.zeros((scratch.shape[0], scratch.shape[1] - rows), jnp.float32)
    part_blocks(scratch, bit, value.shape[1] // (2 * part), part, keep_ref, give_ref)


def like(shape, dtype=jnp.float32):
    return jax.ShapeDtypeStruct(shape, dtype)


def enter_kernel(state_ref, scales_ref, weight_ref, bias_ref, act_ref, out_ref):
    which = pl.program_id(0)

    @pl.when(which == 0)
    def _():
        act_ref[...] = layer_norm(
            state_ref[...].astype(jnp.float32), scales_ref[0:1], scales_ref[1:2]
        )[0].astype(jnp.bfloat16)

    biases = bias_ref[...].astype(jnp.float32)
    zero = jnp.zeros_like(biases[0:1])
    bias = jnp.where(which == 0, biases[0:1], jnp.where(which == 2, biases[1:2], zero))
    out_ref[0] = (dot(act_ref[...], weight_ref[0]) + bias).astype(jnp.bfloat16)


def enter(states, scales, weight, bias):
    rows, width = states.shape
    local = weight.shape[2]
    return pl.pallas_call(
        enter_kernel,
        out_shape=(
            like((rows, width), jnp.bfloat16),
            like((3, rows, local), jnp.bfloat16),
        ),
        grid=(3,),
        in_specs=[
            pl.BlockSpec((rows, width), lambda i: (0, 0)),
            pl.BlockSpec((2, width), lambda i: (0, 0)),
            pl.BlockSpec((1, width, local), lambda i: (i, 0, 0)),
            pl.BlockSpec((2, local), lambda i: (0, 0)),
        ],
        out_specs=(
            pl.BlockSpec((rows, width), lambda i: (0, 0)),
            pl.BlockSpec((1, rows, local), lambda i: (i, 0, 0)),
        ),
        compiler_params=pltpu.CompilerParams(vmem_limit_bytes=VMEM_BYTES),
        cost_estimate=BRIEF,
        name="norm_project",
    )(states, scales, weight, bias)


def attend_kernel(projected_ref, first_ref, second_ref, log_ref):
    _, seq_len, width = projected_ref.shape
    cut = first_ref.shape[0]
    low = first_head((seq_len, 2 * HD))
    zero = jnp.zeros((), jnp.bfloat16)
    for pair in range(width // (2 * HD)):
        start, stop = 2 * HD * pair, 2 * HD * (pair + 1)
        cols = slice(start, stop)
        query, key = projected_ref[0, :, cols], projected_ref[1, :, cols]
        value_t = jnp.transpose(projected_ref[2, :, cols])
        parts = []
        for half in range(2):
            one_key = jnp.where(low if half == 0 else ~low, key, zero)
            scores = dot(one_key, query, NT)
            top = jnp.max(scores, axis=0, keepdims=True)
            weights = jnp.exp2((scores - top) * score_rate)
            total = jnp.sum(weights, axis=0, keepdims=True)
            weights_low = (weights * (1.0 / total)).astype(jnp.bfloat16)
            parts.append(dot(value_t[HD * half : HD * (half + 1)], weights_low))
            head = 2 * pair + half
            log_ref[head : head + 1, :] = top * score_rate + jnp.log2(total)
        context = jnp.transpose(jnp.concatenate(parts, axis=0)).astype(jnp.bfloat16)
        context = context.astype(jnp.float32)
        first_ref[:, cols] = context[:cut]
        second_ref[:, cols] = context[cut:]


def attend(projected, cut, after=()):
    _, rows, width = projected.shape
    return local_call(
        attend_kernel,
        (like((cut, width)), like((rows - cut, width)), like((width // HD, rows))),
        (projected,),
        after,
        name="attend",
    )


def turn_step(bit, value, part, after=()):
    rows, width = value.shape
    half = like((width // 2, lanes(rows)))

    def kernel(bit_ref, value_ref, keep_ref, give_ref, scratch):
        turn(value_ref[...].astype(jnp.float32), bit_ref[0], part, scratch, keep_ref, give_ref)

    return local_call(
        kernel,
        (half, half),
        (bit, value),
        after,
        scratch=(pltpu.VMEM((width, lanes(rows)), jnp.float32),),
        smem=1,
        name="turn",
    )


def attend_back_kernel(projected_ref, log_ref, *refs):
    grad_refs, grads_ref = refs[:-1], refs[-1]
    _, seq_len, width = projected_ref.shape
    low = first_head((seq_len, 2 * HD))
    zero = jnp.zeros((), jnp.bfloat16)
    round_low = lambda v: v.astype(jnp.bfloat16).astype(jnp.float32)
    for pair in range(width // (2 * HD)):
        start, stop = 2 * HD * pair, 2 * HD * (pair + 1)
        cols = slice(start, stop)
        query, key, value = (projected_ref[j, :, cols] for j in range(3))
        grad = jnp.concatenate([one[:, cols] for one in grad_refs], axis=0)
        key_t = jnp.transpose(key)
        grad_query, grad_key, grad_value = [], [], []
        for half in range(2):
            kept = low if half == 0 else ~low
            head = 2 * pair + half
            scores = dot(jnp.where(kept, key, zero), query, NT)
            weights = jnp.exp2(scores * score_rate - log_ref[head : head + 1, :])
            grad_weights = dot(jnp.where(kept, value, zero), grad, NT)
            grad_value.append(dot(weights.astype(jnp.bfloat16), grad))
            row_sum = jnp.sum(grad_weights * weights, axis=0, keepdims=True)
            grad_scores = (weights * (grad_weights - row_sum)).astype(jnp.bfloat16)
            grad_key.append(dot(grad_scores, query))
            grad_query.append(dot(key_t[HD * half : HD * (half + 1)], grad_scores))
        grads_ref[:, start:stop] = round_low(
            jnp.transpose(jnp.concatenate(grad_query, axis=0)) * score_scale
        )
        grads_ref[:, width + start : width + stop] = round_low(
            jnp.where(low, grad_key[0], grad_key[1]) * score_scale
        )
        grads_ref[:, 2 * width + start : 2 * width + stop] = round_low(
            jnp.where(low, grad_value[0], grad_value[1])
        )


def attend_back(projected, log_total, grad_context, after=()):
    _, seq_len, width = projected.shape
    return local_call(
        attend_back_kernel,
        (like((seq_len, 3 * width)),),
        (projected, log_total, *grad_context),
        after,
        name="attend_back",
    )[0]


def mlp_kernel(
    rows, inside, part, places_ref, bit_ref, hidden_ref, context_ref, other_ref, weight_ref, *refs
):
    pieces, (bias_ref, gain_ref, shift_ref, up_ref, up_bias_ref, down_ref) = refs[:4], refs[4:10]
    middle_ref, normed_ref, inverse_ref, turned_ref, given_ref, inner_ref, slope_ref, part_ref = (
        refs[10:18]
    )
    weight_other, act_ref, scratch = refs[18:]

    @pl.when(pl.program_id(0) == 0)
    def _():
        block = pieces[0].shape[0]
        for i, piece in enumerate(pieces):
            start = pl.multiple_of(places_ref[i] * block, block)
            weight_other[pl.ds(start, block)] = piece[...].astype(jnp.bfloat16)
        branch = dot(context_ref[inside].astype(jnp.bfloat16), weight_ref[...]) + dot(
            other_ref[inside].astype(jnp.bfloat16), weight_other[...]
        )
        middle = hidden_ref[rows].astype(jnp.float32) + branch + bias_ref[...]
        normed_out, normed, inverse = layer_norm(middle, gain_ref[...], shift_ref[...])
        middle_ref[...] = middle
        normed_ref[...] = normed
        inverse_ref[...] = inverse
        act = normed_out.astype(jnp.bfloat16)
        act_ref[...] = act
        turn(act.astype(jnp.float32), bit_ref[0], part, scratch, turned_ref, given_ref)

    pre_act = dot(act_ref[...], up_ref[...]) + up_bias_ref[...]
    sigma = 0.5 + 0.5 * jnp.tanh((0.5 * quick_rate) * pre_act)
    inner = (pre_act * sigma).astype(jnp.bfloat16)
    inner_ref[...] = inner.astype(jnp.float32)
    slope_ref[...] = sigma + pre_act * quick_rate * sigma * (1.0 - sigma)
    product = dot(inner, down_ref[...])

    @pl.when(pl.program_id(0) == 0)
    def _():
        part_ref[...] = product

    @pl.when(pl.program_id(0) > 0)
    def _():
        part_ref[...] += product


def mlp_step(
    rows, inside, part, places, bit, hidden, context, other, weight, pieces, bias, gain, shift,
    up, up_bias, down, after=(), tile=512,
):
    width = hidden.shape[1]
    count = rows.stop - rows.start
    units = up.shape[1]
    ins = (places, bit, hidden, context, other, weight, *pieces, bias, gain, shift)

    def body(*refs):
        mlp_kernel(rows, inside, part, *refs[: len(ins) + 3], *refs[len(ins) + 3 + len(after) :])

    whole = lambda shape: pl.BlockSpec(shape, lambda i: (0,) * len(shape))
    half = (width // 2, lanes(count))
    return pl.pallas_call(
        body,
        out_shape=(
            like((count, width)),
            like((count, width)),
            like((count, 1)),
            like(half),
            like(half),
            like((count, units)),
            like((count, units)),
            like((count, width)),
        ),
        grid=(units // tile,),
        in_specs=[pl.BlockSpec(memory_space=pltpu.SMEM)] * 2
        + [whole(v.shape) for v in ins[2:]]
        + [
            pl.BlockSpec((width, tile), lambda i: (0, i)),
            pl.BlockSpec((1, tile), lambda i: (0, i)),
            pl.BlockSpec((tile, width), lambda i: (i, 0)),
        ]
        + [pl.BlockSpec(memory_space=pl.ANY)] * len(after),
        out_specs=(
            whole((count, width)),
            whole((count, width)),
            whole((count, 1)),
            whole(half),
            whole(half),
            pl.BlockSpec((count, tile), lambda i: (0, i)),
            pl.BlockSpec((count, tile), lambda i: (0, i)),
            whole((count, width)),
        ),
        scratch_shapes=[
            pltpu.VMEM(weight.shape, jnp.bfloat16),
            pltpu.VMEM((count, width), jnp.bfloat16),
            pltpu.VMEM((width, lanes(count)), jnp.float32),
        ],
        compiler_params=pltpu.CompilerParams(vmem_limit_bytes=VMEM_BYTES),
        cost_estimate=BRIEF,
        name="mlp",
    )(*ins, up, up_bias, down, *after)


def result_kernel(
    rows, part, scale_ref, bit_ref, middle_ref, part_ref, other_ref, bias_ref, target_ref, *outs
):
    out_ref, grad_ref, low_ref, turned_ref, given_ref, sums_ref, scratch = outs
    result = middle_ref[...] + (part_ref[...] + other_ref[...]) + bias_ref[...]
    error = result - target_ref[rows].astype(jnp.float32)
    grad = error * scale_ref[0]
    low = grad.astype(jnp.bfloat16)
    out_ref[...] = result.astype(jnp.bfloat16)
    grad_ref[...] = grad
    low_ref[...] = low
    turn(low.astype(jnp.float32), bit_ref[0], part, scratch, turned_ref, given_ref)
    sums_ref[0:1] = jnp.sum(grad, axis=0, keepdims=True)
    sums_ref[1:2] = jnp.sum(error * error, axis=0, keepdims=True)


def result_step(rows, row_part, scale, bit, middle, part, other, bias, target, after=()):
    count, width = middle.shape
    half = like((width // 2, lanes(count)))
    return local_call(
        lambda *refs: result_kernel(rows, row_part, *refs),
        (
            like((count, width), jnp.bfloat16),
            like((count, width)),
            like((count, width), jnp.bfloat16),
            half,
            half,
            like((2, width)),
        ),
        (scale, bit, middle, part, other, bias, target),
        after,
        scratch=(pltpu.VMEM((width, lanes(count)), jnp.float32),),
        smem=2,
        name="result_error",
    )


def mlp_back_kernel(low_ref, slope_ref, down_ref, up_ref, pre_ref, two_ref, sums_ref):
    pre = (dot(low_ref[...], down_ref[...], NT) * slope_ref[...]).astype(jnp.bfloat16)
    pre_ref[...] = pre.astype(jnp.float32)
    sums_ref[...] = jnp.sum(pre.astype(jnp.float32), axis=0, keepdims=True)
    two = dot(pre, up_ref[...], NT)

    @pl.when(pl.program_id(0) == 0)
    def _():
        two_ref[...] = two

    @pl.when(pl.program_id(0) > 0)
    def _():
        two_ref[...] += two


def mlp_back(low, slope, down, up, after=(), tile=512):
    count, width = low.shape
    units = up.shape[1]

    def body(*refs):
        mlp_back_kernel(*refs[:4], *refs[4 + len(after) :])

    return pl.pallas_call(
        body,
        out_shape=(
            like((count, units)),
            like((count, width)),
            like((1, units)),
        ),
        grid=(units // tile,),
        in_specs=[
            pl.BlockSpec((count, width), lambda i: (0, 0)),
            pl.BlockSpec((count, tile), lambda i: (0, i)),
            pl.BlockSpec((tile, width), lambda i: (i, 0)),
            pl.BlockSpec((width, tile), lambda i: (0, i)),
        ]
        + [pl.BlockSpec(memory_space=pl.ANY)] * len(after),
        out_specs=(
            pl.BlockSpec((count, tile), lambda i: (0, i)),
            pl.BlockSpec((count, width), lambda i: (0, 0)),
            pl.BlockSpec((1, tile), lambda i: (0, i)),
        ),
        compiler_params=pltpu.CompilerParams(vmem_limit_bytes=VMEM_BYTES),
        cost_estimate=BRIEF,
        name="mlp_back",
    )(low, slope, down, up, *after)


def middle_back_kernel(
    row_part, before, bit_ref, part_ref, other_ref, grad_ref, normed_ref, inverse_ref, gain_ref,
    weight_ref, *refs
):
    earlier, outs = refs[: 2 * before], refs[2 * before :]
    mid_ref, turned_ref, given_ref, context_ref, sums_ref, scratch = outs
    grad_two = part_ref[...] + other_ref[...]
    normed = normed_ref[...]
    mid = grad_ref[...] + norm_back(grad_two, normed, inverse_ref[...], gain_ref[...])
    low = mid.astype(jnp.bfloat16)
    mid_ref[...] = mid
    context_ref[...] = dot(low, weight_ref[...], NT).astype(jnp.bfloat16)
    rows = low.shape[0]
    start = turned_ref.shape[1] - lanes(rows)
    if before:
        turned_ref[:, :start] = earlier[0][...]
        given_ref[:, :start] = earlier[1][...]
    turn(
        low.astype(jnp.float32),
        bit_ref[0],
        row_part,
        scratch,
        turned_ref.at[:, start:],
        given_ref.at[:, start:],
    )
    sums_ref[0:1] = jnp.sum(mid, axis=0, keepdims=True)
    sums_ref[1:2] = jnp.sum(grad_two * normed, axis=0, keepdims=True)
    sums_ref[2:3] = jnp.sum(grad_two, axis=0, keepdims=True)


def middle_back(
    row_part, bit, part, other, grad, normed, inverse, gain, weight, earlier=(), after=()
):
    count, width = grad.shape
    start = earlier[0].shape[1] if earlier else 0
    half = like((width // 2, start + lanes(count)))
    return local_call(
        lambda *refs: middle_back_kernel(row_part, len(earlier) // 2, *refs),
        (
            like((count, width)),
            half,
            half,
            like((count, weight.shape[0]), jnp.bfloat16),
            like((3, width)),
        ),
        (bit, part, other, grad, normed, inverse, gain, weight, *earlier),
        after,
        scratch=(pltpu.VMEM((width, lanes(count)), jnp.float32),),
        smem=1,
        name="middle_back",
    )


def project_back_kernel(grads_ref, weight_ref, state_ref, part_ref, sums_ref, bias_ref):
    width = weight_ref.shape[2]
    low = lambda j: grads_ref[:, j * width : (j + 1) * width].astype(jnp.bfloat16)
    part = dot(low(0), weight_ref[0], NT)
    for j in (1, 2):
        part = part + dot(low(j), weight_ref[j], NT)
    part_ref[...] = part
    normed = layer_norm(state_ref[...].astype(jnp.float32), 1.0, 0.0)[1]
    sums_ref[0:1] = jnp.sum(part * normed, axis=0, keepdims=True)
    sums_ref[1:2] = jnp.sum(part, axis=0, keepdims=True)
    bias_ref[...] = jnp.sum(grads_ref[...], axis=0, keepdims=True)


def project_back(grads, weight, states, after=()):
    rows, width = states.shape
    return local_call(
        project_back_kernel,
        (like((rows, width)), like((2, width)), like((1, grads.shape[1]))),
        (grads, weight, states),
        after,
        name="project_back",
    )


def last_kernel(count, part_ref, other_ref, state_ref, gain_ref, *refs):
    mids, results, (grad_ref, out_ref) = refs[:count], refs[count : 2 * count], refs[2 * count :]
    start = 0
    for mid, result in zip(mids, results):
        rows = slice(start, start + mid.shape[0])
        _, normed, inverse = layer_norm(state_ref[rows].astype(jnp.float32), 1.0, 0.0)
        grad_one = part_ref[rows] + other_ref[rows]
        grad_ref[rows] = (
            mid[...] + norm_back(grad_one, normed, inverse, gain_ref[...])
        ).astype(jnp.bfloat16)
        out_ref[rows] = result[...]
        start = rows.stop


def last_step(mids, part, other, states, gain, results, after=()):
    return local_call(
        lambda *refs: last_kernel(len(mids), *refs),
        (like(states.shape, jnp.bfloat16),) * 2,
        (part, other, states, gain, *mids, *results),
        after,
        name="input_grad",
    )


def outer_kernel(high, low, plans, bit_ref, *refs):
    count = sum(len(lefts) + rights for _, lefts, rights in plans)
    operands, (give_ref, keep_ref), scratch = refs[:count], refs[count : count + 2], refs[count + 2 :]
    rounded, full = list(scratch[:-1]), scratch[-1]
    operands = list(operands)
    for (first, last), lefts, rights in plans:
        left_refs = [operands.pop(0) for _ in lefts]
        offsets = [start for _, _, start in lefts]
        right_refs = [operands.pop(0) for _ in range(rights)]
        low_refs = [rounded.pop(0) for _ in lefts]

        @pl.when(pl.program_id(0) == first)
        def _():
            for out, left in zip(low_refs, zip(left_refs, offsets)):
                out[...] = left[0][:, left[1] : left[1] + out.shape[1]].astype(jnp.bfloat16)

        @pl.when((pl.program_id(0) >= first) & (pl.program_id(0) < last))
        def _():
            total = None
            for out, (index, rows, _) in zip(low_refs, lefts):
                product = dot(out[...], right_refs[index][rows].astype(jnp.bfloat16))
                total = product if total is None else total + product
            full[...] = total

    part_blocks(full, bit_ref[0], high, low, keep_ref, give_ref)


def outer_sum(bit, high, groups, after=(), tile=512):
    width = groups[0][0][0][0].shape[0]
    low = width // (2 * high)
    operands, specs, scratch, plans = [], [], [], []
    first = 0
    for lefts, rights, start, columns in groups:
        last = first + columns // tile
        places, index, row = [], 0, 0
        for v, offset, rows in lefts:
            operands.append(v)
            specs.append(pl.BlockSpec(v.shape, lambda i: (0, 0)))
            scratch.append(pltpu.VMEM((width, rows), jnp.bfloat16))
            if row == rights[index].shape[0]:
                index, row = index + 1, 0
            places.append((index, slice(row, row + rows), offset))
            row += rows
        for v in rights:
            operands.append(v)
            place = lambda i, s=start // tile, f=first, n=last - first: (
                0,
                s + jnp.clip(i - f, 0, n - 1),
            )
            specs.append(pl.BlockSpec((v.shape[0], tile), place))
        plans.append(((first, last), places, len(rights)))
        first = last

    def body(*refs):
        count = 1 + len(operands)
        outer_kernel(high, low, plans, *refs[:count], *refs[count + len(after) :])

    return pl.pallas_call(
        body,
        out_shape=(like((width // 2, first * tile)),) * 2,
        grid=(first,),
        in_specs=[pl.BlockSpec(memory_space=pltpu.SMEM)]
        + specs
        + [pl.BlockSpec(memory_space=pl.ANY)] * len(after),
        out_specs=(pl.BlockSpec((width // 2, tile), lambda i: (0, i)),) * 2,
        scratch_shapes=scratch + [pltpu.VMEM((width, tile), jnp.float32)],
        compiler_params=pltpu.CompilerParams(vmem_limit_bytes=VMEM_BYTES),
        cost_estimate=BRIEF,
        name="weight_grad",
    )(bit, *operands, *after)


def split_kernel(count, bit_ref, *refs):
    bit = bit_ref[0]
    keeps, cames, (give_out, keep_out) = refs[:count], refs[count : 2 * count], refs[2 * count :]
    start = 0
    for keep_ref, came_ref in zip(keeps, cames):
        columns = slice(start, start + keep_ref.shape[-1])
        keep_out[0, :, columns] = keep_ref[0, bit] + came_ref[0, bit]
        give_out[0, :, columns] = keep_ref[0, 1 - bit] + came_ref[0, 1 - bit]
        start = columns.stop


def add_split(bit, keeps, cames, high):
    rows = keeps[0].shape[0]
    low = rows // (2 * high)
    blocks = [v.reshape(high, 2, low, v.shape[1]) for v in (*keeps, *cames)]
    columns = sum(v.shape[1] for v in keeps)
    give, kept = pl.pallas_call(
        lambda *refs: split_kernel(len(keeps), *refs),
        out_shape=(like((high, low, columns)),) * 2,
        grid=(high,),
        in_specs=[pl.BlockSpec(memory_space=pltpu.SMEM)]
        + [pl.BlockSpec((1, *v.shape[1:]), lambda i: (i, 0, 0, 0)) for v in blocks],
        out_specs=(pl.BlockSpec((1, low, columns), lambda i: (i, 0, 0)),) * 2,
        compiler_params=pltpu.CompilerParams(vmem_limit_bytes=VMEM_BYTES),
        cost_estimate=BRIEF,
        name="add_split",
    )(bit, *blocks)
    return give.reshape(rows // 2, columns), kept.reshape(rows // 2, columns)


def finish_kernel(counts, *refs):
    total = sum(counts)
    pairs, outs = list(zip(refs[:total], refs[total : 2 * total])), refs[2 * total :]
    for count, out in zip(counts, outs):
        start = 0
        for _ in range(count):
            keep_ref, came_ref = pairs.pop(0)
            stop = start + keep_ref.shape[1]
            out[:, start:stop] = keep_ref[...] + came_ref[...]
            start = stop


def finish_all(results, after=()):
    return local_call(
        lambda *refs: finish_kernel([len(keeps) for keeps, _ in results], *refs),
        [like((one[0].shape[0], sum(v.shape[1] for v in one))) for one, _ in results],
        (*(v for one, _ in results for v in one), *(v for _, one in results for v in one)),
        after,
        name="finish",
    )


def finish_pair(first, second):
    width = first.keep[0].shape[1]
    local = width // 2
    rows = first.keep[0].shape[0]

    def kernel(keep_one, came_one, keep_two, came_two, in_ref, out_ref):
        in_ref[:, :width] = keep_one[...] + came_one[...]
        value = keep_two[...] + came_two[...]
        in_ref[:, width:] = value[:, :local]
        out_ref[...] = value[:, local:]

    return local_call(
        kernel,
        (like((rows, width + local)), like((rows, local))),
        (*first.keep, *first.came, *second.keep, *second.came),
        name="finish",
    )


def pack_kernel(counts, valid_ref, *refs):
    ins, out = list(refs[:-1]), refs[-1]
    one, other, projected = ins[:3]
    rest = ins[3:]
    middles, ups, results = (
        rest[: counts],
        rest[counts : 2 * counts],
        rest[2 * counts :],
    )
    width = out.shape[1]
    total = lambda parts: sum(part[...] for part in parts[1:]) + parts[0][...]
    out[...] = jnp.zeros_like(out)
    out[0:2] = one[...] + other[...]
    local = projected.shape[1] // 3
    out[2:3, :local] = projected[:, :local]
    out[2:3, local : 2 * local] = projected[:, 2 * local :]
    out[3:6] = total(middles)
    up = total(ups)
    rows = up.shape[1] // width
    for row in range(rows):
        out[6 + row : 7 + row] = up[:, row * width : (row + 1) * width]
    result = total(results)
    out[6 + rows : 7 + rows] = result[0:1]
    out[7 + rows : 8 + rows] = result[1:2] * valid_ref[0]


def pack(valid, one, other, projected, middles, ups, results):
    width = one.shape[1]
    rows = -(-(8 + ups[0].shape[1] // width) // 8) * 8
    return local_call(
        lambda *refs: pack_kernel(len(middles), *refs),
        (like((rows, width)),),
        (valid, one, other, projected, *middles, *ups, *results),
        smem=1,
        name="pack",
    )[0]


def tie(value, *others):
    return lax.optimization_barrier((value, *others))[0]


def make_shards(mesh):
    groups = mesh.shape["dp"]
    bits = groups.bit_length() - 1
    assert groups == 1 << bits and mesh.shape["tensor"] == 2

    def swap_tensor(value):
        return lax.ppermute(value, "tensor", [(0, 1), (1, 0)])

    def swap_bit(value, bit):
        return lax.ppermute(value, "dp", [(i, i ^ (1 << bit)) for i in range(groups)])

    def sum_dp(value):
        for bit in range(bits):
            value = value + swap_bit(value, bit)
        return value

    def own_bit(bit):
        return ((lax.axis_index("dp") >> bit) & 1).astype(jnp.int32).reshape(1)

    class Scatter:
        def __init__(self, groups_of, order, after=()):
            self.left = list(range(1, bits))[::-1]
            self.order = list(order)
            bit = self.order[0]
            self.give, self.keep = outer_sum(
                own_bit(bit), 1 << self.left.index(bit), groups_of, after
            )
            self.keep, self.came = [self.keep], None

        def send(self):
            bit = self.order.pop(0)
            self.came = [swap_bit(self.give, bit)]
            self.left.remove(bit)
            self.give = None

        def join(self, other):
            self.keep = self.keep + other.keep
            self.came = self.came + other.came

        def fold(self):
            bit = self.order[0]
            self.give, keep = add_split(
                own_bit(bit), self.keep, self.came, 1 << self.left.index(bit)
            )
            self.keep, self.came = [keep], None

        def move(self):
            self.fold()
            self.send()

        def last(self):
            while self.order:
                self.move()
            return self

    def sync(scatters, *arrays):
        held = [(one.give, one.keep, one.came) for one in scatters]
        held, arrays = lax.optimization_barrier((held, arrays))
        for one, (give, keep, came) in zip(scatters, held):
            one.give, one.keep, one.came = give, keep, came
        return arrays

    def shards(
        images,
        teacher,
        image_mask,
        attn_gain,
        attn_shift,
        in_weight,
        in_bias,
        out_weight,
        out_bias,
        mlp_gain,
        mlp_shift,
        up_weight,
        up_bias,
        down_weight,
        down_bias,
    ):
        image_count, seq_len, width = images.shape
        row_count = image_count * seq_len
        local_width = in_weight.shape[2]
        scales_one = jnp.stack([attn_gain, attn_shift]).astype(jnp.float32)
        gain_one = scales_one[0:1]
        gain_two = mlp_gain.astype(jnp.float32)[None]
        shift_two = mlp_shift.astype(jnp.float32)[None]
        bias_out = out_bias.astype(jnp.float32)[None]
        bias_up = up_bias.astype(jnp.float32)[None]
        bias_down = down_bias.astype(jnp.float32)[None]
        weights_in = jnp.swapaxes(in_weight, 0, 1)
        chunks, start = [], 0
        for stop in (352, row_count):
            chunks.append(slice(start, stop))
            start = stop
        cut = chunks[0].stop
        part = width // groups
        core_bit = own_bit(0)
        low_first = tuple(range(1, bits))
        swap_core = lambda value: swap_bit(value, 0)

        quarter = local_width // 4
        dp_index = lax.axis_index("dp")
        piece = lax.dynamic_slice_in_dim(out_weight, (dp_index & 3) * quarter, quarter, axis=0)
        pieces = [swap_tensor(piece.astype(jnp.float32))]
        places = jnp.stack([(dp_index & 3) ^ way for way in (0, 2, 1, 3)]).astype(jnp.int32)

        states = images.reshape(row_count, width)
        targets = teacher.reshape(row_count, width)
        act_one, projected = enter(states, scales_one, weights_in, in_bias)
        *context, log_total = attend(projected, chunks[0].stop)
        context_other = [swap_tensor(one) for one in context]
        pieces.append(swap_bit(tie(pieces[0], log_total), 1))
        pieces += [swap_core(one) for one in pieces]

        valid = image_mask.astype(jnp.float32)[0]
        count = tie(jnp.full((8, 128), valid * seq_len, jnp.float32), log_total)
        count = count + swap_bit(count, 0)
        turned_one, given_one = turn_step(core_bit, act_one, part, (log_total,))

        middle, normed_two, inverse_two, turned_two, given_two, inner, slope, mlp_part = mlp_out = [
            [] for _ in range(8)
        ]
        count, turned_one, given_one, context, context_other[0], pieces = sync(
            [], count, turned_one, given_one, context, context_other[0], pieces
        )
        more = swap_bit(count, 1)

        def mlp_of(i):
            rows = chunks[i]
            step = mlp_step(
                rows,
                slice(0, rows.stop - rows.start),
                part,
                places,
                core_bit,
                states,
                context[i],
                context_other[i],
                out_weight,
                pieces,
                bias_out,
                gain_two,
                shift_two,
                up_weight,
                bias_up,
                down_weight,
            )
            for kept, one in zip(mlp_out, step):
                kept.append(one)

        mlp_of(0)
        mlp_part[0], given_two[0], inner[0], given_one, context, context_other[1], count, more = sync(
            [], mlp_part[0], given_two[0], inner[0], given_one, context, context_other[1], count, more
        )
        count = count + more
        mlp_other = [swap_tensor(mlp_part[0])]
        came_two, came_inner = [swap_core(given_two[0])], [swap_core(inner[0])]
        came_one = swap_core(given_one)
        more = swap_bit(count, 2)
        mlp_of(1)
        mlp_part[1], given_two[1], inner[1], came_two, came_inner, came_one, count, more = sync(
            [], mlp_part[1], given_two[1], inner[1], came_two, came_inner, came_one, count, more
        )
        count = count + more
        mlp_other.append(swap_tensor(mlp_part[1]))
        for bit in range(3, bits):
            count = count + swap_bit(count, bit)
        mlp_other[0], given_two[1], inner[1], count = sync(
            [], mlp_other[0], given_two[1], inner[1], count
        )
        count_all = count[:1, 0]
        scale = 2.0 * valid / count_all

        result, grad_result, grad_low, turned_low, given_low, result_sums = result_out = [
            [] for _ in range(6)
        ]
        grad_pre, two_part, up_sums = back_out = [[], [], []]
        two_other = []

        def result_of(i, after):
            step = result_step(
                chunks[i],
                part,
                scale,
                core_bit,
                middle[i],
                mlp_part[i],
                mlp_other[i],
                bias_down,
                targets,
                after,
            )
            for kept, one in zip(result_out, step):
                kept.append(one)

        def back_of(i, after):
            step = mlp_back(grad_low[i], slope[i], down_weight, up_weight, after)
            for kept, one in zip(back_out, step):
                kept.append(one)
            two_other.append(swap_tensor(two_part[i]))
            return (two_part[i],)

        grad_middle, turned_attn, given_attn, grad_context, middle_sums = middle_out = [
            [] for _ in range(5)
        ]

        def middle_of(i, earlier, after):
            step = middle_back(
                part,
                core_bit,
                two_part[i],
                two_other[i],
                grad_result[i],
                normed_two[i],
                inverse_two[i],
                gain_two,
                out_weight,
                earlier,
                after,
            )
            for kept, one in zip(middle_out, step):
                kept.append(one)
            return (grad_context[i],)

        def rows_of(values):
            return [(one, 0, rows.stop - rows.start) for one, rows in zip(values, chunks * 2)]

        half = up_weight.shape[1] // 2
        came_two.append(swap_core(given_two[1]))
        came_inner.append(swap_core(inner[1]))
        came_context = [swap_core(one) for one in context]
        result_of(0, ())
        back_of(0, ())
        came_two, came_inner, came_context, grad_pre[0], given_low[0], two_part[0] = sync(
            [], came_two, came_inner, came_context, grad_pre[0], given_low[0], two_part[0]
        )
        two_other = [swap_tensor(two_part[0])]
        came_low = [swap_core(given_low[0])]
        result_of(1, (two_part[0],))
        given_low[1], grad_low[1], slope[1] = sync([], given_low[1], grad_low[1], slope[1])

        came_low.append(swap_core(given_low[1]))
        (came_low,) = sync([], came_low)

        left, right = rows_of(turned_low + came_low), inner + came_inner
        down_b = Scatter([(left, right, 0, half)], low_first)
        grad_low[1], slope[1] = sync([down_b], grad_low[1], slope[1])

        down_b.send()
        back_of(1, ())
        down_d = Scatter([(left, right, half, half)], low_first, (two_part[1],))
        two_part[1], grad_pre, two_other[0] = sync(
            [down_b, down_d], two_part[1], grad_pre, two_other[0]
        )

        two_other.append(swap_tensor(two_part[1]))
        down_d.send()
        came_pre = [swap_core(one) for one in grad_pre]
        down_b.move()
        middle_of(0, (), ())
        left, right = rows_of(turned_two + came_two), grad_pre + came_pre
        up_a = Scatter([(left, right, 0, half)], low_first, (grad_context[0],))
        up_b = Scatter([(left, right, half, half)], low_first, (up_a.give,))
        two_other[1], turned_attn, given_attn = sync(
            [down_b, down_d, up_a, up_b], two_other[1], turned_attn, given_attn
        )
        middle_out[1], middle_out[2] = turned_attn, given_attn

        up_a.send()
        down_b.move()
        down_d.move()
        middle_of(1, (turned_attn[0], given_attn[0]), ())
        grads = attend_back(projected, log_total, grad_context)
        grads, given = sync([down_b, down_d, up_a, up_b], grads, given_attn[1])

        up_b.send()
        came_grads = swap_core(grads)
        came_attn = swap_core(given)
        up_a.move()
        down_d.move()
        one_part, one_sums, in_sums = project_back(grads, weights_in, states)
        left = [(turned_one, 0, row_count), (came_one, 0, row_count)]
        right = [grads, came_grads]
        in_a = Scatter([(left, right, 0, 2 * local_width)], low_first, (one_part,))
        starts = (0, lanes(chunks[0].stop))
        in_b = Scatter(
            [
                (left, right, 2 * local_width, local_width),
                (
                    [
                        (one, start, rows.stop - rows.start)
                        for one in (turned_attn[1], came_attn)
                        for start, rows in zip(starts, chunks)
                    ],
                    [*context, *came_context],
                    0,
                    local_width,
                ),
            ],
            low_first,
            (in_a.give,),
        )
        first = swap_tensor(one_sums)
        one_part, one_sums, first = sync(
            [down_b, down_d, up_a, up_b, in_a, in_b], one_part, one_sums, first
        )

        one_other = swap_tensor(one_part)
        in_a.send()
        up_a.move()
        up_b.move()
        small = pack(valid.reshape(1), one_sums, first, in_sums, middle_sums, up_sums, result_sums)
        small = small + swap_bit(small, 0)
        more = swap_bit(small, 1)
        small, more = sync([up_a, up_b, in_a, in_b], small, more)

        in_b.send()
        up_b.move()
        in_a.move()
        small = small + more
        more = swap_bit(small, 2)
        small, more = sync([up_a, up_b, in_a, in_b], small, more)

        in_b.move()
        in_a.move()
        small = small + more
        more = swap_bit(small, 3)
        up_a.last(), up_b.last()
        (full_up,) = finish_all([(up_a.keep + up_b.keep, up_a.came + up_b.came)])
        small, more, full_up, one_other = sync([in_a, in_b], small, more, full_up, one_other)

        in_b.move()
        small = small + more
        for bit in range(4, bits):
            small = small + swap_bit(small, bit)
        grad_images, block_out = last_step(
            grad_middle, one_part, one_other, states, gain_one, result
        )
        downs = [one.last() for one in (down_b, down_d)]
        (full_down,) = finish_all(
            [([one.keep[0] for one in downs], [one.came[0] for one in downs])]
        )
        full_in, full_out = finish_pair(in_a.last(), in_b.last())
        up_rows = up_bias.shape[0] // width
        small_up = small[6 : 6 + up_rows].reshape(-1)
        shape = (image_count, seq_len, width)
        return (
            block_out.reshape(shape),
            jnp.sum(small[7 + up_rows]) / count_all[0],
            grad_images.reshape(shape),
            small[0],
            small[1],
            full_in.reshape(-1, 3, local_width),
            small[2].reshape(2, local_width),
            full_out.T,
            small[3],
            small[4],
            small[5],
            full_up,
            small_up,
            full_down.T,
            small[6 + up_rows],
        )

    return shards


def solution(mesh):
    placed = (
        P("dp", None, None),
        P("dp", None, None),
        P("dp"),
        P(),
        P(),
        P(None, None, "tensor"),
        P(None, "tensor"),
        P("tensor", None),
        P(),
        P(),
        P(),
        P(None, "tensor"),
        P("tensor"),
        P("tensor", None),
        P(),
    )
    return jax.shard_map(
        make_shards(mesh),
        mesh=mesh,
        in_specs=placed,
        out_specs=(
            P("dp", None, None),
            P(),
            P("dp", None, None),
            P(),
            P(),
            P("dp", None, "tensor"),
            P(None, "tensor"),
            P("tensor", "dp"),
            P(),
            P(),
            P(),
            P("dp", "tensor"),
            P("tensor"),
            P("tensor", "dp"),
            P(),
        ),
        check_vma=False,
    )
```

```python
import jax
import jax.numpy as jnp
from jax import lax
from jax.experimental import pallas as pl
from jax.experimental.pallas import tpu as pltpu
from jax.sharding import PartitionSpec as P

HD = 64

epsilon = 1e-05
score_scale = 0.125
quick_rate = 1.702
log2_e = 1.4426950408889634
score_rate = score_scale * log2_e

NN = (((1,), (0,)), ((), ()))
NT = (((1,), (1,)), ((), ()))
VMEM_BYTES = 48 * 2**20
BRIEF = pl.CostEstimate(flops=1, bytes_accessed=1, transcendentals=0)


def dot(matrix_a, matrix_b, dims=NN):
    return lax.dot_general(matrix_a, matrix_b, dims, preferred_element_type=jnp.float32)


def layer_norm(hidden, scales, offset):
    centred = hidden - jnp.mean(hidden, axis=-1, keepdims=True)
    inverse = lax.rsqrt(jnp.mean(centred * centred, axis=-1, keepdims=True) + epsilon)
    normed = centred * inverse
    return (normed * scales + offset, normed, inverse)


def norm_back(grad_out, normed, inverse, scales):
    scaled = grad_out * scales
    centred = scaled - jnp.mean(scaled, axis=-1, keepdims=True)
    return (centred - normed * jnp.mean(scaled * normed, axis=-1, keepdims=True)) * inverse


def first_head(shape):
    return lax.broadcasted_iota(jnp.int32, shape, len(shape) - 1) < HD


def local_call(
    kernel, outs, ins, after=(), scratch=(), smem=0, name=None
):
    count = len(ins)

    def body(*refs):
        kernel(*refs[:count], *refs[count + len(after) :])

    return pl.pallas_call(
        body,
        out_shape=tuple(outs),
        in_specs=[pl.BlockSpec(memory_space=pltpu.SMEM)] * smem
        + [pl.BlockSpec(memory_space=pltpu.VMEM)] * (count - smem)
        + [pl.BlockSpec(memory_space=pl.ANY)] * len(after),
        out_specs=tuple(pl.BlockSpec(memory_space=pltpu.VMEM) for _ in outs),
        scratch_shapes=list(scratch),
        compiler_params=pltpu.CompilerParams(vmem_limit_bytes=VMEM_BYTES),
        cost_estimate=BRIEF,
        name=name,
    )(*ins, *after)


def part_blocks(source, bit, high, low, keep_ref, give_ref):
    for j in range(high):
        keep_ref[low * j : low * (j + 1)] = source[
            pl.ds(pl.multiple_of((2 * j + bit) * low, 8), low)
        ]
        give_ref[low * j : low * (j + 1)] = source[
            pl.ds(pl.multiple_of((2 * j + 1 - bit) * low, 8), low)
        ]


def lanes(rows):
    return -(-rows // 128) * 128


def turn(value, bit, part, scratch, keep_ref, give_ref):
    rows = value.shape[0]
    scratch[:, :rows] = jnp.transpose(value)
    if scratch.shape[1] > rows:
        scratch[:, rows:] = jnp.zeros((scratch.shape[0], scratch.shape[1] - rows), jnp.float32)
    part_blocks(scratch, bit, value.shape[1] // (2 * part), part, keep_ref, give_ref)


def like(shape, dtype=jnp.float32):
    return jax.ShapeDtypeStruct(shape, dtype)


def enter_kernel(state_ref, scales_ref, weight_ref, bias_ref, act_ref, out_ref):
    which = pl.program_id(0)

    @pl.when(which == 0)
    def _():
        act_ref[...] = layer_norm(
            state_ref[...].astype(jnp.float32), scales_ref[0:1], scales_ref[1:2]
        )[0].astype(jnp.bfloat16)

    biases = bias_ref[...].astype(jnp.float32)
    zero = jnp.zeros_like(biases[0:1])
    bias = jnp.where(which == 0, biases[0:1], jnp.where(which == 2, biases[1:2], zero))
    out_ref[0] = (dot(act_ref[...], weight_ref[0]) + bias).astype(jnp.bfloat16)


def enter(states, scales, weight, bias):
    rows, width = states.shape
    local = weight.shape[2]
    return pl.pallas_call(
        enter_kernel,
        out_shape=(
            like((rows, width), jnp.bfloat16),
            like((3, rows, local), jnp.bfloat16),
        ),
        grid=(3,),
        in_specs=[
            pl.BlockSpec((rows, width), lambda i: (0, 0)),
            pl.BlockSpec((2, width), lambda i: (0, 0)),
            pl.BlockSpec((1, width, local), lambda i: (i, 0, 0)),
            pl.BlockSpec((2, local), lambda i: (0, 0)),
        ],
        out_specs=(
            pl.BlockSpec((rows, width), lambda i: (0, 0)),
            pl.BlockSpec((1, rows, local), lambda i: (i, 0, 0)),
        ),
        compiler_params=pltpu.CompilerParams(vmem_limit_bytes=VMEM_BYTES),
        cost_estimate=BRIEF,
        name="norm_project",
    )(states, scales, weight, bias)


def attend_kernel(projected_ref, first_ref, second_ref, log_ref):
    _, seq_len, width = projected_ref.shape
    cut = first_ref.shape[0]
    low = first_head((seq_len, 2 * HD))
    zero = jnp.zeros((), jnp.bfloat16)
    for pair in range(width // (2 * HD)):
        start, stop = 2 * HD * pair, 2 * HD * (pair + 1)
        cols = slice(start, stop)
        query, key = projected_ref[0, :, cols], projected_ref[1, :, cols]
        value_t = jnp.transpose(projected_ref[2, :, cols])
        parts = []
        for half in range(2):
            one_key = jnp.where(low if half == 0 else ~low, key, zero)
            scores = dot(one_key, query, NT)
            top = jnp.max(scores, axis=0, keepdims=True)
            weights = jnp.exp2((scores - top) * score_rate)
            total = jnp.sum(weights, axis=0, keepdims=True)
            weights_low = (weights * (1.0 / total)).astype(jnp.bfloat16)
            parts.append(dot(value_t[HD * half : HD * (half + 1)], weights_low))
            head = 2 * pair + half
            log_ref[head : head + 1, :] = top * score_rate + jnp.log2(total)
        context = jnp.transpose(jnp.concatenate(parts, axis=0)).astype(jnp.bfloat16)
        context = context.astype(jnp.float32)
        first_ref[:, cols] = context[:cut]
        second_ref[:, cols] = context[cut:]


def attend(projected, cut, after=()):
    _, rows, width = projected.shape
    return local_call(
        attend_kernel,
        (like((cut, width)), like((rows - cut, width)), like((width // HD, rows))),
        (projected,),
        after,
        name="attend",
    )


def turn_step(bit, value, part, after=()):
    rows, width = value.shape
    half = like((width // 2, lanes(rows)))

    def kernel(bit_ref, value_ref, keep_ref, give_ref, scratch):
        turn(value_ref[...].astype(jnp.float32), bit_ref[0], part, scratch, keep_ref, give_ref)

    return local_call(
        kernel,
        (half, half),
        (bit, value),
        after,
        scratch=(pltpu.VMEM((width, lanes(rows)), jnp.float32),),
        smem=1,
        name="turn",
    )


def attend_back_kernel(projected_ref, log_ref, *refs):
    grad_refs, grads_ref = refs[:-1], refs[-1]
    _, seq_len, width = projected_ref.shape
    low = first_head((seq_len, 2 * HD))
    zero = jnp.zeros((), jnp.bfloat16)
    round_low = lambda v: v.astype(jnp.bfloat16).astype(jnp.float32)
    for pair in range(width // (2 * HD)):
        start, stop = 2 * HD * pair, 2 * HD * (pair + 1)
        cols = slice(start, stop)
        query, key, value = (projected_ref[j, :, cols] for j in range(3))
        grad = jnp.concatenate([one[:, cols] for one in grad_refs], axis=0)
        key_t = jnp.transpose(key)
        grad_query, grad_key, grad_value = [], [], []
        for half in range(2):
            kept = low if half == 0 else ~low
            head = 2 * pair + half
            scores = dot(jnp.where(kept, key, zero), query, NT)
            weights = jnp.exp2(scores * score_rate - log_ref[head : head + 1, :])
            grad_weights = dot(jnp.where(kept, value, zero), grad, NT)
            grad_value.append(dot(weights.astype(jnp.bfloat16), grad))
            row_sum = jnp.sum(grad_weights * weights, axis=0, keepdims=True)
            grad_scores = (weights * (grad_weights - row_sum)).astype(jnp.bfloat16)
            grad_key.append(dot(grad_scores, query))
            grad_query.append(dot(key_t[HD * half : HD * (half + 1)], grad_scores))
        grads_ref[:, start:stop] = round_low(
            jnp.transpose(jnp.concatenate(grad_query, axis=0)) * score_scale
        )
        grads_ref[:, width + start : width + stop] = round_low(
            jnp.where(low, grad_key[0], grad_key[1]) * score_scale
        )
        grads_ref[:, 2 * width + start : 2 * width + stop] = round_low(
            jnp.where(low, grad_value[0], grad_value[1])
        )


def attend_back(projected, log_total, grad_context, after=()):
    _, seq_len, width = projected.shape
    return local_call(
        attend_back_kernel,
        (like((seq_len, 3 * width)),),
        (projected, log_total, *grad_context),
        after,
        name="attend_back",
    )[0]


def mlp_kernel(
    rows, inside, part, places_ref, bit_ref, hidden_ref, context_ref, other_ref, weight_ref, *refs
):
    pieces, (bias_ref, gain_ref, shift_ref, up_ref, up_bias_ref, down_ref) = refs[:4], refs[4:10]
    middle_ref, normed_ref, inverse_ref, turned_ref, given_ref, inner_ref, slope_ref, part_ref = (
        refs[10:18]
    )
    weight_other, act_ref, scratch = refs[18:]

    @pl.when(pl.program_id(0) == 0)
    def _():
        block = pieces[0].shape[0]
        for i, piece in enumerate(pieces):
            start = pl.multiple_of(places_ref[i] * block, block)
            weight_other[pl.ds(start, block)] = piece[...].astype(jnp.bfloat16)
        branch = dot(context_ref[inside].astype(jnp.bfloat16), weight_ref[...]) + dot(
            other_ref[inside].astype(jnp.bfloat16), weight_other[...]
        )
        middle = hidden_ref[rows].astype(jnp.float32) + branch + bias_ref[...]
        normed_out, normed, inverse = layer_norm(middle, gain_ref[...], shift_ref[...])
        middle_ref[...] = middle
        normed_ref[...] = normed
        inverse_ref[...] = inverse
        act = normed_out.astype(jnp.bfloat16)
        act_ref[...] = act
        turn(act.astype(jnp.float32), bit_ref[0], part, scratch, turned_ref, given_ref)

    pre_act = dot(act_ref[...], up_ref[...]) + up_bias_ref[...]
    sigma = 0.5 + 0.5 * jnp.tanh((0.5 * quick_rate) * pre_act)
    inner = (pre_act * sigma).astype(jnp.bfloat16)
    inner_ref[...] = inner.astype(jnp.float32)
    slope_ref[...] = sigma + pre_act * quick_rate * sigma * (1.0 - sigma)
    product = dot(inner, down_ref[...])

    @pl.when(pl.program_id(0) == 0)
    def _():
        part_ref[...] = product

    @pl.when(pl.program_id(0) > 0)
    def _():
        part_ref[...] += product


def mlp_step(
    rows, inside, part, places, bit, hidden, context, other, weight, pieces, bias, gain, shift,
    up, up_bias, down, after=(), tile=1024,
):
    width = hidden.shape[1]
    count = rows.stop - rows.start
    units = up.shape[1]
    ins = (places, bit, hidden, context, other, weight, *pieces, bias, gain, shift)

    def body(*refs):
        mlp_kernel(rows, inside, part, *refs[: len(ins) + 3], *refs[len(ins) + 3 + len(after) :])

    whole = lambda shape: pl.BlockSpec(shape, lambda i: (0,) * len(shape))
    half = (width // 2, lanes(count))
    return pl.pallas_call(
        body,
        out_shape=(
            like((count, width)),
            like((count, width)),
            like((count, 1)),
            like(half),
            like(half),
            like((count, units)),
            like((count, units)),
            like((count, width)),
        ),
        grid=(units // tile,),
        in_specs=[pl.BlockSpec(memory_space=pltpu.SMEM)] * 2
        + [whole(v.shape) for v in ins[2:]]
        + [
            pl.BlockSpec((width, tile), lambda i: (0, i)),
            pl.BlockSpec((1, tile), lambda i: (0, i)),
            pl.BlockSpec((tile, width), lambda i: (i, 0)),
        ]
        + [pl.BlockSpec(memory_space=pl.ANY)] * len(after),
        out_specs=(
            whole((count, width)),
            whole((count, width)),
            whole((count, 1)),
            whole(half),
            whole(half),
            pl.BlockSpec((count, tile), lambda i: (0, i)),
            pl.BlockSpec((count, tile), lambda i: (0, i)),
            whole((count, width)),
        ),
        scratch_shapes=[
            pltpu.VMEM(weight.shape, jnp.bfloat16),
            pltpu.VMEM((count, width), jnp.bfloat16),
            pltpu.VMEM((width, lanes(count)), jnp.float32),
        ],
        compiler_params=pltpu.CompilerParams(vmem_limit_bytes=VMEM_BYTES),
        cost_estimate=BRIEF,
        name="mlp",
    )(*ins, up, up_bias, down, *after)


def result_kernel(
    rows, part, scale_ref, bit_ref, middle_ref, part_ref, other_ref, bias_ref, target_ref, *outs
):
    out_ref, grad_ref, low_ref, turned_ref, given_ref, sums_ref, scratch = outs
    result = middle_ref[...] + (part_ref[...] + other_ref[...]) + bias_ref[...]
    error = result - target_ref[rows].astype(jnp.float32)
    grad = error * scale_ref[0]
    low = grad.astype(jnp.bfloat16)
    out_ref[...] = result.astype(jnp.bfloat16)
    grad_ref[...] = grad
    low_ref[...] = low
    turn(low.astype(jnp.float32), bit_ref[0], part, scratch, turned_ref, given_ref)
    sums_ref[0:1] = jnp.sum(grad, axis=0, keepdims=True)
    sums_ref[1:2] = jnp.sum(error * error, axis=0, keepdims=True)


def result_step(rows, row_part, scale, bit, middle, part, other, bias, target, after=()):
    count, width = middle.shape
    half = like((width // 2, lanes(count)))
    return local_call(
        lambda *refs: result_kernel(rows, row_part, *refs),
        (
            like((count, width), jnp.bfloat16),
            like((count, width)),
            like((count, width), jnp.bfloat16),
            half,
            half,
            like((2, width)),
        ),
        (scale, bit, middle, part, other, bias, target),
        after,
        scratch=(pltpu.VMEM((width, lanes(count)), jnp.float32),),
        smem=2,
        name="result_error",
    )


def mlp_back_kernel(low_ref, slope_ref, down_ref, up_ref, pre_ref, two_ref, sums_ref):
    pre = (dot(low_ref[...], down_ref[...], NT) * slope_ref[...]).astype(jnp.bfloat16)
    pre_ref[...] = pre.astype(jnp.float32)
    sums_ref[...] = jnp.sum(pre.astype(jnp.float32), axis=0, keepdims=True)
    two = dot(pre, up_ref[...], NT)

    @pl.when(pl.program_id(0) == 0)
    def _():
        two_ref[...] = two

    @pl.when(pl.program_id(0) > 0)
    def _():
        two_ref[...] += two


def mlp_back(low, slope, down, up, after=(), tile=512):
    count, width = low.shape
    units = up.shape[1]

    def body(*refs):
        mlp_back_kernel(*refs[:4], *refs[4 + len(after) :])

    return pl.pallas_call(
        body,
        out_shape=(
            like((count, units)),
            like((count, width)),
            like((1, units)),
        ),
        grid=(units // tile,),
        in_specs=[
            pl.BlockSpec((count, width), lambda i: (0, 0)),
            pl.BlockSpec((count, tile), lambda i: (0, i)),
            pl.BlockSpec((tile, width), lambda i: (i, 0)),
            pl.BlockSpec((width, tile), lambda i: (0, i)),
        ]
        + [pl.BlockSpec(memory_space=pl.ANY)] * len(after),
        out_specs=(
            pl.BlockSpec((count, tile), lambda i: (0, i)),
            pl.BlockSpec((count, width), lambda i: (0, 0)),
            pl.BlockSpec((1, tile), lambda i: (0, i)),
        ),
        compiler_params=pltpu.CompilerParams(vmem_limit_bytes=VMEM_BYTES),
        cost_estimate=BRIEF,
        name="mlp_back",
    )(low, slope, down, up, *after)


def middle_back_kernel(
    row_part, before, bit_ref, part_ref, other_ref, grad_ref, normed_ref, inverse_ref, gain_ref,
    weight_ref, *refs
):
    earlier, outs = refs[: 2 * before], refs[2 * before :]
    mid_ref, turned_ref, given_ref, context_ref, sums_ref, scratch = outs
    grad_two = part_ref[...] + other_ref[...]
    normed = normed_ref[...]
    mid = grad_ref[...] + norm_back(grad_two, normed, inverse_ref[...], gain_ref[...])
    low = mid.astype(jnp.bfloat16)
    mid_ref[...] = mid
    context_ref[...] = dot(low, weight_ref[...], NT).astype(jnp.bfloat16)
    rows = low.shape[0]
    start = turned_ref.shape[1] - lanes(rows)
    if before:
        turned_ref[:, :start] = earlier[0][...]
        given_ref[:, :start] = earlier[1][...]
    turn(
        low.astype(jnp.float32),
        bit_ref[0],
        row_part,
        scratch,
        turned_ref.at[:, start:],
        given_ref.at[:, start:],
    )
    sums_ref[0:1] = jnp.sum(mid, axis=0, keepdims=True)
    sums_ref[1:2] = jnp.sum(grad_two * normed, axis=0, keepdims=True)
    sums_ref[2:3] = jnp.sum(grad_two, axis=0, keepdims=True)


def middle_back(
    row_part, bit, part, other, grad, normed, inverse, gain, weight, earlier=(), after=()
):
    count, width = grad.shape
    start = earlier[0].shape[1] if earlier else 0
    half = like((width // 2, start + lanes(count)))
    return local_call(
        lambda *refs: middle_back_kernel(row_part, len(earlier) // 2, *refs),
        (
            like((count, width)),
            half,
            half,
            like((count, weight.shape[0]), jnp.bfloat16),
            like((3, width)),
        ),
        (bit, part, other, grad, normed, inverse, gain, weight, *earlier),
        after,
        scratch=(pltpu.VMEM((width, lanes(count)), jnp.float32),),
        smem=1,
        name="middle_back",
    )


def project_back_kernel(grads_ref, weight_ref, state_ref, part_ref, sums_ref, bias_ref):
    width = weight_ref.shape[2]
    low = lambda j: grads_ref[:, j * width : (j + 1) * width].astype(jnp.bfloat16)
    part = dot(low(0), weight_ref[0], NT)
    for j in (1, 2):
        part = part + dot(low(j), weight_ref[j], NT)
    part_ref[...] = part
    normed = layer_norm(state_ref[...].astype(jnp.float32), 1.0, 0.0)[1]
    sums_ref[0:1] = jnp.sum(part * normed, axis=0, keepdims=True)
    sums_ref[1:2] = jnp.sum(part, axis=0, keepdims=True)
    bias_ref[...] = jnp.sum(grads_ref[...], axis=0, keepdims=True)


def project_back(grads, weight, states, after=()):
    rows, width = states.shape
    return local_call(
        project_back_kernel,
        (like((rows, width)), like((2, width)), like((1, grads.shape[1]))),
        (grads, weight, states),
        after,
        name="project_back",
    )


def last_kernel(count, part_ref, other_ref, state_ref, gain_ref, *refs):
    mids, results, (grad_ref, out_ref) = refs[:count], refs[count : 2 * count], refs[2 * count :]
    start = 0
    for mid, result in zip(mids, results):
        rows = slice(start, start + mid.shape[0])
        _, normed, inverse = layer_norm(state_ref[rows].astype(jnp.float32), 1.0, 0.0)
        grad_one = part_ref[rows] + other_ref[rows]
        grad_ref[rows] = (
            mid[...] + norm_back(grad_one, normed, inverse, gain_ref[...])
        ).astype(jnp.bfloat16)
        out_ref[rows] = result[...]
        start = rows.stop


def last_step(mids, part, other, states, gain, results, after=()):
    return local_call(
        lambda *refs: last_kernel(len(mids), *refs),
        (like(states.shape, jnp.bfloat16),) * 2,
        (part, other, states, gain, *mids, *results),
        after,
        name="input_grad",
    )


def outer_kernel(high, low, plans, bit_ref, *refs):
    count = sum(len(lefts) + rights for _, lefts, rights in plans)
    operands, (give_ref, keep_ref), scratch = refs[:count], refs[count : count + 2], refs[count + 2 :]
    rounded, full = list(scratch[:-1]), scratch[-1]
    operands = list(operands)
    for (first, last), lefts, rights in plans:
        left_refs = [operands.pop(0) for _ in lefts]
        offsets = [start for _, _, start in lefts]
        right_refs = [operands.pop(0) for _ in range(rights)]
        low_refs = [rounded.pop(0) for _ in lefts]

        @pl.when(pl.program_id(0) == first)
        def _():
            for out, left in zip(low_refs, zip(left_refs, offsets)):
                out[...] = left[0][:, left[1] : left[1] + out.shape[1]].astype(jnp.bfloat16)

        @pl.when((pl.program_id(0) >= first) & (pl.program_id(0) < last))
        def _():
            total = None
            for out, (index, rows, _) in zip(low_refs, lefts):
                product = dot(out[...], right_refs[index][rows].astype(jnp.bfloat16))
                total = product if total is None else total + product
            full[...] = total

    part_blocks(full, bit_ref[0], high, low, keep_ref, give_ref)


def outer_sum(bit, high, groups, after=(), tile=512):
    width = groups[0][0][0][0].shape[0]
    low = width // (2 * high)
    operands, specs, scratch, plans = [], [], [], []
    first = 0
    for lefts, rights, start, columns in groups:
        last = first + columns // tile
        places, index, row = [], 0, 0
        for v, offset, rows in lefts:
            operands.append(v)
            specs.append(pl.BlockSpec(v.shape, lambda i: (0, 0)))
            scratch.append(pltpu.VMEM((width, rows), jnp.bfloat16))
            if row == rights[index].shape[0]:
                index, row = index + 1, 0
            places.append((index, slice(row, row + rows), offset))
            row += rows
        for v in rights:
            operands.append(v)
            place = lambda i, s=start // tile, f=first, n=last - first: (
                0,
                s + jnp.clip(i - f, 0, n - 1),
            )
            specs.append(pl.BlockSpec((v.shape[0], tile), place))
        plans.append(((first, last), places, len(rights)))
        first = last

    def body(*refs):
        count = 1 + len(operands)
        outer_kernel(high, low, plans, *refs[:count], *refs[count + len(after) :])

    return pl.pallas_call(
        body,
        out_shape=(like((width // 2, first * tile)),) * 2,
        grid=(first,),
        in_specs=[pl.BlockSpec(memory_space=pltpu.SMEM)]
        + specs
        + [pl.BlockSpec(memory_space=pl.ANY)] * len(after),
        out_specs=(pl.BlockSpec((width // 2, tile), lambda i: (0, i)),) * 2,
        scratch_shapes=scratch + [pltpu.VMEM((width, tile), jnp.float32)],
        compiler_params=pltpu.CompilerParams(vmem_limit_bytes=VMEM_BYTES),
        cost_estimate=BRIEF,
        name="weight_grad",
    )(bit, *operands, *after)


def split_kernel(count, bit_ref, *refs):
    bit = bit_ref[0]
    keeps, cames, (give_out, keep_out) = refs[:count], refs[count : 2 * count], refs[2 * count :]
    start = 0
    for keep_ref, came_ref in zip(keeps, cames):
        columns = slice(start, start + keep_ref.shape[-1])
        keep_out[0, :, columns] = keep_ref[0, bit] + came_ref[0, bit]
        give_out[0, :, columns] = keep_ref[0, 1 - bit] + came_ref[0, 1 - bit]
        start = columns.stop


def add_split(bit, keeps, cames, high):
    rows = keeps[0].shape[0]
    low = rows // (2 * high)
    blocks = [v.reshape(high, 2, low, v.shape[1]) for v in (*keeps, *cames)]
    columns = sum(v.shape[1] for v in keeps)
    give, kept = pl.pallas_call(
        lambda *refs: split_kernel(len(keeps), *refs),
        out_shape=(like((high, low, columns)),) * 2,
        grid=(high,),
        in_specs=[pl.BlockSpec(memory_space=pltpu.SMEM)]
        + [pl.BlockSpec((1, *v.shape[1:]), lambda i: (i, 0, 0, 0)) for v in blocks],
        out_specs=(pl.BlockSpec((1, low, columns), lambda i: (i, 0, 0)),) * 2,
        compiler_params=pltpu.CompilerParams(vmem_limit_bytes=VMEM_BYTES),
        cost_estimate=BRIEF,
        name="add_split",
    )(bit, *blocks)
    return give.reshape(rows // 2, columns), kept.reshape(rows // 2, columns)


def finish_kernel(counts, *refs):
    total = sum(counts)
    pairs, outs = list(zip(refs[:total], refs[total : 2 * total])), refs[2 * total :]
    for count, out in zip(counts, outs):
        start = 0
        for _ in range(count):
            keep_ref, came_ref = pairs.pop(0)
            stop = start + keep_ref.shape[1]
            out[:, start:stop] = keep_ref[...] + came_ref[...]
            start = stop


def finish_all(results, after=()):
    return local_call(
        lambda *refs: finish_kernel([len(keeps) for keeps, _ in results], *refs),
        [like((one[0].shape[0], sum(v.shape[1] for v in one))) for one, _ in results],
        (*(v for one, _ in results for v in one), *(v for _, one in results for v in one)),
        after,
        name="finish",
    )


def pack_kernel(counts, valid_ref, *refs):
    ins, out = list(refs[:-1]), refs[-1]
    one, other, projected = ins[:3]
    rest = ins[3:]
    middles, ups, results = (
        rest[: counts],
        rest[counts : 2 * counts],
        rest[2 * counts :],
    )
    width = out.shape[1]
    total = lambda parts: sum(part[...] for part in parts[1:]) + parts[0][...]
    out[...] = jnp.zeros_like(out)
    out[0:2] = one[...] + other[...]
    local = projected.shape[1] // 3
    out[2:3, :local] = projected[:, :local]
    out[2:3, local : 2 * local] = projected[:, 2 * local :]
    out[3:6] = total(middles)
    up = total(ups)
    rows = up.shape[1] // width
    for row in range(rows):
        out[6 + row : 7 + row] = up[:, row * width : (row + 1) * width]
    result = total(results)
    out[6 + rows : 7 + rows] = result[0:1]
    out[7 + rows : 8 + rows] = result[1:2] * valid_ref[0]


def pack(valid, one, other, projected, middles, ups, results):
    width = one.shape[1]
    rows = -(-(8 + ups[0].shape[1] // width) // 8) * 8
    return local_call(
        lambda *refs: pack_kernel(len(middles), *refs),
        (like((rows, width)),),
        (valid, one, other, projected, *middles, *ups, *results),
        smem=1,
        name="pack",
    )[0]


def tie(value, *others):
    return lax.optimization_barrier((value, *others))[0]


def make_shards(mesh):
    groups = mesh.shape["dp"]
    bits = groups.bit_length() - 1
    assert groups == 1 << bits and mesh.shape["tensor"] == 2

    def swap_tensor(value):
        return lax.ppermute(value, "tensor", [(0, 1), (1, 0)])

    def swap_bit(value, bit):
        return lax.ppermute(value, "dp", [(i, i ^ (1 << bit)) for i in range(groups)])

    def sum_dp(value):
        for bit in range(bits):
            value = value + swap_bit(value, bit)
        return value

    def own_bit(bit):
        return ((lax.axis_index("dp") >> bit) & 1).astype(jnp.int32).reshape(1)

    class Scatter:
        def __init__(self, groups_of, order, after=(), tile=512):
            self.left = list(range(1, bits))[::-1]
            self.order = list(order)
            bit = self.order[0]
            self.give, self.keep = outer_sum(
                own_bit(bit), 1 << self.left.index(bit), groups_of, after, tile
            )
            self.keep, self.came = [self.keep], None

        def send(self):
            bit = self.order.pop(0)
            self.came = [swap_bit(self.give, bit)]
            self.left.remove(bit)
            self.give = None

        def join(self, other):
            self.keep = self.keep + other.keep
            self.came = self.came + other.came

        def fold(self):
            bit = self.order[0]
            self.give, keep = add_split(
                own_bit(bit), self.keep, self.came, 1 << self.left.index(bit)
            )
            self.keep, self.came = [keep], None

        def move(self):
            self.fold()
            self.send()

        def last(self):
            while self.order:
                self.move()
            return self

    def sync(scatters, *arrays):
        held = [(one.give, one.keep, one.came) for one in scatters]
        held, arrays = lax.optimization_barrier((held, arrays))
        for one, (give, keep, came) in zip(scatters, held):
            one.give, one.keep, one.came = give, keep, came
        return arrays

    def shards(
        images,
        teacher,
        image_mask,
        attn_gain,
        attn_shift,
        in_weight,
        in_bias,
        out_weight,
        out_bias,
        mlp_gain,
        mlp_shift,
        up_weight,
        up_bias,
        down_weight,
        down_bias,
    ):
        image_count, seq_len, width = images.shape
        row_count = image_count * seq_len
        local_width = in_weight.shape[2]
        scales_one = jnp.stack([attn_gain, attn_shift]).astype(jnp.float32)
        gain_one = scales_one[0:1]
        gain_two = mlp_gain.astype(jnp.float32)[None]
        shift_two = mlp_shift.astype(jnp.float32)[None]
        bias_out = out_bias.astype(jnp.float32)[None]
        bias_up = up_bias.astype(jnp.float32)[None]
        bias_down = down_bias.astype(jnp.float32)[None]
        weights_in = jnp.swapaxes(in_weight, 0, 1)
        chunks, start = [], 0
        for stop in (352, row_count):
            chunks.append(slice(start, stop))
            start = stop
        cut = chunks[0].stop
        part = width // groups
        core_bit = own_bit(0)
        low_first = tuple(range(1, bits))
        swap_core = lambda value: swap_bit(value, 0)

        quarter = local_width // 4
        dp_index = lax.axis_index("dp")
        piece = lax.dynamic_slice_in_dim(out_weight, (dp_index & 3) * quarter, quarter, axis=0)
        pieces = [swap_tensor(piece.astype(jnp.float32))]
        places = jnp.stack([(dp_index & 3) ^ way for way in (0, 2, 1, 3)]).astype(jnp.int32)

        states = images.reshape(row_count, width)
        targets = teacher.reshape(row_count, width)
        act_one, projected = enter(states, scales_one, weights_in, in_bias)
        *context, log_total = attend(projected, chunks[0].stop)
        context_other = [swap_tensor(one) for one in context]
        pieces.append(swap_bit(tie(pieces[0], log_total), 1))
        pieces += [swap_core(one) for one in pieces]

        valid = image_mask.astype(jnp.float32)[0]
        count = tie(jnp.full((8, 128), valid * seq_len, jnp.float32), log_total)
        count = count + swap_bit(count, 0)
        turned_one, given_one = turn_step(core_bit, act_one, part, (log_total,))

        middle, normed_two, inverse_two, turned_two, given_two, inner, slope, mlp_part = mlp_out = [
            [] for _ in range(8)
        ]
        count, turned_one, given_one, context, context_other[0], pieces = sync(
            [], count, turned_one, given_one, context, context_other[0], pieces
        )
        more = swap_bit(count, 1)

        def mlp_of(i):
            rows = chunks[i]
            step = mlp_step(
                rows,
                slice(0, rows.stop - rows.start),
                part,
                places,
                core_bit,
                states,
                context[i],
                context_other[i],
                out_weight,
                pieces,
                bias_out,
                gain_two,
                shift_two,
                up_weight,
                bias_up,
                down_weight,
            )
            for kept, one in zip(mlp_out, step):
                kept.append(one)

        mlp_of(0)
        mlp_part[0], given_two[0], inner[0], given_one, context, context_other[1], count, more = sync(
            [], mlp_part[0], given_two[0], inner[0], given_one, context, context_other[1], count, more
        )
        count = count + more
        mlp_other = [swap_tensor(mlp_part[0])]
        came_two, came_inner = [swap_core(given_two[0])], [swap_core(inner[0])]
        came_one = swap_core(given_one)
        more = swap_bit(count, 2)
        mlp_of(1)
        mlp_part[1], given_two[1], inner[1], came_two, came_inner, came_one, count, more = sync(
            [], mlp_part[1], given_two[1], inner[1], came_two, came_inner, came_one, count, more
        )
        count = count + more
        mlp_other.append(swap_tensor(mlp_part[1]))
        for bit in range(3, bits):
            count = count + swap_bit(count, bit)
        mlp_other[0], given_two[1], inner[1], count = sync(
            [], mlp_other[0], given_two[1], inner[1], count
        )
        count_all = count[:1, 0]
        scale = 2.0 * valid / count_all

        result, grad_result, grad_low, turned_low, given_low, result_sums = result_out = [
            [] for _ in range(6)
        ]
        grad_pre, two_part, up_sums = back_out = [[], [], []]
        two_other = []

        def result_of(i, after):
            step = result_step(
                chunks[i],
                part,
                scale,
                core_bit,
                middle[i],
                mlp_part[i],
                mlp_other[i],
                bias_down,
                targets,
                after,
            )
            for kept, one in zip(result_out, step):
                kept.append(one)

        def back_of(i, after):
            step = mlp_back(grad_low[i], slope[i], down_weight, up_weight, after)
            for kept, one in zip(back_out, step):
                kept.append(one)
            two_other.append(swap_tensor(two_part[i]))
            return (two_part[i],)

        grad_middle, turned_attn, given_attn, grad_context, middle_sums = middle_out = [
            [] for _ in range(5)
        ]

        def middle_of(i, earlier, after):
            step = middle_back(
                part,
                core_bit,
                two_part[i],
                two_other[i],
                grad_result[i],
                normed_two[i],
                inverse_two[i],
                gain_two,
                out_weight,
                earlier,
                after,
            )
            for kept, one in zip(middle_out, step):
                kept.append(one)
            return (grad_context[i],)

        def rows_of(values):
            return [(one, 0, rows.stop - rows.start) for one, rows in zip(values, chunks * 2)]

        half = up_weight.shape[1] // 2
        came_two.append(swap_core(given_two[1]))
        came_inner.append(swap_core(inner[1]))
        came_context = [swap_core(one) for one in context]
        result_of(0, ())
        back_of(0, ())
        came_two, came_inner, came_context, grad_pre[0], given_low[0], two_part[0] = sync(
            [], came_two, came_inner, came_context, grad_pre[0], given_low[0], two_part[0]
        )
        two_other = [swap_tensor(two_part[0])]
        came_low = [swap_core(given_low[0])]
        result_of(1, (two_part[0],))
        given_low[1], grad_low[1], slope[1] = sync([], given_low[1], grad_low[1], slope[1])

        came_low.append(swap_core(given_low[1]))
        (came_low,) = sync([], came_low)

        left, right = rows_of(turned_low + came_low), inner + came_inner
        first_units = 3 * half // 4
        down_b = Scatter([(left, right, 0, first_units)], low_first, (), first_units)
        grad_low[1], slope[1] = sync([down_b], grad_low[1], slope[1])

        down_b.send()
        back_of(1, ())
        down_d = Scatter(
            [(left, right, first_units, 2 * half - first_units)],
            low_first,
            (two_part[1],),
            first_units // 3,
        )
        two_part[1], grad_pre, two_other[0] = sync(
            [down_b, down_d], two_part[1], grad_pre, two_other[0]
        )

        two_other.append(swap_tensor(two_part[1]))
        down_d.send()
        came_pre = [swap_core(one) for one in grad_pre]
        down_b.move()
        middle_of(0, (), ())
        left, right = rows_of(turned_two + came_two), grad_pre + came_pre
        up_a = Scatter([(left, right, 0, half)], low_first, (grad_context[0],))
        up_b = Scatter([(left, right, half, half)], low_first, (up_a.give,))
        middle_of(1, (turned_attn[0], given_attn[0]), (up_b.give,))
        turned_attn[1], given, grad_context = sync(
            [down_b, down_d, up_a, up_b], turned_attn[1], given_attn[1], grad_context
        )

        up_a.send()
        down_b.move()
        down_d.move()
        grads = attend_back(projected, log_total, grad_context)
        grads, given = sync([down_b, down_d, up_a, up_b], grads, given)

        up_b.send()
        came_grads = swap_core(grads)
        came_attn = swap_core(given)
        up_a.move()
        down_d.move()
        one_part, one_sums, in_sums = project_back(grads, weights_in, states)
        left = [(turned_one, 0, row_count), (came_one, 0, row_count)]
        right = [grads, came_grads]
        in_a = Scatter([(left, right, 0, 2 * local_width)], low_first, (one_part,))
        in_b = Scatter([(left, right, 2 * local_width, local_width)], low_first, (in_a.give,))
        first = swap_tensor(one_sums)
        one_part, one_sums, first, came_attn = sync(
            [down_b, down_d, up_a, up_b, in_a, in_b], one_part, one_sums, first, came_attn
        )

        one_other = swap_tensor(one_part)
        in_a.send()
        up_a.move()
        up_b.move()
        starts = (0, lanes(chunks[0].stop))
        left = [
            (one, start, rows.stop - rows.start)
            for one in (turned_attn[1], came_attn)
            for start, rows in zip(starts, chunks)
        ]
        out_all = Scatter([(left, [*context, *came_context], 0, local_width)], low_first)
        full_down = finish_all(
            [(down_b.last().keep + down_d.last().keep, down_b.came + down_d.came)]
        )[0]
        small = pack(valid.reshape(1), one_sums, first, in_sums, middle_sums, up_sums, result_sums)
        small = small + swap_bit(small, 0)
        more = swap_bit(small, 1)
        small, more, full_down = sync([up_a, up_b, in_a, in_b, out_all], small, more, full_down)

        in_b.send()
        in_a.move()
        up_b.move()
        small = small + more
        more = swap_bit(small, 2)
        small, more = sync([up_a, up_b, in_a, in_b, out_all], small, more)

        out_all.send()
        in_b.move()
        in_a.move()
        small = small + more
        more = swap_bit(small, 3)
        (full_up,) = finish_all(
            [(up_a.last().keep + up_b.last().keep, up_a.came + up_b.came)]
        )
        small, more, full_up = sync([in_a, in_b, out_all], small, more, full_up)

        out_all.move()
        in_b.move()
        small = small + more
        for bit in range(4, bits):
            small = small + swap_bit(small, bit)
        grad_images, block_out = last_step(
            grad_middle, one_part, one_other, states, gain_one, result
        )
        small, grad_images, block_out = sync([in_a, in_b, out_all], small, grad_images, block_out)

        out_all.move()
        in_a.last(), in_b.last()
        (full_in,) = finish_all([(in_a.keep + in_b.keep, in_a.came + in_b.came)])
        (full_out,) = finish_all([(out_all.last().keep, out_all.came)])
        up_rows = up_bias.shape[0] // width
        small_up = small[6 : 6 + up_rows].reshape(-1)
        shape = (image_count, seq_len, width)
        return (
            block_out.reshape(shape),
            jnp.sum(small[7 + up_rows]) / count_all[0],
            grad_images.reshape(shape),
            small[0],
            small[1],
            full_in.reshape(-1, 3, local_width),
            small[2].reshape(2, local_width),
            full_out.T,
            small[3],
            small[4],
            small[5],
            full_up,
            small_up,
            full_down.T,
            small[6 + up_rows],
        )

    return shards


def solution(mesh):
    placed = (
        P("dp", None, None),
        P("dp", None, None),
        P("dp"),
        P(),
        P(),
        P(None, None, "tensor"),
        P(None, "tensor"),
        P("tensor", None),
        P(),
        P(),
        P(),
        P(None, "tensor"),
        P("tensor"),
        P("tensor", None),
        P(),
    )
    return jax.shard_map(
        make_shards(mesh),
        mesh=mesh,
        in_specs=placed,
        out_specs=(
            P("dp", None, None),
            P(),
            P("dp", None, None),
            P(),
            P(),
            P("dp", None, "tensor"),
            P(None, "tensor"),
            P("tensor", "dp"),
            P(),
            P(),
            P(),
            P("dp", "tensor"),
            P("tensor"),
            P("tensor", "dp"),
            P(),
        ),
        check_vma=False,
    )
```

```python
import jax
import jax.numpy as jnp
from jax import lax
from jax.experimental import pallas as pl
from jax.experimental.pallas import tpu as pltpu
from jax.sharding import PartitionSpec as P

HD = 64

epsilon = 1e-05
score_scale = 0.125
quick_rate = 1.702
log2_e = 1.4426950408889634
score_rate = score_scale * log2_e

NN = (((1,), (0,)), ((), ()))
NT = (((1,), (1,)), ((), ()))
VMEM_BYTES = 48 * 2**20
BRIEF = pl.CostEstimate(flops=1, bytes_accessed=1, transcendentals=0)


def dot(matrix_a, matrix_b, dims=NN):
    return lax.dot_general(matrix_a, matrix_b, dims, preferred_element_type=jnp.float32)


def layer_norm(hidden, scales, offset):
    centred = hidden - jnp.mean(hidden, axis=-1, keepdims=True)
    inverse = lax.rsqrt(jnp.mean(centred * centred, axis=-1, keepdims=True) + epsilon)
    normed = centred * inverse
    return (normed * scales + offset, normed, inverse)


def norm_back(grad_out, normed, inverse, scales):
    scaled = grad_out * scales
    centred = scaled - jnp.mean(scaled, axis=-1, keepdims=True)
    return (centred - normed * jnp.mean(scaled * normed, axis=-1, keepdims=True)) * inverse


def first_head(shape):
    return lax.broadcasted_iota(jnp.int32, shape, len(shape) - 1) < HD


def local_call(
    kernel, outs, ins, after=(), scratch=(), smem=0, name=None
):
    count = len(ins)

    def body(*refs):
        kernel(*refs[:count], *refs[count + len(after) :])

    return pl.pallas_call(
        body,
        out_shape=tuple(outs),
        in_specs=[pl.BlockSpec(memory_space=pltpu.SMEM)] * smem
        + [pl.BlockSpec(memory_space=pltpu.VMEM)] * (count - smem)
        + [pl.BlockSpec(memory_space=pl.ANY)] * len(after),
        out_specs=tuple(pl.BlockSpec(memory_space=pltpu.VMEM) for _ in outs),
        scratch_shapes=list(scratch),
        compiler_params=pltpu.CompilerParams(vmem_limit_bytes=VMEM_BYTES),
        cost_estimate=BRIEF,
        name=name,
    )(*ins, *after)


def part_blocks(source, bit, high, low, keep_ref, give_ref):
    for j in range(high):
        keep_ref[low * j : low * (j + 1)] = source[
            pl.ds(pl.multiple_of((2 * j + bit) * low, 8), low)
        ]
        give_ref[low * j : low * (j + 1)] = source[
            pl.ds(pl.multiple_of((2 * j + 1 - bit) * low, 8), low)
        ]


def lanes(rows):
    return -(-rows // 128) * 128


def turn(value, bit, part, scratch, keep_ref, give_ref):
    rows = value.shape[0]
    scratch[:, :rows] = jnp.transpose(value)
    if scratch.shape[1] > rows:
        scratch[:, rows:] = jnp.zeros((scratch.shape[0], scratch.shape[1] - rows), jnp.float32)
    part_blocks(scratch, bit, value.shape[1] // (2 * part), part, keep_ref, give_ref)


def like(shape, dtype=jnp.float32):
    return jax.ShapeDtypeStruct(shape, dtype)


def enter_kernel(state_ref, scales_ref, weight_ref, bias_ref, act_ref, out_ref):
    which = pl.program_id(0)

    @pl.when(which == 0)
    def _():
        act_ref[...] = layer_norm(
            state_ref[...].astype(jnp.float32), scales_ref[0:1], scales_ref[1:2]
        )[0].astype(jnp.bfloat16)

    biases = bias_ref[...].astype(jnp.float32)
    zero = jnp.zeros_like(biases[0:1])
    bias = jnp.where(which == 0, biases[0:1], jnp.where(which == 2, biases[1:2], zero))
    out_ref[0] = (dot(act_ref[...], weight_ref[0]) + bias).astype(jnp.bfloat16)


def enter(states, scales, weight, bias):
    rows, width = states.shape
    local = weight.shape[2]
    return pl.pallas_call(
        enter_kernel,
        out_shape=(
            like((rows, width), jnp.bfloat16),
            like((3, rows, local), jnp.bfloat16),
        ),
        grid=(3,),
        in_specs=[
            pl.BlockSpec((rows, width), lambda i: (0, 0)),
            pl.BlockSpec((2, width), lambda i: (0, 0)),
            pl.BlockSpec((1, width, local), lambda i: (i, 0, 0)),
            pl.BlockSpec((2, local), lambda i: (0, 0)),
        ],
        out_specs=(
            pl.BlockSpec((rows, width), lambda i: (0, 0)),
            pl.BlockSpec((1, rows, local), lambda i: (i, 0, 0)),
        ),
        compiler_params=pltpu.CompilerParams(vmem_limit_bytes=VMEM_BYTES),
        cost_estimate=BRIEF,
        name="norm_project",
    )(states, scales, weight, bias)


def attend_kernel(projected_ref, first_ref, second_ref, log_ref):
    _, seq_len, width = projected_ref.shape
    cut = first_ref.shape[0]
    low = first_head((seq_len, 2 * HD))
    zero = jnp.zeros((), jnp.bfloat16)
    for pair in range(width // (2 * HD)):
        start, stop = 2 * HD * pair, 2 * HD * (pair + 1)
        cols = slice(start, stop)
        query, key = projected_ref[0, :, cols], projected_ref[1, :, cols]
        value_t = jnp.transpose(projected_ref[2, :, cols])
        parts = []
        for half in range(2):
            one_key = jnp.where(low if half == 0 else ~low, key, zero)
            scores = dot(one_key, query, NT)
            top = jnp.max(scores, axis=0, keepdims=True)
            weights = jnp.exp2((scores - top) * score_rate)
            total = jnp.sum(weights, axis=0, keepdims=True)
            weights_low = (weights * (1.0 / total)).astype(jnp.bfloat16)
            parts.append(dot(value_t[HD * half : HD * (half + 1)], weights_low))
            head = 2 * pair + half
            log_ref[head : head + 1, :] = top * score_rate + jnp.log2(total)
        context = jnp.transpose(jnp.concatenate(parts, axis=0)).astype(jnp.bfloat16)
        context = context.astype(jnp.float32)
        first_ref[:, cols] = context[:cut]
        second_ref[:, cols] = context[cut:]


def attend(projected, cut, after=()):
    _, rows, width = projected.shape
    return local_call(
        attend_kernel,
        (like((cut, width)), like((rows - cut, width)), like((width // HD, rows))),
        (projected,),
        after,
        name="attend",
    )


def turn_step(bit, value, part, after=()):
    rows, width = value.shape
    half = like((width // 2, lanes(rows)))

    def kernel(bit_ref, value_ref, keep_ref, give_ref, scratch):
        turn(value_ref[...].astype(jnp.float32), bit_ref[0], part, scratch, keep_ref, give_ref)

    return local_call(
        kernel,
        (half, half),
        (bit, value),
        after,
        scratch=(pltpu.VMEM((width, lanes(rows)), jnp.float32),),
        smem=1,
        name="turn",
    )


def attend_back_kernel(projected_ref, log_ref, *refs):
    grad_refs, grads_ref = refs[:-1], refs[-1]
    _, seq_len, width = projected_ref.shape
    low = first_head((seq_len, 2 * HD))
    zero = jnp.zeros((), jnp.bfloat16)
    round_low = lambda v: v.astype(jnp.bfloat16).astype(jnp.float32)
    for pair in range(width // (2 * HD)):
        start, stop = 2 * HD * pair, 2 * HD * (pair + 1)
        cols = slice(start, stop)
        query, key, value = (projected_ref[j, :, cols] for j in range(3))
        grad = jnp.concatenate([one[:, cols] for one in grad_refs], axis=0)
        key_t = jnp.transpose(key)
        grad_query, grad_key, grad_value = [], [], []
        for half in range(2):
            kept = low if half == 0 else ~low
            head = 2 * pair + half
            scores = dot(jnp.where(kept, key, zero), query, NT)
            weights = jnp.exp2(scores * score_rate - log_ref[head : head + 1, :])
            grad_weights = dot(jnp.where(kept, value, zero), grad, NT)
            grad_value.append(dot(weights.astype(jnp.bfloat16), grad))
            row_sum = jnp.sum(grad_weights * weights, axis=0, keepdims=True)
            grad_scores = (weights * (grad_weights - row_sum)).astype(jnp.bfloat16)
            grad_key.append(dot(grad_scores, query))
            grad_query.append(dot(key_t[HD * half : HD * (half + 1)], grad_scores))
        grads_ref[:, start:stop] = round_low(
            jnp.transpose(jnp.concatenate(grad_query, axis=0)) * score_scale
        )
        grads_ref[:, width + start : width + stop] = round_low(
            jnp.where(low, grad_key[0], grad_key[1]) * score_scale
        )
        grads_ref[:, 2 * width + start : 2 * width + stop] = round_low(
            jnp.where(low, grad_value[0], grad_value[1])
        )


def attend_back(projected, log_total, grad_context, after=()):
    _, seq_len, width = projected.shape
    return local_call(
        attend_back_kernel,
        (like((seq_len, 3 * width)),),
        (projected, log_total, *grad_context),
        after,
        name="attend_back",
    )[0]


def mlp_kernel(
    rows, inside, part, places_ref, bit_ref, hidden_ref, context_ref, other_ref, weight_ref, *refs
):
    pieces, (bias_ref, gain_ref, shift_ref, up_ref, up_bias_ref, down_ref) = refs[:4], refs[4:10]
    middle_ref, normed_ref, inverse_ref, turned_ref, given_ref, inner_ref, slope_ref, part_ref = (
        refs[10:18]
    )
    weight_other, act_ref, scratch = refs[18:]

    @pl.when(pl.program_id(0) == 0)
    def _():
        block = pieces[0].shape[0]
        for i, piece in enumerate(pieces):
            start = pl.multiple_of(places_ref[i] * block, block)
            weight_other[pl.ds(start, block)] = piece[...].astype(jnp.bfloat16)
        branch = dot(context_ref[inside].astype(jnp.bfloat16), weight_ref[...]) + dot(
            other_ref[inside].astype(jnp.bfloat16), weight_other[...]
        )
        middle = hidden_ref[rows].astype(jnp.float32) + branch + bias_ref[...]
        normed_out, normed, inverse = layer_norm(middle, gain_ref[...], shift_ref[...])
        middle_ref[...] = middle
        normed_ref[...] = normed
        inverse_ref[...] = inverse
        act = normed_out.astype(jnp.bfloat16)
        act_ref[...] = act
        turn(act.astype(jnp.float32), bit_ref[0], part, scratch, turned_ref, given_ref)

    pre_act = dot(act_ref[...], up_ref[...]) + up_bias_ref[...]
    sigma = 0.5 + 0.5 * jnp.tanh((0.5 * quick_rate) * pre_act)
    inner = (pre_act * sigma).astype(jnp.bfloat16)
    inner_ref[...] = inner.astype(jnp.float32)
    slope_ref[...] = sigma + pre_act * quick_rate * sigma * (1.0 - sigma)
    product = dot(inner, down_ref[...])

    @pl.when(pl.program_id(0) == 0)
    def _():
        part_ref[...] = product

    @pl.when(pl.program_id(0) > 0)
    def _():
        part_ref[...] += product


def mlp_step(
    rows, inside, part, places, bit, hidden, context, other, weight, pieces, bias, gain, shift,
    up, up_bias, down, after=(), tile=1024,
):
    width = hidden.shape[1]
    count = rows.stop - rows.start
    units = up.shape[1]
    ins = (places, bit, hidden, context, other, weight, *pieces, bias, gain, shift)

    def body(*refs):
        mlp_kernel(rows, inside, part, *refs[: len(ins) + 3], *refs[len(ins) + 3 + len(after) :])

    whole = lambda shape: pl.BlockSpec(shape, lambda i: (0,) * len(shape))
    half = (width // 2, lanes(count))
    return pl.pallas_call(
        body,
        out_shape=(
            like((count, width)),
            like((count, width)),
            like((count, 1)),
            like(half),
            like(half),
            like((count, units)),
            like((count, units)),
            like((count, width)),
        ),
        grid=(units // tile,),
        in_specs=[pl.BlockSpec(memory_space=pltpu.SMEM)] * 2
        + [whole(v.shape) for v in ins[2:]]
        + [
            pl.BlockSpec((width, tile), lambda i: (0, i)),
            pl.BlockSpec((1, tile), lambda i: (0, i)),
            pl.BlockSpec((tile, width), lambda i: (i, 0)),
        ]
        + [pl.BlockSpec(memory_space=pl.ANY)] * len(after),
        out_specs=(
            whole((count, width)),
            whole((count, width)),
            whole((count, 1)),
            whole(half),
            whole(half),
            pl.BlockSpec((count, tile), lambda i: (0, i)),
            pl.BlockSpec((count, tile), lambda i: (0, i)),
            whole((count, width)),
        ),
        scratch_shapes=[
            pltpu.VMEM(weight.shape, jnp.bfloat16),
            pltpu.VMEM((count, width), jnp.bfloat16),
            pltpu.VMEM((width, lanes(count)), jnp.float32),
        ],
        compiler_params=pltpu.CompilerParams(vmem_limit_bytes=VMEM_BYTES),
        cost_estimate=BRIEF,
        name="mlp",
    )(*ins, up, up_bias, down, *after)


def result_kernel(
    rows, part, scale_ref, bit_ref, middle_ref, part_ref, other_ref, bias_ref, target_ref, *outs
):
    out_ref, grad_ref, low_ref, turned_ref, given_ref, sums_ref, scratch = outs
    result = middle_ref[...] + (part_ref[...] + other_ref[...]) + bias_ref[...]
    error = result - target_ref[rows].astype(jnp.float32)
    grad = error * scale_ref[0]
    low = grad.astype(jnp.bfloat16)
    out_ref[...] = result.astype(jnp.bfloat16)
    grad_ref[...] = grad
    low_ref[...] = low
    turn(low.astype(jnp.float32), bit_ref[0], part, scratch, turned_ref, given_ref)
    sums_ref[0:1] = jnp.sum(grad, axis=0, keepdims=True)
    sums_ref[1:2] = jnp.sum(error * error, axis=0, keepdims=True)


def result_step(rows, row_part, scale, bit, middle, part, other, bias, target, after=()):
    count, width = middle.shape
    half = like((width // 2, lanes(count)))
    return local_call(
        lambda *refs: result_kernel(rows, row_part, *refs),
        (
            like((count, width), jnp.bfloat16),
            like((count, width)),
            like((count, width), jnp.bfloat16),
            half,
            half,
            like((2, width)),
        ),
        (scale, bit, middle, part, other, bias, target),
        after,
        scratch=(pltpu.VMEM((width, lanes(count)), jnp.float32),),
        smem=2,
        name="result_error",
    )


def mlp_back_kernel(low_ref, slope_ref, down_ref, up_ref, pre_ref, two_ref, sums_ref):
    pre = (dot(low_ref[...], down_ref[...], NT) * slope_ref[...]).astype(jnp.bfloat16)
    pre_ref[...] = pre.astype(jnp.float32)
    sums_ref[...] = jnp.sum(pre.astype(jnp.float32), axis=0, keepdims=True)
    two = dot(pre, up_ref[...], NT)

    @pl.when(pl.program_id(0) == 0)
    def _():
        two_ref[...] = two

    @pl.when(pl.program_id(0) > 0)
    def _():
        two_ref[...] += two


def mlp_back(low, slope, down, up, after=(), tile=512):
    count, width = low.shape
    units = up.shape[1]

    def body(*refs):
        mlp_back_kernel(*refs[:4], *refs[4 + len(after) :])

    return pl.pallas_call(
        body,
        out_shape=(
            like((count, units)),
            like((count, width)),
            like((1, units)),
        ),
        grid=(units // tile,),
        in_specs=[
            pl.BlockSpec((count, width), lambda i: (0, 0)),
            pl.BlockSpec((count, tile), lambda i: (0, i)),
            pl.BlockSpec((tile, width), lambda i: (i, 0)),
            pl.BlockSpec((width, tile), lambda i: (0, i)),
        ]
        + [pl.BlockSpec(memory_space=pl.ANY)] * len(after),
        out_specs=(
            pl.BlockSpec((count, tile), lambda i: (0, i)),
            pl.BlockSpec((count, width), lambda i: (0, 0)),
            pl.BlockSpec((1, tile), lambda i: (0, i)),
        ),
        compiler_params=pltpu.CompilerParams(vmem_limit_bytes=VMEM_BYTES),
        cost_estimate=BRIEF,
        name="mlp_back",
    )(low, slope, down, up, *after)


def middle_back_kernel(
    row_part, before, bit_ref, part_ref, other_ref, grad_ref, normed_ref, inverse_ref, gain_ref,
    weight_ref, *refs
):
    earlier, outs = refs[: 2 * before], refs[2 * before :]
    mid_ref, turned_ref, given_ref, context_ref, sums_ref, scratch = outs
    grad_two = part_ref[...] + other_ref[...]
    normed = normed_ref[...]
    mid = grad_ref[...] + norm_back(grad_two, normed, inverse_ref[...], gain_ref[...])
    low = mid.astype(jnp.bfloat16)
    mid_ref[...] = mid
    context_ref[...] = dot(low, weight_ref[...], NT).astype(jnp.bfloat16)
    rows = low.shape[0]
    start = turned_ref.shape[1] - lanes(rows)
    if before:
        turned_ref[:, :start] = earlier[0][...]
        given_ref[:, :start] = earlier[1][...]
    turn(
        low.astype(jnp.float32),
        bit_ref[0],
        row_part,
        scratch,
        turned_ref.at[:, start:],
        given_ref.at[:, start:],
    )
    sums_ref[0:1] = jnp.sum(mid, axis=0, keepdims=True)
    sums_ref[1:2] = jnp.sum(grad_two * normed, axis=0, keepdims=True)
    sums_ref[2:3] = jnp.sum(grad_two, axis=0, keepdims=True)


def middle_back(
    row_part, bit, part, other, grad, normed, inverse, gain, weight, earlier=(), after=()
):
    count, width = grad.shape
    start = earlier[0].shape[1] if earlier else 0
    half = like((width // 2, start + lanes(count)))
    return local_call(
        lambda *refs: middle_back_kernel(row_part, len(earlier) // 2, *refs),
        (
            like((count, width)),
            half,
            half,
            like((count, weight.shape[0]), jnp.bfloat16),
            like((3, width)),
        ),
        (bit, part, other, grad, normed, inverse, gain, weight, *earlier),
        after,
        scratch=(pltpu.VMEM((width, lanes(count)), jnp.float32),),
        smem=1,
        name="middle_back",
    )


def project_back_kernel(grads_ref, weight_ref, state_ref, part_ref, sums_ref, bias_ref):
    width = weight_ref.shape[2]
    low = lambda j: grads_ref[:, j * width : (j + 1) * width].astype(jnp.bfloat16)
    part = dot(low(0), weight_ref[0], NT)
    for j in (1, 2):
        part = part + dot(low(j), weight_ref[j], NT)
    part_ref[...] = part
    normed = layer_norm(state_ref[...].astype(jnp.float32), 1.0, 0.0)[1]
    sums_ref[0:1] = jnp.sum(part * normed, axis=0, keepdims=True)
    sums_ref[1:2] = jnp.sum(part, axis=0, keepdims=True)
    bias_ref[...] = jnp.sum(grads_ref[...], axis=0, keepdims=True)


def project_back(grads, weight, states, after=()):
    rows, width = states.shape
    return local_call(
        project_back_kernel,
        (like((rows, width)), like((2, width)), like((1, grads.shape[1]))),
        (grads, weight, states),
        after,
        name="project_back",
    )


def last_kernel(count, part_ref, other_ref, state_ref, gain_ref, *refs):
    mids, results, (grad_ref, out_ref) = refs[:count], refs[count : 2 * count], refs[2 * count :]
    start = 0
    for mid, result in zip(mids, results):
        rows = slice(start, start + mid.shape[0])
        _, normed, inverse = layer_norm(state_ref[rows].astype(jnp.float32), 1.0, 0.0)
        grad_one = part_ref[rows] + other_ref[rows]
        grad_ref[rows] = (
            mid[...] + norm_back(grad_one, normed, inverse, gain_ref[...])
        ).astype(jnp.bfloat16)
        out_ref[rows] = result[...]
        start = rows.stop


def last_step(mids, part, other, states, gain, results, after=()):
    return local_call(
        lambda *refs: last_kernel(len(mids), *refs),
        (like(states.shape, jnp.bfloat16),) * 2,
        (part, other, states, gain, *mids, *results),
        after,
        name="input_grad",
    )


def outer_kernel(high, low, plans, bit_ref, *refs):
    count = sum(len(lefts) + rights for _, lefts, rights in plans)
    operands, (give_ref, keep_ref), scratch = refs[:count], refs[count : count + 2], refs[count + 2 :]
    rounded, full = list(scratch[:-1]), scratch[-1]
    operands = list(operands)
    for (first, last), lefts, rights in plans:
        left_refs = [operands.pop(0) for _ in lefts]
        offsets = [start for _, _, start in lefts]
        right_refs = [operands.pop(0) for _ in range(rights)]
        low_refs = [rounded.pop(0) for _ in lefts]

        @pl.when(pl.program_id(0) == first)
        def _():
            for out, left in zip(low_refs, zip(left_refs, offsets)):
                out[...] = left[0][:, left[1] : left[1] + out.shape[1]].astype(jnp.bfloat16)

        @pl.when((pl.program_id(0) >= first) & (pl.program_id(0) < last))
        def _():
            total = None
            for out, (index, rows, _) in zip(low_refs, lefts):
                product = dot(out[...], right_refs[index][rows].astype(jnp.bfloat16))
                total = product if total is None else total + product
            full[...] = total

    part_blocks(full, bit_ref[0], high, low, keep_ref, give_ref)


def outer_sum(bit, high, groups, after=(), tile=512):
    width = groups[0][0][0][0].shape[0]
    low = width // (2 * high)
    operands, specs, scratch, plans = [], [], [], []
    first = 0
    for lefts, rights, start, columns in groups:
        last = first + columns // tile
        places, index, row = [], 0, 0
        for v, offset, rows in lefts:
            operands.append(v)
            specs.append(pl.BlockSpec(v.shape, lambda i: (0, 0)))
            scratch.append(pltpu.VMEM((width, rows), jnp.bfloat16))
            if row == rights[index].shape[0]:
                index, row = index + 1, 0
            places.append((index, slice(row, row + rows), offset))
            row += rows
        for v in rights:
            operands.append(v)
            place = lambda i, s=start // tile, f=first, n=last - first: (
                0,
                s + jnp.clip(i - f, 0, n - 1),
            )
            specs.append(pl.BlockSpec((v.shape[0], tile), place))
        plans.append(((first, last), places, len(rights)))
        first = last

    def body(*refs):
        count = 1 + len(operands)
        outer_kernel(high, low, plans, *refs[:count], *refs[count + len(after) :])

    return pl.pallas_call(
        body,
        out_shape=(like((width // 2, first * tile)),) * 2,
        grid=(first,),
        in_specs=[pl.BlockSpec(memory_space=pltpu.SMEM)]
        + specs
        + [pl.BlockSpec(memory_space=pl.ANY)] * len(after),
        out_specs=(pl.BlockSpec((width // 2, tile), lambda i: (0, i)),) * 2,
        scratch_shapes=scratch + [pltpu.VMEM((width, tile), jnp.float32)],
        compiler_params=pltpu.CompilerParams(vmem_limit_bytes=VMEM_BYTES),
        cost_estimate=BRIEF,
        name="weight_grad",
    )(bit, *operands, *after)


def split_kernel(count, bit_ref, *refs):
    bit = bit_ref[0]
    keeps, cames, (give_out, keep_out) = refs[:count], refs[count : 2 * count], refs[2 * count :]
    start = 0
    for keep_ref, came_ref in zip(keeps, cames):
        columns = slice(start, start + keep_ref.shape[-1])
        keep_out[0, :, columns] = keep_ref[0, bit] + came_ref[0, bit]
        give_out[0, :, columns] = keep_ref[0, 1 - bit] + came_ref[0, 1 - bit]
        start = columns.stop


def add_split(bit, keeps, cames, high):
    rows = keeps[0].shape[0]
    low = rows // (2 * high)
    blocks = [v.reshape(high, 2, low, v.shape[1]) for v in (*keeps, *cames)]
    columns = sum(v.shape[1] for v in keeps)
    give, kept = pl.pallas_call(
        lambda *refs: split_kernel(len(keeps), *refs),
        out_shape=(like((high, low, columns)),) * 2,
        grid=(high,),
        in_specs=[pl.BlockSpec(memory_space=pltpu.SMEM)]
        + [pl.BlockSpec((1, *v.shape[1:]), lambda i: (i, 0, 0, 0)) for v in blocks],
        out_specs=(pl.BlockSpec((1, low, columns), lambda i: (i, 0, 0)),) * 2,
        compiler_params=pltpu.CompilerParams(vmem_limit_bytes=VMEM_BYTES),
        cost_estimate=BRIEF,
        name="add_split",
    )(bit, *blocks)
    return give.reshape(rows // 2, columns), kept.reshape(rows // 2, columns)


def finish_kernel(counts, *refs):
    total = sum(counts)
    pairs, outs = list(zip(refs[:total], refs[total : 2 * total])), refs[2 * total :]
    for count, out in zip(counts, outs):
        start = 0
        for _ in range(count):
            keep_ref, came_ref = pairs.pop(0)
            stop = start + keep_ref.shape[1]
            out[:, start:stop] = keep_ref[...] + came_ref[...]
            start = stop


def finish_all(results, after=()):
    return local_call(
        lambda *refs: finish_kernel([len(keeps) for keeps, _ in results], *refs),
        [like((one[0].shape[0], sum(v.shape[1] for v in one))) for one, _ in results],
        (*(v for one, _ in results for v in one), *(v for _, one in results for v in one)),
        after,
        name="finish",
    )


def pack_kernel(counts, valid_ref, *refs):
    ins, out = list(refs[:-1]), refs[-1]
    one, other, projected = ins[:3]
    rest = ins[3:]
    middles, ups, results = (
        rest[: counts],
        rest[counts : 2 * counts],
        rest[2 * counts :],
    )
    width = out.shape[1]
    total = lambda parts: sum(part[...] for part in parts[1:]) + parts[0][...]
    out[...] = jnp.zeros_like(out)
    out[0:2] = one[...] + other[...]
    local = projected.shape[1] // 3
    out[2:3, :local] = projected[:, :local]
    out[2:3, local : 2 * local] = projected[:, 2 * local :]
    out[3:6] = total(middles)
    up = total(ups)
    rows = up.shape[1] // width
    for row in range(rows):
        out[6 + row : 7 + row] = up[:, row * width : (row + 1) * width]
    result = total(results)
    out[6 + rows : 7 + rows] = result[0:1]
    out[7 + rows : 8 + rows] = result[1:2] * valid_ref[0]


def pack(valid, one, other, projected, middles, ups, results):
    width = one.shape[1]
    rows = -(-(8 + ups[0].shape[1] // width) // 8) * 8
    return local_call(
        lambda *refs: pack_kernel(len(middles), *refs),
        (like((rows, width)),),
        (valid, one, other, projected, *middles, *ups, *results),
        smem=1,
        name="pack",
    )[0]


def tie(value, *others):
    return lax.optimization_barrier((value, *others))[0]


def make_shards(mesh):
    groups = mesh.shape["dp"]
    bits = groups.bit_length() - 1
    assert groups == 1 << bits and mesh.shape["tensor"] == 2

    def swap_tensor(value):
        return lax.ppermute(value, "tensor", [(0, 1), (1, 0)])

    def swap_bit(value, bit):
        return lax.ppermute(value, "dp", [(i, i ^ (1 << bit)) for i in range(groups)])

    def sum_dp(value):
        for bit in range(bits):
            value = value + swap_bit(value, bit)
        return value

    def own_bit(bit):
        return ((lax.axis_index("dp") >> bit) & 1).astype(jnp.int32).reshape(1)

    class Scatter:
        def __init__(self, groups_of, order, after=(), tile=512):
            self.left = list(range(1, bits))[::-1]
            self.order = list(order)
            bit = self.order[0]
            self.give, self.keep = outer_sum(
                own_bit(bit), 1 << self.left.index(bit), groups_of, after, tile
            )
            self.keep, self.came = [self.keep], None

        def send(self):
            bit = self.order.pop(0)
            self.came = [swap_bit(self.give, bit)]
            self.left.remove(bit)
            self.give = None

        def join(self, other):
            self.keep = self.keep + other.keep
            self.came = self.came + other.came

        def fold(self):
            bit = self.order[0]
            self.give, keep = add_split(
                own_bit(bit), self.keep, self.came, 1 << self.left.index(bit)
            )
            self.keep, self.came = [keep], None

        def move(self):
            self.fold()
            self.send()

        def last(self):
            while self.order:
                self.move()
            return self

    def sync(scatters, *arrays):
        held = [(one.give, one.keep, one.came) for one in scatters]
        held, arrays = lax.optimization_barrier((held, arrays))
        for one, (give, keep, came) in zip(scatters, held):
            one.give, one.keep, one.came = give, keep, came
        return arrays

    def shards(
        images,
        teacher,
        image_mask,
        attn_gain,
        attn_shift,
        in_weight,
        in_bias,
        out_weight,
        out_bias,
        mlp_gain,
        mlp_shift,
        up_weight,
        up_bias,
        down_weight,
        down_bias,
    ):
        image_count, seq_len, width = images.shape
        row_count = image_count * seq_len
        local_width = in_weight.shape[2]
        scales_one = jnp.stack([attn_gain, attn_shift]).astype(jnp.float32)
        gain_one = scales_one[0:1]
        gain_two = mlp_gain.astype(jnp.float32)[None]
        shift_two = mlp_shift.astype(jnp.float32)[None]
        bias_out = out_bias.astype(jnp.float32)[None]
        bias_up = up_bias.astype(jnp.float32)[None]
        bias_down = down_bias.astype(jnp.float32)[None]
        weights_in = jnp.swapaxes(in_weight, 0, 1)
        chunks, start = [], 0
        for stop in (352, row_count):
            chunks.append(slice(start, stop))
            start = stop
        cut = chunks[0].stop
        part = width // groups
        core_bit = own_bit(0)
        low_first = tuple(range(1, bits))
        swap_core = lambda value: swap_bit(value, 0)

        quarter = local_width // 4
        dp_index = lax.axis_index("dp")
        piece = lax.dynamic_slice_in_dim(out_weight, (dp_index & 3) * quarter, quarter, axis=0)
        pieces = [swap_tensor(piece.astype(jnp.float32))]
        places = jnp.stack([(dp_index & 3) ^ way for way in (0, 2, 1, 3)]).astype(jnp.int32)

        states = images.reshape(row_count, width)
        targets = teacher.reshape(row_count, width)
        act_one, projected = enter(states, scales_one, weights_in, in_bias)
        *context, log_total = attend(projected, chunks[0].stop)
        context_other = [swap_tensor(one) for one in context]
        pieces.append(swap_bit(tie(pieces[0], log_total), 1))
        pieces += [swap_core(one) for one in pieces]

        valid = image_mask.astype(jnp.float32)[0]
        count = tie(jnp.full((8, 128), valid * seq_len, jnp.float32), log_total)
        count = count + swap_bit(count, 0)
        turned_one, given_one = turn_step(core_bit, act_one, part, (log_total,))

        middle, normed_two, inverse_two, turned_two, given_two, inner, slope, mlp_part = mlp_out = [
            [] for _ in range(8)
        ]
        count, turned_one, given_one, context, context_other[0], pieces = sync(
            [], count, turned_one, given_one, context, context_other[0], pieces
        )
        more = swap_bit(count, 1)

        def mlp_of(i):
            rows = chunks[i]
            step = mlp_step(
                rows,
                slice(0, rows.stop - rows.start),
                part,
                places,
                core_bit,
                states,
                context[i],
                context_other[i],
                out_weight,
                pieces,
                bias_out,
                gain_two,
                shift_two,
                up_weight,
                bias_up,
                down_weight,
            )
            for kept, one in zip(mlp_out, step):
                kept.append(one)

        mlp_of(0)
        mlp_part[0], given_two[0], inner[0], given_one, context, context_other[1], count, more = sync(
            [], mlp_part[0], given_two[0], inner[0], given_one, context, context_other[1], count, more
        )
        count = count + more
        mlp_other = [swap_tensor(mlp_part[0])]
        came_two, came_inner = [swap_core(given_two[0])], [swap_core(inner[0])]
        came_one = swap_core(given_one)
        more = swap_bit(count, 2)
        mlp_of(1)
        mlp_part[1], given_two[1], inner[1], came_two, came_inner, came_one, count, more = sync(
            [], mlp_part[1], given_two[1], inner[1], came_two, came_inner, came_one, count, more
        )
        count = count + more
        mlp_other.append(swap_tensor(mlp_part[1]))
        for bit in range(3, bits):
            count = count + swap_bit(count, bit)
        mlp_other[0], given_two[1], inner[1], count = sync(
            [], mlp_other[0], given_two[1], inner[1], count
        )
        count_all = count[:1, 0]
        scale = 2.0 * valid / count_all

        result, grad_result, grad_low, turned_low, given_low, result_sums = result_out = [
            [] for _ in range(6)
        ]
        grad_pre, two_part, up_sums = back_out = [[], [], []]
        two_other = []

        def result_of(i, after):
            step = result_step(
                chunks[i],
                part,
                scale,
                core_bit,
                middle[i],
                mlp_part[i],
                mlp_other[i],
                bias_down,
                targets,
                after,
            )
            for kept, one in zip(result_out, step):
                kept.append(one)

        def back_of(i, after):
            step = mlp_back(grad_low[i], slope[i], down_weight, up_weight, after)
            for kept, one in zip(back_out, step):
                kept.append(one)
            two_other.append(swap_tensor(two_part[i]))
            return (two_part[i],)

        grad_middle, turned_attn, given_attn, grad_context, middle_sums = middle_out = [
            [] for _ in range(5)
        ]

        def middle_of(i, earlier, after):
            step = middle_back(
                part,
                core_bit,
                two_part[i],
                two_other[i],
                grad_result[i],
                normed_two[i],
                inverse_two[i],
                gain_two,
                out_weight,
                earlier,
                after,
            )
            for kept, one in zip(middle_out, step):
                kept.append(one)
            return (grad_context[i],)

        def rows_of(values):
            return [(one, 0, rows.stop - rows.start) for one, rows in zip(values, chunks * 2)]

        half = up_weight.shape[1] // 2
        came_two.append(swap_core(given_two[1]))
        came_inner.append(swap_core(inner[1]))
        came_context = [swap_core(one) for one in context]
        result_of(0, ())
        back_of(0, ())
        came_two, came_inner, came_context, grad_pre[0], given_low[0], two_part[0] = sync(
            [], came_two, came_inner, came_context, grad_pre[0], given_low[0], two_part[0]
        )
        two_other = [swap_tensor(two_part[0])]
        came_low = [swap_core(given_low[0])]
        result_of(1, (two_part[0],))
        given_low[1], grad_low[1], slope[1] = sync([], given_low[1], grad_low[1], slope[1])

        came_low.append(swap_core(given_low[1]))
        (came_low,) = sync([], came_low)

        left, right = rows_of(turned_low + came_low), inner + came_inner
        first_units = 3 * half // 4
        down_b = Scatter([(left, right, 0, first_units)], low_first, (), first_units)
        grad_low[1], slope[1] = sync([down_b], grad_low[1], slope[1])

        down_b.send()
        back_of(1, ())
        down_d = Scatter(
            [(left, right, first_units, 2 * half - first_units)],
            low_first,
            (two_part[1],),
            first_units // 3,
        )
        two_part[1], grad_pre, two_other[0] = sync(
            [down_b, down_d], two_part[1], grad_pre, two_other[0]
        )

        two_other.append(swap_tensor(two_part[1]))
        down_d.send()
        came_pre = [swap_core(one) for one in grad_pre]
        down_b.move()
        middle_of(0, (), ())
        left, right = rows_of(turned_two + came_two), grad_pre + came_pre
        up_a = Scatter([(left, right, 0, half)], low_first, (grad_context[0],))
        up_b = Scatter([(left, right, half, half)], low_first, (up_a.give,))
        middle_of(1, (turned_attn[0], given_attn[0]), (up_b.give,))
        turned_attn[1], given, grad_context = sync(
            [down_b, down_d, up_a, up_b], turned_attn[1], given_attn[1], grad_context
        )

        up_a.send()
        down_b.move()
        down_d.move()
        grads = attend_back(projected, log_total, grad_context)
        grads, given = sync([down_b, down_d, up_a, up_b], grads, given)

        up_b.send()
        came_grads = swap_core(grads)
        came_attn = swap_core(given)
        up_a.move()
        down_d.move()
        one_part, one_sums, in_sums = project_back(grads, weights_in, states)
        left = [(turned_one, 0, row_count), (came_one, 0, row_count)]
        right = [grads, came_grads]
        in_a = Scatter([(left, right, 0, 2 * local_width)], low_first, (one_part,))
        first = swap_tensor(one_sums)
        one_part, one_sums, first, came_attn, came_grads = sync(
            [down_b, down_d, up_a, up_b, in_a], one_part, one_sums, first, came_attn, came_grads
        )
        in_b = Scatter(
            [(left, [grads, came_grads], 2 * local_width, local_width)], low_first
        )

        one_other = swap_tensor(one_part)
        in_a.send()
        up_a.move()
        up_b.move()
        starts = (0, lanes(chunks[0].stop))
        left = [
            (one, start, rows.stop - rows.start)
            for one in (turned_attn[1], came_attn)
            for start, rows in zip(starts, chunks)
        ]
        out_all = Scatter(
            [(left, [*context, *came_context], 0, local_width)], low_first, (in_b.give,)
        )
        full_down = finish_all(
            [(down_b.last().keep + down_d.last().keep, down_b.came + down_d.came)]
        )[0]
        small = pack(valid.reshape(1), one_sums, first, in_sums, middle_sums, up_sums, result_sums)
        small = small + swap_bit(small, 0)
        more = swap_bit(small, 2)
        small, more, full_down = sync([up_a, up_b, in_a, in_b, out_all], small, more, full_down)

        in_b.send()
        in_a.move()
        up_b.move()
        small = small + more
        (small,) = sync([up_a, up_b, in_a, in_b, out_all], small)

        out_all.send()
        in_b.move()
        in_a.move()
        more = swap_bit(small, 1)
        (full_up,) = finish_all(
            [(up_a.last().keep + up_b.last().keep, up_a.came + up_b.came)]
        )
        small, more, full_up = sync([in_a, in_b, out_all], small, more, full_up)

        out_all.move()
        in_b.move()
        small = small + more
        for bit in range(3, bits - 1):
            small = small + swap_bit(small, bit)
        more = swap_bit(small, bits - 1)
        grad_images, block_out = last_step(
            grad_middle, one_part, one_other, states, gain_one, result
        )
        small, more, grad_images, block_out = sync(
            [in_a, in_b, out_all], small, more, grad_images, block_out
        )
        small = small + more

        out_all.move()
        in_a.last(), in_b.last()
        (full_in,) = finish_all([(in_a.keep + in_b.keep, in_a.came + in_b.came)])
        (full_out,) = finish_all([(out_all.last().keep, out_all.came)])
        up_rows = up_bias.shape[0] // width
        small_up = small[6 : 6 + up_rows].reshape(-1)
        shape = (image_count, seq_len, width)
        return (
            block_out.reshape(shape),
            jnp.sum(small[7 + up_rows]) / count_all[0],
            grad_images.reshape(shape),
            small[0],
            small[1],
            full_in.reshape(-1, 3, local_width),
            small[2].reshape(2, local_width),
            full_out.T,
            small[3],
            small[4],
            small[5],
            full_up,
            small_up,
            full_down.T,
            small[6 + up_rows],
        )

    return shards


def solution(mesh):
    placed = (
        P("dp", None, None),
        P("dp", None, None),
        P("dp"),
        P(),
        P(),
        P(None, None, "tensor"),
        P(None, "tensor"),
        P("tensor", None),
        P(),
        P(),
        P(),
        P(None, "tensor"),
        P("tensor"),
        P("tensor", None),
        P(),
    )
    return jax.shard_map(
        make_shards(mesh),
        mesh=mesh,
        in_specs=placed,
        out_specs=(
            P("dp", None, None),
            P(),
            P("dp", None, None),
            P(),
            P(),
            P("dp", None, "tensor"),
            P(None, "tensor"),
            P("tensor", "dp"),
            P(),
            P(),
            P(),
            P("dp", "tensor"),
            P("tensor"),
            P("tensor", "dp"),
            P(),
        ),
        check_vma=False,
    )
```

```python
import jax
import jax.numpy as jnp
from jax import lax
from jax.experimental import pallas as pl
from jax.experimental.pallas import tpu as pltpu
from jax.sharding import PartitionSpec as P

HD = 64

epsilon = 1e-05
score_scale = 0.125
quick_rate = 1.702
log2_e = 1.4426950408889634
score_rate = score_scale * log2_e

NN = (((1,), (0,)), ((), ()))
NT = (((1,), (1,)), ((), ()))
VMEM_BYTES = 48 * 2**20
BRIEF = pl.CostEstimate(flops=1, bytes_accessed=1, transcendentals=0)


def dot(matrix_a, matrix_b, dims=NN):
    return lax.dot_general(matrix_a, matrix_b, dims, preferred_element_type=jnp.float32)


def layer_norm(hidden, scales, offset):
    centred = hidden - jnp.mean(hidden, axis=-1, keepdims=True)
    inverse = lax.rsqrt(jnp.mean(centred * centred, axis=-1, keepdims=True) + epsilon)
    normed = centred * inverse
    return (normed * scales + offset, normed, inverse)


def norm_back(grad_out, normed, inverse, scales):
    scaled = grad_out * scales
    centred = scaled - jnp.mean(scaled, axis=-1, keepdims=True)
    return (centred - normed * jnp.mean(scaled * normed, axis=-1, keepdims=True)) * inverse


def first_head(shape):
    return lax.broadcasted_iota(jnp.int32, shape, len(shape) - 1) < HD


def local_call(
    kernel, outs, ins, after=(), scratch=(), smem=0, name=None
):
    count = len(ins)

    def body(*refs):
        kernel(*refs[:count], *refs[count + len(after) :])

    return pl.pallas_call(
        body,
        out_shape=tuple(outs),
        in_specs=[pl.BlockSpec(memory_space=pltpu.SMEM)] * smem
        + [pl.BlockSpec(memory_space=pltpu.VMEM)] * (count - smem)
        + [pl.BlockSpec(memory_space=pl.ANY)] * len(after),
        out_specs=tuple(pl.BlockSpec(memory_space=pltpu.VMEM) for _ in outs),
        scratch_shapes=list(scratch),
        compiler_params=pltpu.CompilerParams(vmem_limit_bytes=VMEM_BYTES),
        cost_estimate=BRIEF,
        name=name,
    )(*ins, *after)


def part_blocks(source, bit, high, low, keep_ref, give_ref):
    for j in range(high):
        keep_ref[low * j : low * (j + 1)] = source[
            pl.ds(pl.multiple_of((2 * j + bit) * low, 8), low)
        ]
        give_ref[low * j : low * (j + 1)] = source[
            pl.ds(pl.multiple_of((2 * j + 1 - bit) * low, 8), low)
        ]


def lanes(rows):
    return -(-rows // 128) * 128


def turn(value, bit, part, scratch, keep_ref, give_ref):
    rows = value.shape[0]
    scratch[:, :rows] = jnp.transpose(value)
    if scratch.shape[1] > rows:
        scratch[:, rows:] = jnp.zeros((scratch.shape[0], scratch.shape[1] - rows), jnp.float32)
    part_blocks(scratch, bit, value.shape[1] // (2 * part), part, keep_ref, give_ref)


def like(shape, dtype=jnp.float32):
    return jax.ShapeDtypeStruct(shape, dtype)


def enter_kernel(state_ref, scales_ref, weight_ref, bias_ref, act_ref, out_ref):
    which = pl.program_id(0)

    @pl.when(which == 0)
    def _():
        act_ref[...] = layer_norm(
            state_ref[...].astype(jnp.float32), scales_ref[0:1], scales_ref[1:2]
        )[0].astype(jnp.bfloat16)

    biases = bias_ref[...].astype(jnp.float32)
    zero = jnp.zeros_like(biases[0:1])
    bias = jnp.where(which == 0, biases[0:1], jnp.where(which == 2, biases[1:2], zero))
    out_ref[0] = (dot(act_ref[...], weight_ref[0]) + bias).astype(jnp.bfloat16)


def enter(states, scales, weight, bias):
    rows, width = states.shape
    local = weight.shape[2]
    return pl.pallas_call(
        enter_kernel,
        out_shape=(
            like((rows, width), jnp.bfloat16),
            like((3, rows, local), jnp.bfloat16),
        ),
        grid=(3,),
        in_specs=[
            pl.BlockSpec((rows, width), lambda i: (0, 0)),
            pl.BlockSpec((2, width), lambda i: (0, 0)),
            pl.BlockSpec((1, width, local), lambda i: (i, 0, 0)),
            pl.BlockSpec((2, local), lambda i: (0, 0)),
        ],
        out_specs=(
            pl.BlockSpec((rows, width), lambda i: (0, 0)),
            pl.BlockSpec((1, rows, local), lambda i: (i, 0, 0)),
        ),
        compiler_params=pltpu.CompilerParams(vmem_limit_bytes=VMEM_BYTES),
        cost_estimate=BRIEF,
        name="norm_project",
    )(states, scales, weight, bias)


def attend_kernel(projected_ref, first_ref, second_ref, log_ref):
    _, seq_len, width = projected_ref.shape
    cut = first_ref.shape[0]
    low = first_head((seq_len, 2 * HD))
    zero = jnp.zeros((), jnp.bfloat16)
    for pair in range(width // (2 * HD)):
        start, stop = 2 * HD * pair, 2 * HD * (pair + 1)
        cols = slice(start, stop)
        query, key = projected_ref[0, :, cols], projected_ref[1, :, cols]
        value_t = jnp.transpose(projected_ref[2, :, cols])
        parts = []
        for half in range(2):
            one_key = jnp.where(low if half == 0 else ~low, key, zero)
            scores = dot(one_key, query, NT)
            top = jnp.max(scores, axis=0, keepdims=True)
            weights = jnp.exp2((scores - top) * score_rate)
            total = jnp.sum(weights, axis=0, keepdims=True)
            weights_low = (weights * (1.0 / total)).astype(jnp.bfloat16)
            parts.append(dot(value_t[HD * half : HD * (half + 1)], weights_low))
            head = 2 * pair + half
            log_ref[head : head + 1, :] = top * score_rate + jnp.log2(total)
        context = jnp.transpose(jnp.concatenate(parts, axis=0)).astype(jnp.bfloat16)
        context = context.astype(jnp.float32)
        first_ref[:, cols] = context[:cut]
        second_ref[:, cols] = context[cut:]


def attend(projected, cut, after=()):
    _, rows, width = projected.shape
    return local_call(
        attend_kernel,
        (like((cut, width)), like((rows - cut, width)), like((width // HD, rows))),
        (projected,),
        after,
        name="attend",
    )


def turn_step(bit, value, part, after=()):
    rows, width = value.shape
    half = like((width // 2, lanes(rows)))

    def kernel(bit_ref, value_ref, keep_ref, give_ref, scratch):
        turn(value_ref[...].astype(jnp.float32), bit_ref[0], part, scratch, keep_ref, give_ref)

    return local_call(
        kernel,
        (half, half),
        (bit, value),
        after,
        scratch=(pltpu.VMEM((width, lanes(rows)), jnp.float32),),
        smem=1,
        name="turn",
    )


def attend_back_kernel(projected_ref, log_ref, *refs):
    grad_refs, grads_ref = refs[:-1], refs[-1]
    _, seq_len, width = projected_ref.shape
    low = first_head((seq_len, 2 * HD))
    zero = jnp.zeros((), jnp.bfloat16)
    round_low = lambda v: v.astype(jnp.bfloat16).astype(jnp.float32)
    for pair in range(width // (2 * HD)):
        start, stop = 2 * HD * pair, 2 * HD * (pair + 1)
        cols = slice(start, stop)
        query, key, value = (projected_ref[j, :, cols] for j in range(3))
        grad = jnp.concatenate([one[:, cols] for one in grad_refs], axis=0)
        key_t = jnp.transpose(key)
        grad_query, grad_key, grad_value = [], [], []
        for half in range(2):
            kept = low if half == 0 else ~low
            head = 2 * pair + half
            scores = dot(jnp.where(kept, key, zero), query, NT)
            weights = jnp.exp2(scores * score_rate - log_ref[head : head + 1, :])
            grad_weights = dot(jnp.where(kept, value, zero), grad, NT)
            grad_value.append(dot(weights.astype(jnp.bfloat16), grad))
            row_sum = jnp.sum(grad_weights * weights, axis=0, keepdims=True)
            grad_scores = (weights * (grad_weights - row_sum)).astype(jnp.bfloat16)
            grad_key.append(dot(grad_scores, query))
            grad_query.append(dot(key_t[HD * half : HD * (half + 1)], grad_scores))
        grads_ref[:, start:stop] = round_low(
            jnp.transpose(jnp.concatenate(grad_query, axis=0)) * score_scale
        )
        grads_ref[:, width + start : width + stop] = round_low(
            jnp.where(low, grad_key[0], grad_key[1]) * score_scale
        )
        grads_ref[:, 2 * width + start : 2 * width + stop] = round_low(
            jnp.where(low, grad_value[0], grad_value[1])
        )


def attend_back(projected, log_total, grad_context, after=()):
    _, seq_len, width = projected.shape
    return local_call(
        attend_back_kernel,
        (like((seq_len, 3 * width)),),
        (projected, log_total, *grad_context),
        after,
        name="attend_back",
    )[0]


def mlp_kernel(
    rows, inside, part, places_ref, bit_ref, hidden_ref, context_ref, other_ref, weight_ref, *refs
):
    pieces, (bias_ref, gain_ref, shift_ref, up_ref, up_bias_ref, down_ref) = refs[:4], refs[4:10]
    middle_ref, normed_ref, inverse_ref, turned_ref, given_ref, inner_ref, slope_ref, part_ref = (
        refs[10:18]
    )
    weight_other, act_ref, scratch = refs[18:]

    @pl.when(pl.program_id(0) == 0)
    def _():
        block = pieces[0].shape[0]
        for i, piece in enumerate(pieces):
            start = pl.multiple_of(places_ref[i] * block, block)
            weight_other[pl.ds(start, block)] = piece[...].astype(jnp.bfloat16)
        branch = dot(context_ref[inside].astype(jnp.bfloat16), weight_ref[...]) + dot(
            other_ref[inside].astype(jnp.bfloat16), weight_other[...]
        )
        middle = hidden_ref[rows].astype(jnp.float32) + branch + bias_ref[...]
        normed_out, normed, inverse = layer_norm(middle, gain_ref[...], shift_ref[...])
        middle_ref[...] = middle
        normed_ref[...] = normed
        inverse_ref[...] = inverse
        act = normed_out.astype(jnp.bfloat16)
        act_ref[...] = act
        turn(act.astype(jnp.float32), bit_ref[0], part, scratch, turned_ref, given_ref)

    pre_act = dot(act_ref[...], up_ref[...]) + up_bias_ref[...]
    sigma = 0.5 + 0.5 * jnp.tanh((0.5 * quick_rate) * pre_act)
    inner = (pre_act * sigma).astype(jnp.bfloat16)
    inner_ref[...] = inner.astype(jnp.float32)
    slope_ref[...] = sigma + pre_act * quick_rate * sigma * (1.0 - sigma)
    product = dot(inner, down_ref[...])

    @pl.when(pl.program_id(0) == 0)
    def _():
        part_ref[...] = product

    @pl.when(pl.program_id(0) > 0)
    def _():
        part_ref[...] += product


def mlp_step(
    rows, inside, part, places, bit, hidden, context, other, weight, pieces, bias, gain, shift,
    up, up_bias, down, after=(), tile=1024,
):
    width = hidden.shape[1]
    count = rows.stop - rows.start
    units = up.shape[1]
    ins = (places, bit, hidden, context, other, weight, *pieces, bias, gain, shift)

    def body(*refs):
        mlp_kernel(rows, inside, part, *refs[: len(ins) + 3], *refs[len(ins) + 3 + len(after) :])

    whole = lambda shape: pl.BlockSpec(shape, lambda i: (0,) * len(shape))
    half = (width // 2, lanes(count))
    return pl.pallas_call(
        body,
        out_shape=(
            like((count, width)),
            like((count, width)),
            like((count, 1)),
            like(half),
            like(half),
            like((count, units)),
            like((count, units)),
            like((count, width)),
        ),
        grid=(units // tile,),
        in_specs=[pl.BlockSpec(memory_space=pltpu.SMEM)] * 2
        + [whole(v.shape) for v in ins[2:]]
        + [
            pl.BlockSpec((width, tile), lambda i: (0, i)),
            pl.BlockSpec((1, tile), lambda i: (0, i)),
            pl.BlockSpec((tile, width), lambda i: (i, 0)),
        ]
        + [pl.BlockSpec(memory_space=pl.ANY)] * len(after),
        out_specs=(
            whole((count, width)),
            whole((count, width)),
            whole((count, 1)),
            whole(half),
            whole(half),
            pl.BlockSpec((count, tile), lambda i: (0, i)),
            pl.BlockSpec((count, tile), lambda i: (0, i)),
            whole((count, width)),
        ),
        scratch_shapes=[
            pltpu.VMEM(weight.shape, jnp.bfloat16),
            pltpu.VMEM((count, width), jnp.bfloat16),
            pltpu.VMEM((width, lanes(count)), jnp.float32),
        ],
        compiler_params=pltpu.CompilerParams(vmem_limit_bytes=VMEM_BYTES),
        cost_estimate=BRIEF,
        name="mlp",
    )(*ins, up, up_bias, down, *after)


def result_kernel(
    rows, part, scale_ref, bit_ref, middle_ref, part_ref, other_ref, bias_ref, target_ref, *outs
):
    out_ref, grad_ref, low_ref, turned_ref, given_ref, sums_ref, scratch = outs
    result = middle_ref[...] + (part_ref[...] + other_ref[...]) + bias_ref[...]
    error = result - target_ref[rows].astype(jnp.float32)
    grad = error * scale_ref[0]
    low = grad.astype(jnp.bfloat16)
    out_ref[...] = result.astype(jnp.bfloat16)
    grad_ref[...] = grad
    low_ref[...] = low
    turn(low.astype(jnp.float32), bit_ref[0], part, scratch, turned_ref, given_ref)
    sums_ref[0:1] = jnp.sum(grad, axis=0, keepdims=True)
    sums_ref[1:2] = jnp.sum(error * error, axis=0, keepdims=True)


def result_step(rows, row_part, scale, bit, middle, part, other, bias, target, after=()):
    count, width = middle.shape
    half = like((width // 2, lanes(count)))
    return local_call(
        lambda *refs: result_kernel(rows, row_part, *refs),
        (
            like((count, width), jnp.bfloat16),
            like((count, width)),
            like((count, width), jnp.bfloat16),
            half,
            half,
            like((2, width)),
        ),
        (scale, bit, middle, part, other, bias, target),
        after,
        scratch=(pltpu.VMEM((width, lanes(count)), jnp.float32),),
        smem=2,
        name="result_error",
    )


def mlp_back_kernel(low_ref, slope_ref, down_ref, up_ref, pre_ref, two_ref, sums_ref):
    pre = (dot(low_ref[...], down_ref[...], NT) * slope_ref[...]).astype(jnp.bfloat16)
    pre_ref[...] = pre.astype(jnp.float32)
    sums_ref[...] = jnp.sum(pre.astype(jnp.float32), axis=0, keepdims=True)
    two = dot(pre, up_ref[...], NT)

    @pl.when(pl.program_id(0) == 0)
    def _():
        two_ref[...] = two

    @pl.when(pl.program_id(0) > 0)
    def _():
        two_ref[...] += two


def mlp_back(low, slope, down, up, after=(), tile=512):
    count, width = low.shape
    units = up.shape[1]

    def body(*refs):
        mlp_back_kernel(*refs[:4], *refs[4 + len(after) :])

    return pl.pallas_call(
        body,
        out_shape=(
            like((count, units)),
            like((count, width)),
            like((1, units)),
        ),
        grid=(units // tile,),
        in_specs=[
            pl.BlockSpec((count, width), lambda i: (0, 0)),
            pl.BlockSpec((count, tile), lambda i: (0, i)),
            pl.BlockSpec((tile, width), lambda i: (i, 0)),
            pl.BlockSpec((width, tile), lambda i: (0, i)),
        ]
        + [pl.BlockSpec(memory_space=pl.ANY)] * len(after),
        out_specs=(
            pl.BlockSpec((count, tile), lambda i: (0, i)),
            pl.BlockSpec((count, width), lambda i: (0, 0)),
            pl.BlockSpec((1, tile), lambda i: (0, i)),
        ),
        compiler_params=pltpu.CompilerParams(vmem_limit_bytes=VMEM_BYTES),
        cost_estimate=BRIEF,
        name="mlp_back",
    )(low, slope, down, up, *after)


def middle_back_kernel(
    row_part, before, bit_ref, part_ref, other_ref, grad_ref, normed_ref, inverse_ref, gain_ref,
    weight_ref, *refs
):
    earlier, outs = refs[: 2 * before], refs[2 * before :]
    mid_ref, turned_ref, given_ref, context_ref, sums_ref, scratch = outs
    grad_two = part_ref[...] + other_ref[...]
    normed = normed_ref[...]
    mid = grad_ref[...] + norm_back(grad_two, normed, inverse_ref[...], gain_ref[...])
    low = mid.astype(jnp.bfloat16)
    mid_ref[...] = mid
    context_ref[...] = dot(low, weight_ref[...], NT).astype(jnp.bfloat16)
    rows = low.shape[0]
    start = turned_ref.shape[1] - lanes(rows)
    if before:
        turned_ref[:, :start] = earlier[0][...]
        given_ref[:, :start] = earlier[1][...]
    turn(
        low.astype(jnp.float32),
        bit_ref[0],
        row_part,
        scratch,
        turned_ref.at[:, start:],
        given_ref.at[:, start:],
    )
    sums_ref[0:1] = jnp.sum(mid, axis=0, keepdims=True)
    sums_ref[1:2] = jnp.sum(grad_two * normed, axis=0, keepdims=True)
    sums_ref[2:3] = jnp.sum(grad_two, axis=0, keepdims=True)


def middle_back(
    row_part, bit, part, other, grad, normed, inverse, gain, weight, earlier=(), after=()
):
    count, width = grad.shape
    start = earlier[0].shape[1] if earlier else 0
    half = like((width // 2, start + lanes(count)))
    return local_call(
        lambda *refs: middle_back_kernel(row_part, len(earlier) // 2, *refs),
        (
            like((count, width)),
            half,
            half,
            like((count, weight.shape[0]), jnp.bfloat16),
            like((3, width)),
        ),
        (bit, part, other, grad, normed, inverse, gain, weight, *earlier),
        after,
        scratch=(pltpu.VMEM((width, lanes(count)), jnp.float32),),
        smem=1,
        name="middle_back",
    )


def project_back_kernel(grads_ref, weight_ref, state_ref, part_ref, sums_ref, bias_ref):
    width = weight_ref.shape[2]
    low = lambda j: grads_ref[:, j * width : (j + 1) * width].astype(jnp.bfloat16)
    part = dot(low(0), weight_ref[0], NT)
    for j in (1, 2):
        part = part + dot(low(j), weight_ref[j], NT)
    part_ref[...] = part
    normed = layer_norm(state_ref[...].astype(jnp.float32), 1.0, 0.0)[1]
    sums_ref[0:1] = jnp.sum(part * normed, axis=0, keepdims=True)
    sums_ref[1:2] = jnp.sum(part, axis=0, keepdims=True)
    bias_ref[...] = jnp.sum(grads_ref[...], axis=0, keepdims=True)


def project_back(grads, weight, states, after=()):
    rows, width = states.shape
    return local_call(
        project_back_kernel,
        (like((rows, width)), like((2, width)), like((1, grads.shape[1]))),
        (grads, weight, states),
        after,
        name="project_back",
    )


def last_kernel(count, part_ref, other_ref, state_ref, gain_ref, *refs):
    mids, results, (grad_ref, out_ref) = refs[:count], refs[count : 2 * count], refs[2 * count :]
    start = 0
    for mid, result in zip(mids, results):
        rows = slice(start, start + mid.shape[0])
        _, normed, inverse = layer_norm(state_ref[rows].astype(jnp.float32), 1.0, 0.0)
        grad_one = part_ref[rows] + other_ref[rows]
        grad_ref[rows] = (
            mid[...] + norm_back(grad_one, normed, inverse, gain_ref[...])
        ).astype(jnp.bfloat16)
        out_ref[rows] = result[...]
        start = rows.stop


def last_step(mids, part, other, states, gain, results, after=()):
    return local_call(
        lambda *refs: last_kernel(len(mids), *refs),
        (like(states.shape, jnp.bfloat16),) * 2,
        (part, other, states, gain, *mids, *results),
        after,
        name="input_grad",
    )


def outer_kernel(high, low, plans, bit_ref, *refs):
    count = sum(len(lefts) + rights for _, lefts, rights in plans)
    operands, (give_ref, keep_ref), scratch = refs[:count], refs[count : count + 2], refs[count + 2 :]
    rounded, full = list(scratch[:-1]), scratch[-1]
    operands = list(operands)
    for (first, last), lefts, rights in plans:
        left_refs = [operands.pop(0) for _ in lefts]
        offsets = [start for _, _, start in lefts]
        right_refs = [operands.pop(0) for _ in range(rights)]
        low_refs = [rounded.pop(0) for _ in lefts]

        @pl.when(pl.program_id(0) == first)
        def _():
            for out, left in zip(low_refs, zip(left_refs, offsets)):
                out[...] = left[0][:, left[1] : left[1] + out.shape[1]].astype(jnp.bfloat16)

        @pl.when((pl.program_id(0) >= first) & (pl.program_id(0) < last))
        def _():
            total = None
            for out, (index, rows, _) in zip(low_refs, lefts):
                product = dot(out[...], right_refs[index][rows].astype(jnp.bfloat16))
                total = product if total is None else total + product
            full[...] = total

    part_blocks(full, bit_ref[0], high, low, keep_ref, give_ref)


def outer_sum(bit, high, groups, after=(), tile=512):
    width = groups[0][0][0][0].shape[0]
    low = width // (2 * high)
    operands, specs, scratch, plans = [], [], [], []
    first = 0
    for lefts, rights, start, columns in groups:
        last = first + columns // tile
        places, index, row = [], 0, 0
        for v, offset, rows in lefts:
            operands.append(v)
            specs.append(pl.BlockSpec(v.shape, lambda i: (0, 0)))
            scratch.append(pltpu.VMEM((width, rows), jnp.bfloat16))
            if row == rights[index].shape[0]:
                index, row = index + 1, 0
            places.append((index, slice(row, row + rows), offset))
            row += rows
        for v in rights:
            operands.append(v)
            place = lambda i, s=start // tile, f=first, n=last - first: (
                0,
                s + jnp.clip(i - f, 0, n - 1),
            )
            specs.append(pl.BlockSpec((v.shape[0], tile), place))
        plans.append(((first, last), places, len(rights)))
        first = last

    def body(*refs):
        count = 1 + len(operands)
        outer_kernel(high, low, plans, *refs[:count], *refs[count + len(after) :])

    return pl.pallas_call(
        body,
        out_shape=(like((width // 2, first * tile)),) * 2,
        grid=(first,),
        in_specs=[pl.BlockSpec(memory_space=pltpu.SMEM)]
        + specs
        + [pl.BlockSpec(memory_space=pl.ANY)] * len(after),
        out_specs=(pl.BlockSpec((width // 2, tile), lambda i: (0, i)),) * 2,
        scratch_shapes=scratch + [pltpu.VMEM((width, tile), jnp.float32)],
        compiler_params=pltpu.CompilerParams(vmem_limit_bytes=VMEM_BYTES),
        cost_estimate=BRIEF,
        name="weight_grad",
    )(bit, *operands, *after)


def split_kernel(count, bit_ref, *refs):
    bit = bit_ref[0]
    keeps, cames, (give_out, keep_out) = refs[:count], refs[count : 2 * count], refs[2 * count :]
    start = 0
    for keep_ref, came_ref in zip(keeps, cames):
        columns = slice(start, start + keep_ref.shape[-1])
        keep_out[0, :, columns] = keep_ref[0, bit] + came_ref[0, bit]
        give_out[0, :, columns] = keep_ref[0, 1 - bit] + came_ref[0, 1 - bit]
        start = columns.stop


def add_split(bit, keeps, cames, high):
    rows = keeps[0].shape[0]
    low = rows // (2 * high)
    blocks = [v.reshape(high, 2, low, v.shape[1]) for v in (*keeps, *cames)]
    columns = sum(v.shape[1] for v in keeps)
    give, kept = pl.pallas_call(
        lambda *refs: split_kernel(len(keeps), *refs),
        out_shape=(like((high, low, columns)),) * 2,
        grid=(high,),
        in_specs=[pl.BlockSpec(memory_space=pltpu.SMEM)]
        + [pl.BlockSpec((1, *v.shape[1:]), lambda i: (i, 0, 0, 0)) for v in blocks],
        out_specs=(pl.BlockSpec((1, low, columns), lambda i: (i, 0, 0)),) * 2,
        compiler_params=pltpu.CompilerParams(vmem_limit_bytes=20 * 2**20),
        cost_estimate=BRIEF,
        name="add_split",
    )(bit, *blocks)
    return give.reshape(rows // 2, columns), kept.reshape(rows // 2, columns)


def finish_kernel(counts, *refs):
    total = sum(counts)
    pairs, outs = list(zip(refs[:total], refs[total : 2 * total])), refs[2 * total :]
    for count, out in zip(counts, outs):
        start = 0
        for _ in range(count):
            keep_ref, came_ref = pairs.pop(0)
            stop = start + keep_ref.shape[1]
            out[:, start:stop] = keep_ref[...] + came_ref[...]
            start = stop


def finish_all(results, after=()):
    return local_call(
        lambda *refs: finish_kernel([len(keeps) for keeps, _ in results], *refs),
        [like((one[0].shape[0], sum(v.shape[1] for v in one))) for one, _ in results],
        (*(v for one, _ in results for v in one), *(v for _, one in results for v in one)),
        after,
        name="finish",
    )


def pack_kernel(counts, valid_ref, *refs):
    ins, out = list(refs[:-1]), refs[-1]
    one, other, projected = ins[:3]
    rest = ins[3:]
    middles, ups, results = (
        rest[: counts],
        rest[counts : 2 * counts],
        rest[2 * counts :],
    )
    width = out.shape[1]
    total = lambda parts: sum(part[...] for part in parts[1:]) + parts[0][...]
    out[...] = jnp.zeros_like(out)
    out[0:2] = one[...] + other[...]
    local = projected.shape[1] // 3
    out[2:3, :local] = projected[:, :local]
    out[2:3, local : 2 * local] = projected[:, 2 * local :]
    out[3:6] = total(middles)
    up = total(ups)
    rows = up.shape[1] // width
    for row in range(rows):
        out[6 + row : 7 + row] = up[:, row * width : (row + 1) * width]
    result = total(results)
    out[6 + rows : 7 + rows] = result[0:1]
    out[7 + rows : 8 + rows] = result[1:2] * valid_ref[0]


def pack(valid, one, other, projected, middles, ups, results):
    width = one.shape[1]
    rows = -(-(8 + ups[0].shape[1] // width) // 8) * 8
    return local_call(
        lambda *refs: pack_kernel(len(middles), *refs),
        (like((rows, width)),),
        (valid, one, other, projected, *middles, *ups, *results),
        smem=1,
        name="pack",
    )[0]


def tie(value, *others):
    return lax.optimization_barrier((value, *others))[0]


def make_shards(mesh):
    groups = mesh.shape["dp"]
    bits = groups.bit_length() - 1
    assert groups == 1 << bits and mesh.shape["tensor"] == 2

    def swap_tensor(value):
        return lax.ppermute(value, "tensor", [(0, 1), (1, 0)])

    def swap_bit(value, bit):
        return lax.ppermute(value, "dp", [(i, i ^ (1 << bit)) for i in range(groups)])

    def sum_dp(value):
        for bit in range(bits):
            value = value + swap_bit(value, bit)
        return value

    def own_bit(bit):
        return ((lax.axis_index("dp") >> bit) & 1).astype(jnp.int32).reshape(1)

    class Scatter:
        def __init__(self, groups_of, order, after=(), tile=512):
            self.left = list(range(1, bits))[::-1]
            self.order = list(order)
            bit = self.order[0]
            self.give, self.keep = outer_sum(
                own_bit(bit), 1 << self.left.index(bit), groups_of, after, tile
            )
            self.keep, self.came = [self.keep], None

        def send(self):
            bit = self.order.pop(0)
            self.came = [swap_bit(self.give, bit)]
            self.left.remove(bit)
            self.give = None

        def join(self, other):
            self.keep = self.keep + other.keep
            self.came = self.came + other.came

        def fold(self):
            bit = self.order[0]
            self.give, keep = add_split(
                own_bit(bit), self.keep, self.came, 1 << self.left.index(bit)
            )
            self.keep, self.came = [keep], None

        def move(self):
            self.fold()
            self.send()

        def last(self):
            while self.order:
                self.move()
            return self

    def sync(scatters, *arrays):
        held = [(one.give, one.keep, one.came) for one in scatters]
        held, arrays = lax.optimization_barrier((held, arrays))
        for one, (give, keep, came) in zip(scatters, held):
            one.give, one.keep, one.came = give, keep, came
        return arrays

    def shards(
        images,
        teacher,
        image_mask,
        attn_gain,
        attn_shift,
        in_weight,
        in_bias,
        out_weight,
        out_bias,
        mlp_gain,
        mlp_shift,
        up_weight,
        up_bias,
        down_weight,
        down_bias,
    ):
        image_count, seq_len, width = images.shape
        row_count = image_count * seq_len
        local_width = in_weight.shape[2]
        scales_one = jnp.stack([attn_gain, attn_shift]).astype(jnp.float32)
        gain_one = scales_one[0:1]
        gain_two = mlp_gain.astype(jnp.float32)[None]
        shift_two = mlp_shift.astype(jnp.float32)[None]
        bias_out = out_bias.astype(jnp.float32)[None]
        bias_up = up_bias.astype(jnp.float32)[None]
        bias_down = down_bias.astype(jnp.float32)[None]
        weights_in = jnp.swapaxes(in_weight, 0, 1)
        chunks, start = [], 0
        for stop in (336, row_count):
            chunks.append(slice(start, stop))
            start = stop
        cut = chunks[0].stop
        part = width // groups
        core_bit = own_bit(0)
        low_first = tuple(range(1, bits))
        swap_core = lambda value: swap_bit(value, 0)

        quarter = local_width // 4
        dp_index = lax.axis_index("dp")
        piece = lax.dynamic_slice_in_dim(out_weight, (dp_index & 3) * quarter, quarter, axis=0)
        pieces = [swap_tensor(piece.astype(jnp.float32))]
        places = jnp.stack([(dp_index & 3) ^ way for way in (0, 2, 1, 3)]).astype(jnp.int32)

        states = images.reshape(row_count, width)
        targets = teacher.reshape(row_count, width)
        act_one, projected = enter(states, scales_one, weights_in, in_bias)
        *context, log_total = attend(projected, chunks[0].stop)
        context_other = [swap_tensor(one) for one in context]
        pieces.append(swap_bit(tie(pieces[0], log_total), 1))
        pieces += [swap_core(one) for one in pieces]

        valid = image_mask.astype(jnp.float32)[0]
        count = tie(jnp.full((8, 128), valid * seq_len, jnp.float32), log_total)
        count = count + swap_bit(count, 0)
        turned_one, given_one = turn_step(core_bit, act_one, part, (log_total,))

        middle, normed_two, inverse_two, turned_two, given_two, inner, slope, mlp_part = mlp_out = [
            [] for _ in range(8)
        ]
        count, turned_one, given_one, context, context_other[0], pieces = sync(
            [], count, turned_one, given_one, context, context_other[0], pieces
        )
        more = swap_bit(count, 1)

        def mlp_of(i):
            rows = chunks[i]
            step = mlp_step(
                rows,
                slice(0, rows.stop - rows.start),
                part,
                places,
                core_bit,
                states,
                context[i],
                context_other[i],
                out_weight,
                pieces,
                bias_out,
                gain_two,
                shift_two,
                up_weight,
                bias_up,
                down_weight,
            )
            for kept, one in zip(mlp_out, step):
                kept.append(one)

        mlp_of(0)
        mlp_part[0], given_two[0], inner[0], given_one, context, context_other[1], count, more = sync(
            [], mlp_part[0], given_two[0], inner[0], given_one, context, context_other[1], count, more
        )
        count = count + more
        mlp_other = [swap_tensor(mlp_part[0])]
        came_two, came_inner = [swap_core(given_two[0])], [swap_core(inner[0])]
        came_one = swap_core(given_one)
        more = swap_bit(count, 2)
        mlp_of(1)
        mlp_part[1], given_two[1], inner[1], came_two, came_inner, came_one, count, more = sync(
            [], mlp_part[1], given_two[1], inner[1], came_two, came_inner, came_one, count, more
        )
        count = count + more
        mlp_other.append(swap_tensor(mlp_part[1]))
        for bit in range(3, bits):
            count = count + swap_bit(count, bit)
        mlp_other[0], given_two[1], inner[1], count = sync(
            [], mlp_other[0], given_two[1], inner[1], count
        )
        count_all = count[:1, 0]
        scale = 2.0 * valid / count_all

        result, grad_result, grad_low, turned_low, given_low, result_sums = result_out = [
            [] for _ in range(6)
        ]
        grad_pre, two_part, up_sums = back_out = [[], [], []]
        two_other = []

        def result_of(i, after):
            step = result_step(
                chunks[i],
                part,
                scale,
                core_bit,
                middle[i],
                mlp_part[i],
                mlp_other[i],
                bias_down,
                targets,
                after,
            )
            for kept, one in zip(result_out, step):
                kept.append(one)

        def back_of(i, after):
            step = mlp_back(grad_low[i], slope[i], down_weight, up_weight, after)
            for kept, one in zip(back_out, step):
                kept.append(one)
            two_other.append(swap_tensor(two_part[i]))
            return (two_part[i],)

        grad_middle, turned_attn, given_attn, grad_context, middle_sums = middle_out = [
            [] for _ in range(5)
        ]

        def middle_of(i, earlier, after):
            step = middle_back(
                part,
                core_bit,
                two_part[i],
                two_other[i],
                grad_result[i],
                normed_two[i],
                inverse_two[i],
                gain_two,
                out_weight,
                earlier,
                after,
            )
            for kept, one in zip(middle_out, step):
                kept.append(one)
            return (grad_context[i],)

        def rows_of(values):
            return [(one, 0, rows.stop - rows.start) for one, rows in zip(values, chunks * 2)]

        half = up_weight.shape[1] // 2
        came_two.append(swap_core(given_two[1]))
        came_inner.append(swap_core(inner[1]))
        came_context = [swap_core(one) for one in context]
        result_of(0, ())
        back_of(0, ())
        came_two, came_inner, came_context, grad_pre[0], given_low[0], two_part[0] = sync(
            [], came_two, came_inner, came_context, grad_pre[0], given_low[0], two_part[0]
        )
        two_other = [swap_tensor(two_part[0])]
        came_low = [swap_core(given_low[0])]
        result_of(1, (two_part[0],))
        given_low[1], grad_low[1], slope[1] = sync([], given_low[1], grad_low[1], slope[1])

        came_low.append(swap_core(given_low[1]))
        (came_low,) = sync([], came_low)

        left, right = rows_of(turned_low + came_low), inner + came_inner
        first_units = 3 * half // 4
        down_b = Scatter([(left, right, 0, first_units)], low_first, (), first_units)
        grad_low[1], slope[1] = sync([down_b], grad_low[1], slope[1])

        down_b.send()
        back_of(1, ())
        down_d = Scatter(
            [(left, right, first_units, 2 * half - first_units)],
            low_first,
            (two_part[1],),
            first_units // 3,
        )
        two_part[1], grad_pre, two_other[0] = sync(
            [down_b, down_d], two_part[1], grad_pre, two_other[0]
        )

        two_other.append(swap_tensor(two_part[1]))
        down_d.send()
        came_pre = [swap_core(one) for one in grad_pre]
        down_b.move()
        middle_of(0, (), ())
        left, right = rows_of(turned_two + came_two), grad_pre + came_pre
        up_a = Scatter([(left, right, 0, half)], low_first, (grad_context[0],))
        up_b = Scatter([(left, right, half, half)], low_first, (up_a.give,))
        middle_of(1, (turned_attn[0], given_attn[0]), (up_b.give,))
        turned_attn[1], given, grad_context = sync(
            [down_b, down_d, up_a, up_b], turned_attn[1], given_attn[1], grad_context
        )

        up_a.send()
        down_b.move()
        down_d.move()
        grads = attend_back(projected, log_total, grad_context)
        grads, given = sync([down_b, down_d, up_a, up_b], grads, given)

        up_b.send()
        came_grads = swap_core(grads)
        came_attn = swap_core(given)
        up_a.move()
        down_d.move()
        one_part, one_sums, in_sums = project_back(grads, weights_in, states)
        left = [(turned_one, 0, row_count), (came_one, 0, row_count)]
        right = [grads, came_grads]
        in_a = Scatter([(left, right, 0, 2 * local_width)], low_first, (one_part,))
        first = swap_tensor(one_sums)
        one_part, one_sums, first, came_attn, came_grads = sync(
            [down_b, down_d, up_a, up_b, in_a], one_part, one_sums, first, came_attn, came_grads
        )
        in_b = Scatter(
            [(left, [grads, came_grads], 2 * local_width, local_width)], low_first
        )

        one_other = swap_tensor(one_part)
        in_a.send()
        up_a.move()
        up_b.move()
        starts = (0, lanes(chunks[0].stop))
        left = [
            (one, start, rows.stop - rows.start)
            for one in (turned_attn[1], came_attn)
            for start, rows in zip(starts, chunks)
        ]
        out_all = Scatter(
            [(left, [*context, *came_context], 0, local_width)], low_first, (in_b.give,)
        )
        full_down = finish_all(
            [(down_b.last().keep + down_d.last().keep, down_b.came + down_d.came)]
        )[0]
        small = pack(valid.reshape(1), one_sums, first, in_sums, middle_sums, up_sums, result_sums)
        small = small + swap_bit(small, 0)
        more = swap_bit(small, 2)
        small, more, full_down = sync([up_a, up_b, in_a, in_b, out_all], small, more, full_down)

        in_b.send()
        in_a.move()
        up_b.move()
        small = small + more
        (small,) = sync([up_a, up_b, in_a, in_b, out_all], small)

        out_all.send()
        in_b.move()
        in_a.move()
        more = swap_bit(small, 1)
        (full_up,) = finish_all(
            [(up_a.last().keep + up_b.last().keep, up_a.came + up_b.came)]
        )
        small, more, full_up = sync([in_a, in_b, out_all], small, more, full_up)

        out_all.move()
        in_b.move()
        small = small + more
        for bit in range(3, bits - 1):
            small = small + swap_bit(small, bit)
        more = swap_bit(small, bits - 1)
        grad_images, block_out = last_step(
            grad_middle, one_part, one_other, states, gain_one, result
        )
        small, more, grad_images, block_out = sync(
            [in_a, in_b, out_all], small, more, grad_images, block_out
        )
        small = small + more

        out_all.move()
        in_a.last(), in_b.last()
        (full_in,) = finish_all([(in_a.keep + in_b.keep, in_a.came + in_b.came)])
        (full_out,) = finish_all([(out_all.last().keep, out_all.came)])
        up_rows = up_bias.shape[0] // width
        small_up = small[6 : 6 + up_rows].reshape(-1)
        shape = (image_count, seq_len, width)
        return (
            block_out.reshape(shape),
            jnp.sum(small[7 + up_rows]) / count_all[0],
            grad_images.reshape(shape),
            small[0],
            small[1],
            full_in.reshape(-1, 3, local_width),
            small[2].reshape(2, local_width),
            full_out.T,
            small[3],
            small[4],
            small[5],
            full_up,
            small_up,
            full_down.T,
            small[6 + up_rows],
        )

    return shards


def solution(mesh):
    placed = (
        P("dp", None, None),
        P("dp", None, None),
        P("dp"),
        P(),
        P(),
        P(None, None, "tensor"),
        P(None, "tensor"),
        P("tensor", None),
        P(),
        P(),
        P(),
        P(None, "tensor"),
        P("tensor"),
        P("tensor", None),
        P(),
    )
    return jax.shard_map(
        make_shards(mesh),
        mesh=mesh,
        in_specs=placed,
        out_specs=(
            P("dp", None, None),
            P(),
            P("dp", None, None),
            P(),
            P(),
            P("dp", None, "tensor"),
            P(None, "tensor"),
            P("tensor", "dp"),
            P(),
            P(),
            P(),
            P("dp", "tensor"),
            P("tensor"),
            P("tensor", "dp"),
            P(),
        ),
        check_vma=False,
    )
```

```python
import jax
import jax.numpy as jnp
from jax import lax
from jax.experimental import pallas as pl
from jax.experimental.pallas import tpu as pltpu
from jax.sharding import PartitionSpec as P

HD = 64

epsilon = 1e-05
score_scale = 0.125
quick_rate = 1.702
log2_e = 1.4426950408889634
score_rate = score_scale * log2_e

NN = (((1,), (0,)), ((), ()))
NT = (((1,), (1,)), ((), ()))
VMEM_BYTES = 48 * 2**20
BRIEF = pl.CostEstimate(flops=1, bytes_accessed=1, transcendentals=0)


def dot(matrix_a, matrix_b, dims=NN):
    return lax.dot_general(matrix_a, matrix_b, dims, preferred_element_type=jnp.float32)


def layer_norm(hidden, scales, offset):
    centred = hidden - jnp.mean(hidden, axis=-1, keepdims=True)
    inverse = lax.rsqrt(jnp.mean(centred * centred, axis=-1, keepdims=True) + epsilon)
    normed = centred * inverse
    return (normed * scales + offset, normed, inverse)


def norm_back(grad_out, normed, inverse, scales):
    scaled = grad_out * scales
    centred = scaled - jnp.mean(scaled, axis=-1, keepdims=True)
    return (centred - normed * jnp.mean(scaled * normed, axis=-1, keepdims=True)) * inverse


def first_head(shape):
    return lax.broadcasted_iota(jnp.int32, shape, len(shape) - 1) < HD


def local_call(
    kernel, outs, ins, after=(), scratch=(), smem=0, name=None
):
    count = len(ins)

    def body(*refs):
        kernel(*refs[:count], *refs[count + len(after) :])

    return pl.pallas_call(
        body,
        out_shape=tuple(outs),
        in_specs=[pl.BlockSpec(memory_space=pltpu.SMEM)] * smem
        + [pl.BlockSpec(memory_space=pltpu.VMEM)] * (count - smem)
        + [pl.BlockSpec(memory_space=pl.ANY)] * len(after),
        out_specs=tuple(pl.BlockSpec(memory_space=pltpu.VMEM) for _ in outs),
        scratch_shapes=list(scratch),
        compiler_params=pltpu.CompilerParams(vmem_limit_bytes=VMEM_BYTES),
        cost_estimate=BRIEF,
        name=name,
    )(*ins, *after)


def part_blocks(source, bit, high, low, keep_ref, give_ref):
    for j in range(high):
        keep_ref[low * j : low * (j + 1)] = source[
            pl.ds(pl.multiple_of((2 * j + bit) * low, 8), low)
        ]
        give_ref[low * j : low * (j + 1)] = source[
            pl.ds(pl.multiple_of((2 * j + 1 - bit) * low, 8), low)
        ]


def lanes(rows):
    return -(-rows // 128) * 128


def turn(value, bit, part, scratch, keep_ref, give_ref):
    rows = value.shape[0]
    scratch[:, :rows] = jnp.transpose(value)
    if scratch.shape[1] > rows:
        scratch[:, rows:] = jnp.zeros((scratch.shape[0], scratch.shape[1] - rows), jnp.float32)
    part_blocks(scratch, bit, value.shape[1] // (2 * part), part, keep_ref, give_ref)


def like(shape, dtype=jnp.float32):
    return jax.ShapeDtypeStruct(shape, dtype)


def enter_kernel(state_ref, scales_ref, weight_ref, bias_ref, act_ref, out_ref):
    which = pl.program_id(0)

    @pl.when(which == 0)
    def _():
        act_ref[...] = layer_norm(
            state_ref[...].astype(jnp.float32), scales_ref[0:1], scales_ref[1:2]
        )[0].astype(jnp.bfloat16)

    biases = bias_ref[...].astype(jnp.float32)
    zero = jnp.zeros_like(biases[0:1])
    bias = jnp.where(which == 0, biases[0:1], jnp.where(which == 2, biases[1:2], zero))
    out_ref[0] = (dot(act_ref[...], weight_ref[0]) + bias).astype(jnp.bfloat16)


def enter(states, scales, weight, bias):
    rows, width = states.shape
    local = weight.shape[2]
    return pl.pallas_call(
        enter_kernel,
        out_shape=(
            like((rows, width), jnp.bfloat16),
            like((3, rows, local), jnp.bfloat16),
        ),
        grid=(3,),
        in_specs=[
            pl.BlockSpec((rows, width), lambda i: (0, 0)),
            pl.BlockSpec((2, width), lambda i: (0, 0)),
            pl.BlockSpec((1, width, local), lambda i: (i, 0, 0)),
            pl.BlockSpec((2, local), lambda i: (0, 0)),
        ],
        out_specs=(
            pl.BlockSpec((rows, width), lambda i: (0, 0)),
            pl.BlockSpec((1, rows, local), lambda i: (i, 0, 0)),
        ),
        compiler_params=pltpu.CompilerParams(vmem_limit_bytes=VMEM_BYTES),
        cost_estimate=BRIEF,
        name="norm_project",
    )(states, scales, weight, bias)


def attend_kernel(projected_ref, first_ref, second_ref, log_ref):
    _, seq_len, width = projected_ref.shape
    cut = first_ref.shape[0]
    low = first_head((seq_len, 2 * HD))
    zero = jnp.zeros((), jnp.bfloat16)
    for pair in range(width // (2 * HD)):
        start, stop = 2 * HD * pair, 2 * HD * (pair + 1)
        cols = slice(start, stop)
        query, key = projected_ref[0, :, cols], projected_ref[1, :, cols]
        value_t = jnp.transpose(projected_ref[2, :, cols])
        parts = []
        for half in range(2):
            one_key = jnp.where(low if half == 0 else ~low, key, zero)
            scores = dot(one_key, query, NT)
            top = jnp.max(scores, axis=0, keepdims=True)
            weights = jnp.exp2((scores - top) * score_rate)
            total = jnp.sum(weights, axis=0, keepdims=True)
            weights_low = (weights * (1.0 / total)).astype(jnp.bfloat16)
            parts.append(dot(value_t[HD * half : HD * (half + 1)], weights_low))
            head = 2 * pair + half
            log_ref[head : head + 1, :] = top * score_rate + jnp.log2(total)
        context = jnp.transpose(jnp.concatenate(parts, axis=0)).astype(jnp.bfloat16)
        context = context.astype(jnp.float32)
        first_ref[:, cols] = context[:cut]
        second_ref[:, cols] = context[cut:]


def attend(projected, cut, after=()):
    _, rows, width = projected.shape
    return local_call(
        attend_kernel,
        (like((cut, width)), like((rows - cut, width)), like((width // HD, rows))),
        (projected,),
        after,
        name="attend",
    )


def turn_step(bit, value, part, after=()):
    rows, width = value.shape
    half = like((width // 2, lanes(rows)))

    def kernel(bit_ref, value_ref, keep_ref, give_ref, scratch):
        turn(value_ref[...].astype(jnp.float32), bit_ref[0], part, scratch, keep_ref, give_ref)

    return local_call(
        kernel,
        (half, half),
        (bit, value),
        after,
        scratch=(pltpu.VMEM((width, lanes(rows)), jnp.float32),),
        smem=1,
        name="turn",
    )


def attend_back_kernel(projected_ref, log_ref, *refs):
    grad_refs, grads_ref = refs[:-1], refs[-1]
    _, seq_len, width = projected_ref.shape
    low = first_head((seq_len, 2 * HD))
    zero = jnp.zeros((), jnp.bfloat16)
    round_low = lambda v: v.astype(jnp.bfloat16).astype(jnp.float32)
    for pair in range(width // (2 * HD)):
        start, stop = 2 * HD * pair, 2 * HD * (pair + 1)
        cols = slice(start, stop)
        query, key, value = (projected_ref[j, :, cols] for j in range(3))
        grad = jnp.concatenate([one[:, cols] for one in grad_refs], axis=0)
        key_t = jnp.transpose(key)
        grad_query, grad_key, grad_value = [], [], []
        for half in range(2):
            kept = low if half == 0 else ~low
            head = 2 * pair + half
            scores = dot(jnp.where(kept, key, zero), query, NT)
            weights = jnp.exp2(scores * score_rate - log_ref[head : head + 1, :])
            grad_weights = dot(jnp.where(kept, value, zero), grad, NT)
            grad_value.append(dot(weights.astype(jnp.bfloat16), grad))
            row_sum = jnp.sum(grad_weights * weights, axis=0, keepdims=True)
            grad_scores = (weights * (grad_weights - row_sum)).astype(jnp.bfloat16)
            grad_key.append(dot(grad_scores, query))
            grad_query.append(dot(key_t[HD * half : HD * (half + 1)], grad_scores))
        grads_ref[:, start:stop] = round_low(
            jnp.transpose(jnp.concatenate(grad_query, axis=0)) * score_scale
        )
        grads_ref[:, width + start : width + stop] = round_low(
            jnp.where(low, grad_key[0], grad_key[1]) * score_scale
        )
        grads_ref[:, 2 * width + start : 2 * width + stop] = round_low(
            jnp.where(low, grad_value[0], grad_value[1])
        )


def attend_back(projected, log_total, grad_context, after=()):
    _, seq_len, width = projected.shape
    return local_call(
        attend_back_kernel,
        (like((seq_len, 3 * width)),),
        (projected, log_total, *grad_context),
        after,
        name="attend_back",
    )[0]


def mlp_kernel(
    rows, inside, part, places_ref, bit_ref, hidden_ref, context_ref, other_ref, weight_ref, *refs
):
    pieces, (bias_ref, gain_ref, shift_ref, up_ref, up_bias_ref, down_ref) = refs[:4], refs[4:10]
    middle_ref, normed_ref, inverse_ref, turned_ref, given_ref, inner_ref, slope_ref, part_ref = (
        refs[10:18]
    )
    weight_other, act_ref, scratch = refs[18:]

    @pl.when(pl.program_id(0) == 0)
    def _():
        block = pieces[0].shape[0]
        for i, piece in enumerate(pieces):
            start = pl.multiple_of(places_ref[i] * block, block)
            weight_other[pl.ds(start, block)] = piece[...].astype(jnp.bfloat16)
        branch = dot(context_ref[inside].astype(jnp.bfloat16), weight_ref[...]) + dot(
            other_ref[inside].astype(jnp.bfloat16), weight_other[...]
        )
        middle = hidden_ref[rows].astype(jnp.float32) + branch + bias_ref[...]
        normed_out, normed, inverse = layer_norm(middle, gain_ref[...], shift_ref[...])
        middle_ref[...] = middle
        normed_ref[...] = normed
        inverse_ref[...] = inverse
        act = normed_out.astype(jnp.bfloat16)
        act_ref[...] = act
        turn(act.astype(jnp.float32), bit_ref[0], part, scratch, turned_ref, given_ref)

    pre_act = dot(act_ref[...], up_ref[...]) + up_bias_ref[...]
    sigma = 0.5 + 0.5 * jnp.tanh((0.5 * quick_rate) * pre_act)
    inner = (pre_act * sigma).astype(jnp.bfloat16)
    inner_ref[...] = inner.astype(jnp.float32)
    slope_ref[...] = sigma + pre_act * quick_rate * sigma * (1.0 - sigma)
    product = dot(inner, down_ref[...])

    @pl.when(pl.program_id(0) == 0)
    def _():
        part_ref[...] = product

    @pl.when(pl.program_id(0) > 0)
    def _():
        part_ref[...] += product


def mlp_step(
    rows, inside, part, places, bit, hidden, context, other, weight, pieces, bias, gain, shift,
    up, up_bias, down, after=(), tile=1024,
):
    width = hidden.shape[1]
    count = rows.stop - rows.start
    units = up.shape[1]
    ins = (places, bit, hidden, context, other, weight, *pieces, bias, gain, shift)

    def body(*refs):
        mlp_kernel(rows, inside, part, *refs[: len(ins) + 3], *refs[len(ins) + 3 + len(after) :])

    whole = lambda shape: pl.BlockSpec(shape, lambda i: (0,) * len(shape))
    half = (width // 2, lanes(count))
    return pl.pallas_call(
        body,
        out_shape=(
            like((count, width)),
            like((count, width)),
            like((count, 1)),
            like(half),
            like(half),
            like((count, units)),
            like((count, units)),
            like((count, width)),
        ),
        grid=(units // tile,),
        in_specs=[pl.BlockSpec(memory_space=pltpu.SMEM)] * 2
        + [whole(v.shape) for v in ins[2:]]
        + [
            pl.BlockSpec((width, tile), lambda i: (0, i)),
            pl.BlockSpec((1, tile), lambda i: (0, i)),
            pl.BlockSpec((tile, width), lambda i: (i, 0)),
        ]
        + [pl.BlockSpec(memory_space=pl.ANY)] * len(after),
        out_specs=(
            whole((count, width)),
            whole((count, width)),
            whole((count, 1)),
            whole(half),
            whole(half),
            pl.BlockSpec((count, tile), lambda i: (0, i)),
            pl.BlockSpec((count, tile), lambda i: (0, i)),
            whole((count, width)),
        ),
        scratch_shapes=[
            pltpu.VMEM(weight.shape, jnp.bfloat16),
            pltpu.VMEM((count, width), jnp.bfloat16),
            pltpu.VMEM((width, lanes(count)), jnp.float32),
        ],
        compiler_params=pltpu.CompilerParams(vmem_limit_bytes=VMEM_BYTES),
        cost_estimate=BRIEF,
        name="mlp",
    )(*ins, up, up_bias, down, *after)


def result_kernel(
    rows, part, scale_ref, bit_ref, middle_ref, part_ref, other_ref, bias_ref, target_ref, *outs
):
    out_ref, grad_ref, low_ref, turned_ref, given_ref, sums_ref, scratch = outs
    result = middle_ref[...] + (part_ref[...] + other_ref[...]) + bias_ref[...]
    error = result - target_ref[rows].astype(jnp.float32)
    grad = error * scale_ref[0]
    low = grad.astype(jnp.bfloat16)
    out_ref[...] = result.astype(jnp.bfloat16)
    grad_ref[...] = grad
    low_ref[...] = low
    turn(low.astype(jnp.float32), bit_ref[0], part, scratch, turned_ref, given_ref)
    sums_ref[0:1] = jnp.sum(grad, axis=0, keepdims=True)
    sums_ref[1:2] = jnp.sum(error * error, axis=0, keepdims=True)


def result_step(rows, row_part, scale, bit, middle, part, other, bias, target, after=()):
    count, width = middle.shape
    half = like((width // 2, lanes(count)))
    return local_call(
        lambda *refs: result_kernel(rows, row_part, *refs),
        (
            like((count, width), jnp.bfloat16),
            like((count, width)),
            like((count, width), jnp.bfloat16),
            half,
            half,
            like((2, width)),
        ),
        (scale, bit, middle, part, other, bias, target),
        after,
        scratch=(pltpu.VMEM((width, lanes(count)), jnp.float32),),
        smem=2,
        name="result_error",
    )


def mlp_back_kernel(low_ref, slope_ref, down_ref, up_ref, pre_ref, two_ref, sums_ref):
    pre = (dot(low_ref[...], down_ref[...], NT) * slope_ref[...]).astype(jnp.bfloat16)
    pre_ref[...] = pre.astype(jnp.float32)
    sums_ref[...] = jnp.sum(pre.astype(jnp.float32), axis=0, keepdims=True)
    two = dot(pre, up_ref[...], NT)

    @pl.when(pl.program_id(0) == 0)
    def _():
        two_ref[...] = two

    @pl.when(pl.program_id(0) > 0)
    def _():
        two_ref[...] += two


def mlp_back(low, slope, down, up, after=(), tile=1024):
    count, width = low.shape
    units = up.shape[1]

    def body(*refs):
        mlp_back_kernel(*refs[:4], *refs[4 + len(after) :])

    return pl.pallas_call(
        body,
        out_shape=(
            like((count, units)),
            like((count, width)),
            like((1, units)),
        ),
        grid=(units // tile,),
        in_specs=[
            pl.BlockSpec((count, width), lambda i: (0, 0)),
            pl.BlockSpec((count, tile), lambda i: (0, i)),
            pl.BlockSpec((tile, width), lambda i: (i, 0)),
            pl.BlockSpec((width, tile), lambda i: (0, i)),
        ]
        + [pl.BlockSpec(memory_space=pl.ANY)] * len(after),
        out_specs=(
            pl.BlockSpec((count, tile), lambda i: (0, i)),
            pl.BlockSpec((count, width), lambda i: (0, 0)),
            pl.BlockSpec((1, tile), lambda i: (0, i)),
        ),
        compiler_params=pltpu.CompilerParams(vmem_limit_bytes=VMEM_BYTES),
        cost_estimate=BRIEF,
        name="mlp_back",
    )(low, slope, down, up, *after)


def middle_back_kernel(
    row_part, before, bit_ref, part_ref, other_ref, grad_ref, normed_ref, inverse_ref, gain_ref,
    weight_ref, *refs
):
    earlier, outs = refs[: 2 * before], refs[2 * before :]
    mid_ref, turned_ref, given_ref, context_ref, sums_ref, scratch = outs
    grad_two = part_ref[...] + other_ref[...]
    normed = normed_ref[...]
    mid = grad_ref[...] + norm_back(grad_two, normed, inverse_ref[...], gain_ref[...])
    low = mid.astype(jnp.bfloat16)
    mid_ref[...] = mid
    context_ref[...] = dot(low, weight_ref[...], NT).astype(jnp.bfloat16)
    rows = low.shape[0]
    start = turned_ref.shape[1] - lanes(rows)
    if before:
        turned_ref[:, :start] = earlier[0][...]
        given_ref[:, :start] = earlier[1][...]
    turn(
        low.astype(jnp.float32),
        bit_ref[0],
        row_part,
        scratch,
        turned_ref.at[:, start:],
        given_ref.at[:, start:],
    )
    sums_ref[0:1] = jnp.sum(mid, axis=0, keepdims=True)
    sums_ref[1:2] = jnp.sum(grad_two * normed, axis=0, keepdims=True)
    sums_ref[2:3] = jnp.sum(grad_two, axis=0, keepdims=True)


def middle_back(
    row_part, bit, part, other, grad, normed, inverse, gain, weight, earlier=(), after=()
):
    count, width = grad.shape
    start = earlier[0].shape[1] if earlier else 0
    half = like((width // 2, start + lanes(count)))
    return local_call(
        lambda *refs: middle_back_kernel(row_part, len(earlier) // 2, *refs),
        (
            like((count, width)),
            half,
            half,
            like((count, weight.shape[0]), jnp.bfloat16),
            like((3, width)),
        ),
        (bit, part, other, grad, normed, inverse, gain, weight, *earlier),
        after,
        scratch=(pltpu.VMEM((width, lanes(count)), jnp.float32),),
        smem=1,
        name="middle_back",
    )


def project_back_kernel(grads_ref, weight_ref, state_ref, part_ref, sums_ref, bias_ref):
    width = weight_ref.shape[2]
    low = lambda j: grads_ref[:, j * width : (j + 1) * width].astype(jnp.bfloat16)
    part = dot(low(0), weight_ref[0], NT)
    for j in (1, 2):
        part = part + dot(low(j), weight_ref[j], NT)
    part_ref[...] = part
    normed = layer_norm(state_ref[...].astype(jnp.float32), 1.0, 0.0)[1]
    sums_ref[0:1] = jnp.sum(part * normed, axis=0, keepdims=True)
    sums_ref[1:2] = jnp.sum(part, axis=0, keepdims=True)
    bias_ref[...] = jnp.sum(grads_ref[...], axis=0, keepdims=True)


def project_back(grads, weight, states, after=()):
    rows, width = states.shape
    return local_call(
        project_back_kernel,
        (like((rows, width)), like((2, width)), like((1, grads.shape[1]))),
        (grads, weight, states),
        after,
        name="project_back",
    )


def last_kernel(count, part_ref, other_ref, state_ref, gain_ref, *refs):
    mids, results, (grad_ref, out_ref) = refs[:count], refs[count : 2 * count], refs[2 * count :]
    start = 0
    for mid, result in zip(mids, results):
        rows = slice(start, start + mid.shape[0])
        _, normed, inverse = layer_norm(state_ref[rows].astype(jnp.float32), 1.0, 0.0)
        grad_one = part_ref[rows] + other_ref[rows]
        grad_ref[rows] = (
            mid[...] + norm_back(grad_one, normed, inverse, gain_ref[...])
        ).astype(jnp.bfloat16)
        out_ref[rows] = result[...]
        start = rows.stop


def last_step(mids, part, other, states, gain, results, after=()):
    return local_call(
        lambda *refs: last_kernel(len(mids), *refs),
        (like(states.shape, jnp.bfloat16),) * 2,
        (part, other, states, gain, *mids, *results),
        after,
        name="input_grad",
    )


def outer_kernel(high, low, plans, bit_ref, *refs):
    count = sum(len(lefts) + rights for _, lefts, rights in plans)
    operands, (give_ref, keep_ref), scratch = refs[:count], refs[count : count + 2], refs[count + 2 :]
    rounded, full = list(scratch[:-1]), scratch[-1]
    operands = list(operands)
    for (first, last), lefts, rights in plans:
        left_refs = [operands.pop(0) for _ in lefts]
        offsets = [start for _, _, start in lefts]
        right_refs = [operands.pop(0) for _ in range(rights)]
        low_refs = [rounded.pop(0) for _ in lefts]

        @pl.when(pl.program_id(0) == first)
        def _():
            for out, left in zip(low_refs, zip(left_refs, offsets)):
                out[...] = left[0][:, left[1] : left[1] + out.shape[1]].astype(jnp.bfloat16)

        @pl.when((pl.program_id(0) >= first) & (pl.program_id(0) < last))
        def _():
            total = None
            for out, (index, rows, _) in zip(low_refs, lefts):
                product = dot(out[...], right_refs[index][rows].astype(jnp.bfloat16))
                total = product if total is None else total + product
            full[...] = total

    part_blocks(full, bit_ref[0], high, low, keep_ref, give_ref)


def outer_sum(bit, high, groups, after=(), tile=512):
    width = groups[0][0][0][0].shape[0]
    low = width // (2 * high)
    operands, specs, scratch, plans = [], [], [], []
    first = 0
    for lefts, rights, start, columns in groups:
        last = first + columns // tile
        places, index, row = [], 0, 0
        for v, offset, rows in lefts:
            operands.append(v)
            specs.append(pl.BlockSpec(v.shape, lambda i: (0, 0)))
            scratch.append(pltpu.VMEM((width, rows), jnp.bfloat16))
            if row == rights[index].shape[0]:
                index, row = index + 1, 0
            places.append((index, slice(row, row + rows), offset))
            row += rows
        for v in rights:
            operands.append(v)
            place = lambda i, s=start // tile, f=first, n=last - first: (
                0,
                s + jnp.clip(i - f, 0, n - 1),
            )
            specs.append(pl.BlockSpec((v.shape[0], tile), place))
        plans.append(((first, last), places, len(rights)))
        first = last

    def body(*refs):
        count = 1 + len(operands)
        outer_kernel(high, low, plans, *refs[:count], *refs[count + len(after) :])

    return pl.pallas_call(
        body,
        out_shape=(like((width // 2, first * tile)),) * 2,
        grid=(first,),
        in_specs=[pl.BlockSpec(memory_space=pltpu.SMEM)]
        + specs
        + [pl.BlockSpec(memory_space=pl.ANY)] * len(after),
        out_specs=(pl.BlockSpec((width // 2, tile), lambda i: (0, i)),) * 2,
        scratch_shapes=scratch + [pltpu.VMEM((width, tile), jnp.float32)],
        compiler_params=pltpu.CompilerParams(vmem_limit_bytes=VMEM_BYTES),
        cost_estimate=BRIEF,
        name="weight_grad",
    )(bit, *operands, *after)


def split_kernel(count, bit_ref, *refs):
    bit = bit_ref[0]
    keeps, cames, (give_out, keep_out) = refs[:count], refs[count : 2 * count], refs[2 * count :]
    start = 0
    for keep_ref, came_ref in zip(keeps, cames):
        columns = slice(start, start + keep_ref.shape[-1])
        keep_out[0, :, columns] = keep_ref[0, bit] + came_ref[0, bit]
        give_out[0, :, columns] = keep_ref[0, 1 - bit] + came_ref[0, 1 - bit]
        start = columns.stop


def add_split(bit, keeps, cames, high):
    rows = keeps[0].shape[0]
    low = rows // (2 * high)
    blocks = [v.reshape(high, 2, low, v.shape[1]) for v in (*keeps, *cames)]
    columns = sum(v.shape[1] for v in keeps)
    give, kept = pl.pallas_call(
        lambda *refs: split_kernel(len(keeps), *refs),
        out_shape=(like((high, low, columns)),) * 2,
        grid=(high,),
        in_specs=[pl.BlockSpec(memory_space=pltpu.SMEM)]
        + [pl.BlockSpec((1, *v.shape[1:]), lambda i: (i, 0, 0, 0)) for v in blocks],
        out_specs=(pl.BlockSpec((1, low, columns), lambda i: (i, 0, 0)),) * 2,
        compiler_params=pltpu.CompilerParams(vmem_limit_bytes=20 * 2**20),
        cost_estimate=BRIEF,
        name="add_split",
    )(bit, *blocks)
    return give.reshape(rows // 2, columns), kept.reshape(rows // 2, columns)


def finish_kernel(counts, *refs):
    total = sum(counts)
    pairs, outs = list(zip(refs[:total], refs[total : 2 * total])), refs[2 * total :]
    for count, out in zip(counts, outs):
        start = 0
        for _ in range(count):
            keep_ref, came_ref = pairs.pop(0)
            stop = start + keep_ref.shape[1]
            out[:, start:stop] = keep_ref[...] + came_ref[...]
            start = stop


def finish_all(results, after=()):
    return local_call(
        lambda *refs: finish_kernel([len(keeps) for keeps, _ in results], *refs),
        [like((one[0].shape[0], sum(v.shape[1] for v in one))) for one, _ in results],
        (*(v for one, _ in results for v in one), *(v for _, one in results for v in one)),
        after,
        name="finish",
    )


def pack_kernel(counts, valid_ref, *refs):
    ins, out = list(refs[:-1]), refs[-1]
    one, other, projected = ins[:3]
    rest = ins[3:]
    middles, ups, results = (
        rest[: counts],
        rest[counts : 2 * counts],
        rest[2 * counts :],
    )
    width = out.shape[1]
    total = lambda parts: sum(part[...] for part in parts[1:]) + parts[0][...]
    out[...] = jnp.zeros_like(out)
    out[0:2] = one[...] + other[...]
    local = projected.shape[1] // 3
    out[2:3, :local] = projected[:, :local]
    out[2:3, local : 2 * local] = projected[:, 2 * local :]
    out[3:6] = total(middles)
    up = total(ups)
    rows = up.shape[1] // width
    for row in range(rows):
        out[6 + row : 7 + row] = up[:, row * width : (row + 1) * width]
    result = total(results)
    out[6 + rows : 7 + rows] = result[0:1]
    out[7 + rows : 8 + rows] = result[1:2] * valid_ref[0]


def pack(valid, one, other, projected, middles, ups, results):
    width = one.shape[1]
    rows = -(-(8 + ups[0].shape[1] // width) // 8) * 8
    return local_call(
        lambda *refs: pack_kernel(len(middles), *refs),
        (like((rows, width)),),
        (valid, one, other, projected, *middles, *ups, *results),
        smem=1,
        name="pack",
    )[0]


def tie(value, *others):
    return lax.optimization_barrier((value, *others))[0]


def make_shards(mesh):
    groups = mesh.shape["dp"]
    bits = groups.bit_length() - 1
    assert groups == 1 << bits and mesh.shape["tensor"] == 2

    def swap_tensor(value):
        return lax.ppermute(value, "tensor", [(0, 1), (1, 0)])

    def swap_bit(value, bit):
        return lax.ppermute(value, "dp", [(i, i ^ (1 << bit)) for i in range(groups)])

    def sum_dp(value):
        for bit in range(bits):
            value = value + swap_bit(value, bit)
        return value

    def own_bit(bit):
        return ((lax.axis_index("dp") >> bit) & 1).astype(jnp.int32).reshape(1)

    class Scatter:
        def __init__(self, groups_of, order, after=(), tile=512):
            self.left = list(range(1, bits))[::-1]
            self.order = list(order)
            bit = self.order[0]
            self.give, self.keep = outer_sum(
                own_bit(bit), 1 << self.left.index(bit), groups_of, after, tile
            )
            self.keep, self.came = [self.keep], None

        def send(self):
            bit = self.order.pop(0)
            self.came = [swap_bit(self.give, bit)]
            self.left.remove(bit)
            self.give = None

        def join(self, other):
            self.keep = self.keep + other.keep
            self.came = self.came + other.came

        def fold(self):
            bit = self.order[0]
            self.give, keep = add_split(
                own_bit(bit), self.keep, self.came, 1 << self.left.index(bit)
            )
            self.keep, self.came = [keep], None

        def move(self):
            self.fold()
            self.send()

        def last(self):
            while self.order:
                self.move()
            return self

    def sync(scatters, *arrays):
        held = [(one.give, one.keep, one.came) for one in scatters]
        held, arrays = lax.optimization_barrier((held, arrays))
        for one, (give, keep, came) in zip(scatters, held):
            one.give, one.keep, one.came = give, keep, came
        return arrays

    def shards(
        images,
        teacher,
        image_mask,
        attn_gain,
        attn_shift,
        in_weight,
        in_bias,
        out_weight,
        out_bias,
        mlp_gain,
        mlp_shift,
        up_weight,
        up_bias,
        down_weight,
        down_bias,
    ):
        image_count, seq_len, width = images.shape
        row_count = image_count * seq_len
        local_width = in_weight.shape[2]
        scales_one = jnp.stack([attn_gain, attn_shift]).astype(jnp.float32)
        gain_one = scales_one[0:1]
        gain_two = mlp_gain.astype(jnp.float32)[None]
        shift_two = mlp_shift.astype(jnp.float32)[None]
        bias_out = out_bias.astype(jnp.float32)[None]
        bias_up = up_bias.astype(jnp.float32)[None]
        bias_down = down_bias.astype(jnp.float32)[None]
        weights_in = jnp.swapaxes(in_weight, 0, 1)
        chunks, start = [], 0
        for stop in (336, row_count):
            chunks.append(slice(start, stop))
            start = stop
        cut = chunks[0].stop
        part = width // groups
        core_bit = own_bit(0)
        low_first = tuple(range(1, bits))
        swap_core = lambda value: swap_bit(value, 0)

        quarter = local_width // 4
        dp_index = lax.axis_index("dp")
        piece = lax.dynamic_slice_in_dim(out_weight, (dp_index & 3) * quarter, quarter, axis=0)
        pieces = [swap_tensor(piece.astype(jnp.float32))]
        places = jnp.stack([(dp_index & 3) ^ way for way in (0, 2, 1, 3)]).astype(jnp.int32)

        states = images.reshape(row_count, width)
        targets = teacher.reshape(row_count, width)
        act_one, projected = enter(states, scales_one, weights_in, in_bias)
        *context, log_total = attend(projected, chunks[0].stop)
        context_other = [swap_tensor(one) for one in context]
        pieces.append(swap_bit(tie(pieces[0], log_total), 1))
        pieces += [swap_core(one) for one in pieces]

        valid = image_mask.astype(jnp.float32)[0]
        count = tie(jnp.full((8, 128), valid * seq_len, jnp.float32), log_total)
        count = count + swap_bit(count, 0)
        turned_one, given_one = turn_step(core_bit, act_one, part, (log_total,))

        middle, normed_two, inverse_two, turned_two, given_two, inner, slope, mlp_part = mlp_out = [
            [] for _ in range(8)
        ]
        count, turned_one, given_one, context, context_other[0], pieces = sync(
            [], count, turned_one, given_one, context, context_other[0], pieces
        )
        more = swap_bit(count, 1)

        def mlp_of(i):
            rows = chunks[i]
            step = mlp_step(
                rows,
                slice(0, rows.stop - rows.start),
                part,
                places,
                core_bit,
                states,
                context[i],
                context_other[i],
                out_weight,
                pieces,
                bias_out,
                gain_two,
                shift_two,
                up_weight,
                bias_up,
                down_weight,
            )
            for kept, one in zip(mlp_out, step):
                kept.append(one)

        mlp_of(0)
        mlp_part[0], given_two[0], inner[0], given_one, context, context_other[1], count, more = sync(
            [], mlp_part[0], given_two[0], inner[0], given_one, context, context_other[1], count, more
        )
        count = count + more
        mlp_other = [swap_tensor(mlp_part[0])]
        came_two, came_inner = [swap_core(given_two[0])], [swap_core(inner[0])]
        came_one = swap_core(given_one)
        more = swap_bit(count, 2)
        mlp_of(1)
        mlp_part[1], given_two[1], inner[1], came_two, came_inner, came_one, count, more = sync(
            [], mlp_part[1], given_two[1], inner[1], came_two, came_inner, came_one, count, more
        )
        count = count + more
        mlp_other.append(swap_tensor(mlp_part[1]))
        for bit in range(3, bits):
            count = count + swap_bit(count, bit)
        mlp_other[0], given_two[1], inner[1], count = sync(
            [], mlp_other[0], given_two[1], inner[1], count
        )
        count_all = count[:1, 0]
        scale = 2.0 * valid / count_all

        result, grad_result, grad_low, turned_low, given_low, result_sums = result_out = [
            [] for _ in range(6)
        ]
        grad_pre, two_part, up_sums = back_out = [[], [], []]
        two_other = []

        def result_of(i, after):
            step = result_step(
                chunks[i],
                part,
                scale,
                core_bit,
                middle[i],
                mlp_part[i],
                mlp_other[i],
                bias_down,
                targets,
                after,
            )
            for kept, one in zip(result_out, step):
                kept.append(one)

        def back_of(i, after):
            step = mlp_back(grad_low[i], slope[i], down_weight, up_weight, after)
            for kept, one in zip(back_out, step):
                kept.append(one)
            two_other.append(swap_tensor(two_part[i]))
            return (two_part[i],)

        grad_middle, turned_attn, given_attn, grad_context, middle_sums = middle_out = [
            [] for _ in range(5)
        ]

        def middle_of(i, earlier, after):
            step = middle_back(
                part,
                core_bit,
                two_part[i],
                two_other[i],
                grad_result[i],
                normed_two[i],
                inverse_two[i],
                gain_two,
                out_weight,
                earlier,
                after,
            )
            for kept, one in zip(middle_out, step):
                kept.append(one)
            return (grad_context[i],)

        def rows_of(values):
            return [(one, 0, rows.stop - rows.start) for one, rows in zip(values, chunks * 2)]

        half = up_weight.shape[1] // 2
        came_two.append(swap_core(given_two[1]))
        came_inner.append(swap_core(inner[1]))
        came_context = [swap_core(one) for one in context]
        result_of(0, ())
        back_of(0, ())
        came_two, came_inner, came_context, grad_pre[0], given_low[0], two_part[0] = sync(
            [], came_two, came_inner, came_context, grad_pre[0], given_low[0], two_part[0]
        )
        two_other = [swap_tensor(two_part[0])]
        came_low = [swap_core(given_low[0])]
        result_of(1, (two_part[0],))
        given_low[1], grad_low[1], slope[1] = sync([], given_low[1], grad_low[1], slope[1])

        came_low.append(swap_core(given_low[1]))
        (came_low,) = sync([], came_low)

        left, right = rows_of(turned_low + came_low), inner + came_inner
        first_units = 3 * half // 4
        down_b = Scatter([(left, right, 0, first_units)], low_first, (), first_units)
        grad_low[1], slope[1] = sync([down_b], grad_low[1], slope[1])

        down_b.send()
        back_of(1, ())
        down_d = Scatter(
            [(left, right, first_units, 2 * half - first_units)],
            low_first,
            (two_part[1],),
            first_units // 3,
        )
        two_part[1], grad_pre, two_other[0] = sync(
            [down_b, down_d], two_part[1], grad_pre, two_other[0]
        )

        two_other.append(swap_tensor(two_part[1]))
        down_d.send()
        came_pre = [swap_core(one) for one in grad_pre]
        down_b.move()
        middle_of(0, (), ())
        left, right = rows_of(turned_two + came_two), grad_pre + came_pre
        up_a = Scatter([(left, right, 0, half)], low_first, (grad_context[0],))
        up_b = Scatter([(left, right, half, half)], low_first, (up_a.give,))
        middle_of(1, (turned_attn[0], given_attn[0]), (up_b.give,))
        turned_attn[1], given, grad_context = sync(
            [down_b, down_d, up_a, up_b], turned_attn[1], given_attn[1], grad_context
        )

        up_a.send()
        down_b.move()
        down_d.move()
        grads = attend_back(projected, log_total, grad_context)
        grads, given = sync([down_b, down_d, up_a, up_b], grads, given)

        up_b.send()
        came_grads = swap_core(grads)
        came_attn = swap_core(given)
        up_a.move()
        down_d.move()
        one_part, one_sums, in_sums = project_back(grads, weights_in, states)
        left = [(turned_one, 0, row_count), (came_one, 0, row_count)]
        right = [grads, came_grads]
        in_a = Scatter([(left, right, 0, 2 * local_width)], low_first, (one_part,))
        first = swap_tensor(one_sums)
        one_part, one_sums, first, came_attn, came_grads = sync(
            [down_b, down_d, up_a, up_b, in_a], one_part, one_sums, first, came_attn, came_grads
        )
        in_b = Scatter(
            [(left, [grads, came_grads], 2 * local_width, local_width)], low_first
        )

        one_other = swap_tensor(one_part)
        in_a.send()
        up_a.move()
        up_b.move()
        starts = (0, lanes(chunks[0].stop))
        left = [
            (one, start, rows.stop - rows.start)
            for one in (turned_attn[1], came_attn)
            for start, rows in zip(starts, chunks)
        ]
        out_all = Scatter(
            [(left, [*context, *came_context], 0, local_width)], low_first, (in_b.give,)
        )
        full_down = finish_all(
            [(down_b.last().keep + down_d.last().keep, down_b.came + down_d.came)]
        )[0]
        small = pack(valid.reshape(1), one_sums, first, in_sums, middle_sums, up_sums, result_sums)
        small = small + swap_bit(small, 0)
        more = swap_bit(small, 2)
        small, more, full_down = sync([up_a, up_b, in_a, in_b, out_all], small, more, full_down)

        in_b.send()
        in_a.move()
        up_b.move()
        small = small + more
        (small,) = sync([up_a, up_b, in_a, in_b, out_all], small)

        out_all.send()
        in_b.move()
        in_a.move()
        more = swap_bit(small, 1)
        (full_up,) = finish_all(
            [(up_a.last().keep + up_b.last().keep, up_a.came + up_b.came)]
        )
        small, more, full_up = sync([in_a, in_b, out_all], small, more, full_up)

        out_all.move()
        in_b.move()
        small = small + more
        for bit in range(3, bits - 1):
            small = small + swap_bit(small, bit)
        more = swap_bit(small, bits - 1)
        grad_images, block_out = last_step(
            grad_middle, one_part, one_other, states, gain_one, result
        )
        small, more, grad_images, block_out = sync(
            [in_a, in_b, out_all], small, more, grad_images, block_out
        )
        small = small + more

        out_all.move()
        in_a.last(), in_b.last()
        (full_in,) = finish_all([(in_a.keep + in_b.keep, in_a.came + in_b.came)])
        (full_out,) = finish_all([(out_all.last().keep, out_all.came)])
        up_rows = up_bias.shape[0] // width
        small_up = small[6 : 6 + up_rows].reshape(-1)
        shape = (image_count, seq_len, width)
        return (
            block_out.reshape(shape),
            jnp.sum(small[7 + up_rows]) / count_all[0],
            grad_images.reshape(shape),
            small[0],
            small[1],
            full_in.reshape(-1, 3, local_width),
            small[2].reshape(2, local_width),
            full_out.T,
            small[3],
            small[4],
            small[5],
            full_up,
            small_up,
            full_down.T,
            small[6 + up_rows],
        )

    return shards


def solution(mesh):
    placed = (
        P("dp", None, None),
        P("dp", None, None),
        P("dp"),
        P(),
        P(),
        P(None, None, "tensor"),
        P(None, "tensor"),
        P("tensor", None),
        P(),
        P(),
        P(),
        P(None, "tensor"),
        P("tensor"),
        P("tensor", None),
        P(),
    )
    return jax.shard_map(
        make_shards(mesh),
        mesh=mesh,
        in_specs=placed,
        out_specs=(
            P("dp", None, None),
            P(),
            P("dp", None, None),
            P(),
            P(),
            P("dp", None, "tensor"),
            P(None, "tensor"),
            P("tensor", "dp"),
            P(),
            P(),
            P(),
            P("dp", "tensor"),
            P("tensor"),
            P("tensor", "dp"),
            P(),
        ),
        check_vma=False,
    )
```
